32 devices in a mesh: dp: 8 (over z, y), sub: 4 (over x, core).
Axes of the slice: x: 2, y: 2, z: 4, core: 2. Of those that a mesh axis runs over, the one named last changes fastest.
Arguments:
- activations: bfloat16 [65536, 768], P(('dp', 'sub')), may hold values from -20 to 20
- out_grad: bfloat16 [65536, 768], P(('dp', 'sub')), may hold values from -6 to 6
- species: int32 [65536], P(('dp', 'sub')), may hold values from 0 to 1, as said below
- first_start: int32 [32], P(('dp', 'sub')), may hold values from 0 to 1023, as said below
- species_weight: float32 [2, 768], replicated, may hold values from 0.5 to 2
- conv_weight: bfloat16 [3, 768, 384], P(None, 'dp', 'sub'), may hold values from -0.125 to 0.125
- point_weight: bfloat16 [384, 768], P('sub', 'dp'), may hold values from -0.3125 to 0.3125
- gain_one: float32 [768], replicated, may hold values from 0.1 to 1.9
- bias_one: float32 [768], replicated, may hold values from -3 to 3
- gain_two: float32 [384], replicated, may hold values from 0.1 to 1.9
- bias_two: float32 [384], replicated, may hold values from -3 to 3
- running_one: float32 [2, 768], replicated, may hold values from 0.5 to 2
- running_two: float32 [2, 384], replicated, may hold values from 0.5 to 2
Outputs:
- output: bfloat16 [65536, 768], P(('dp', 'sub'))
- input_grad: bfloat16 [65536, 768], P(('dp', 'sub'))
- conv_grad: float32 [3, 768, 384], P(None, 'dp', 'sub')
- point_grad: float32 [384, 768], P('sub', 'dp')
- gain_one_grad: float32 [768], replicated
- bias_one_grad: float32 [768], replicated
- gain_two_grad: float32 [384], replicated
- bias_two_grad: float32 [384], replicated
- running_one_new: float32 [2, 768], replicated
- running_two_new: float32 [2, 384], replicated
The draws below stay inside these ranges and needn't reach their ends.
Inputs may be any that keep to these rules, and one draw needn't show every extreme that they name: `first_start`: sequence starts in a block follow every 1024 rows after the first; the first block begins with a sequence start and the last block's first start is at 1023. All rows of one sequence have the same species.
All inputs are finite; a program needn't handle non-finite values.
Results may differ from the reference program's by a relative error of at most 0.0053.
Values may be sent and summed in bfloat16 or wider, within the bound.
A program may use at most 128 MiB of HBM per device.

```python
import math
import jax
import jax.numpy as jnp
from jax import lax

C = 768
H = 384
KERN = 3
DILATION_BINS = 11
SEQ_LEN = 1024
SEQ_DEV = 2
ROWS_DEV = 2048
BLOCKS = 32
ROWS = 65536


def block_layout(key):
    layout_key = jax.random.fold_in(key, 11)
    pick_keys = jax.random.split(jax.random.fold_in(key, 15), 4)
    starts = jax.random.randint(layout_key, (BLOCKS,), 0, SEQ_LEN, dtype=jnp.int32)
    late_block = jax.random.randint(pick_keys[0], (), 1, BLOCKS - 1, dtype=jnp.int32)
    step_ahead = jax.random.randint(pick_keys[1], (), 0, BLOCKS - 3, dtype=jnp.int32)
    early_block = (1 + (late_block + step_ahead) % (BLOCKS - 2)).astype(jnp.int32)
    late_value = jax.random.randint(pick_keys[2], (), SEQ_LEN - DILATION_BINS, SEQ_LEN, dtype=jnp.int32)
    early_value = jax.random.randint(pick_keys[3], (), 0, DILATION_BINS, dtype=jnp.int32)
    starts = starts.at[late_block].set(late_value)
    starts = starts.at[early_block].set(early_value)
    starts = starts.at[0].set(0)
    starts = starts.at[BLOCKS - 1].set(SEQ_LEN - 1)
    return starts


def draw_first_start(key, part):
    return block_layout(key)


def draw_species(key, part):
    starts = block_layout(key)
    row_ids = jnp.arange(ROWS, dtype=jnp.int32)
    offsets = row_ids % ROWS_DEV
    begin = starts[row_ids // ROWS_DEV]
    is_start = (offsets >= begin) & ((offsets - begin) % SEQ_LEN == 0)
    segment_index = jnp.cumsum(is_start.astype(jnp.int32)).astype(jnp.int32)
    table = jax.random.randint(jax.random.fold_in(key, 12), (BLOCKS * SEQ_DEV + 2,), 0, 2, dtype=jnp.int32)
    return table[segment_index]


def input_field(key):
    keys = jax.random.split(jax.random.fold_in(key, 13), 4)
    noise = jnp.clip(jax.random.normal(keys[0], (ROWS, C), jnp.float32), -4.0, 4.0)
    shift = 0.3
    col_scale = jnp.exp(jax.random.uniform(keys[1], (C,), jnp.float32, math.log(0.5), math.log(2.0)))
    col_mean = shift * jnp.clip(jax.random.normal(keys[2], (C,), jnp.float32), -3.0, 3.0)
    trend = 0.6 + 1.2 * jnp.arange(ROWS, dtype=jnp.float32) / (ROWS - 1.0)
    rough = jnp.exp(jax.random.uniform(keys[3], (ROWS,), jnp.float32, -0.3, 0.3))
    row_factor = trend * rough
    values = (col_mean + noise) * col_scale * row_factor[:, None]
    return (values, row_factor)


def draw_activations(key, part):
    values, row_factor = input_field(key)
    return values.astype(jnp.bfloat16)


def draw_out_grad(key, part):
    values, row_factor = input_field(key)
    keys = jax.random.split(jax.random.fold_in(key, 14), 2)
    noise = jnp.clip(jax.random.normal(keys[0], (ROWS, C), jnp.float32), -4.0, 4.0)
    offset = jnp.clip(jax.random.normal(keys[1], (C,), jnp.float32), -3.0, 3.0)
    gradient = 0.3 * values + offset[None, :] * row_factor[:, None] + noise
    return jnp.clip(gradient, -6.0, 6.0).astype(jnp.bfloat16)


def block_scale(key, dims, pieces, least, top_value):
    def one(axis_at, blocks):
        heights = jax.random.uniform(jax.random.fold_in(jax.random.fold_in(key, 6), axis_at), (blocks,), jnp.float32, least / len(pieces), top_value / len(pieces))
        return jnp.repeat(jnp.exp(heights), dims[axis_at] // blocks).reshape((-1,) + (1,) * (len(dims) - axis_at - 1))

    level = one(*pieces[0])
    for cut in pieces[1:]:
        level = level * one(*cut)
    return level


def gaussian(rng, shape, spread, limit, cuts=(), held_as=jnp.bfloat16):
    array = spread * jax.random.normal(rng, shape, jnp.float32)
    if cuts:
        array = array * block_scale(rng, shape, cuts, -0.22, 0.18)
    return jnp.clip(array, -limit, limit).astype(held_as)


def setup_inputs(seed: int = 0) -> dict:
    streams_of = jax.random.split(jax.random.key(seed), 14)
    return {
        "activations": draw_activations(jax.random.fold_in(streams_of[13], 71), 0),
        "out_grad": draw_out_grad(jax.random.fold_in(streams_of[13], 71), 0),
        "species": draw_species(jax.random.fold_in(streams_of[13], 71), 0),
        "first_start": draw_first_start(jax.random.fold_in(streams_of[13], 71), 0),
        "species_weight": jnp.clip(jnp.exp(jax.random.uniform(streams_of[4], (2, C), jnp.float32, math.log(0.5), math.log(2.0))), 0.5, 2.0),
        "conv_weight": gaussian(streams_of[5], (KERN, C, H), (KERN * C) ** -0.5, 0.125, ((1, 8), (2, 4))),
        "point_weight": gaussian(streams_of[6], (H, C), H ** -0.5, 0.3125, ((0, 4), (1, 8))),
        "gain_one": jnp.clip(1.0 + 0.18 * jax.random.normal(streams_of[7], (C,), jnp.float32), 0.1, 1.9),
        "bias_one": gaussian(streams_of[8], (C,), 0.5, 3.0, (), jnp.float32),
        "gain_two": jnp.clip(1.0 + 0.18 * jax.random.normal(streams_of[9], (H,), jnp.float32), 0.1, 1.9),
        "bias_two": gaussian(streams_of[10], (H,), 0.5, 3.0, (), jnp.float32),
        "running_one": jnp.clip(jax.random.uniform(streams_of[11], (2, C), jnp.float32, 0.5, 2.0), 0.5, 2.0),
        "running_two": jnp.clip(jax.random.uniform(streams_of[12], (2, H), jnp.float32, 0.5, 2.0), 0.5, 2.0),
    }


@jax.custom_vjp
def low(v):
    return lax.optimization_barrier(v.astype(jnp.bfloat16)).astype(jnp.float32)

@jax.custom_vjp
def low_back(v):
    return v

def low_keep(v):
    return (low(v), None)

def low_pass(kept, grad):
    return (grad,)

def back_keep(v):
    return (v, None)

def back_low(kept, grad):
    return (low(grad),)
low.defvjp(low_keep, low_pass)
low_back.defvjp(back_keep, back_low)
EPSILON = 0.001
MOMENTUM = 0.9
HIGHEST = lax.Precision.HIGHEST

def gelu(value):
    return value * jax.nn.sigmoid(1.702 * value)

def sequence_masks(first_start):
    row_ids = jnp.arange(ROWS, dtype=jnp.int32)
    block_ids = row_ids // ROWS_DEV
    offsets = row_ids % ROWS_DEV
    begin = first_start[block_ids]
    is_start = (offsets >= begin) & ((offsets - begin) % SEQ_LEN == 0)
    segment_index = jnp.cumsum(is_start.astype(jnp.int32)).astype(jnp.int32)
    padded_rows = jnp.concatenate([jnp.full((DILATION_BINS,), -1, jnp.int32), segment_index, jnp.full((DILATION_BINS,), -2, jnp.int32)])
    before = (padded_rows[:ROWS] == segment_index).astype(jnp.float32)
    following_rows = (padded_rows[2 * DILATION_BINS:] == segment_index).astype(jnp.float32)
    return (before, following_rows)

def reference(activations, out_grad, species, first_start, species_weight, conv_weight, point_weight, gain_one, bias_one, gain_two, bias_two, running_one, running_two):
    before, following_rows = sequence_masks(first_start)
    block_length = math.gcd(ROWS, 4096)
    block_count = ROWS // block_length
    block_ids = jnp.arange(block_count, dtype=jnp.int32)

    def forward(block_input, conv_w, point_w, g_one, b_one, g_two, b_two):
        mean_one = lax.optimization_barrier(jnp.mean(block_input, axis=0))
        var_one = lax.optimization_barrier(jnp.mean(block_input * block_input, axis=0)) - mean_one * mean_one
        inv_one = lax.rsqrt(var_one + EPSILON)
        padded_input = jnp.pad(block_input, ((DILATION_BINS, DILATION_BINS), (0, 0)))
        conv_flat = conv_w.reshape(KERN * C, H)

        def conv_block(block_index):
            start_row = (block_index * block_length).astype(jnp.int32)
            broad_rows = lax.dynamic_slice_in_dim(padded_input, start_row, block_length + 2 * DILATION_BINS, 0)
            activation_broad = low(gelu(g_one * ((broad_rows - mean_one) * inv_one) + b_one))
            previous_mask = lax.dynamic_slice_in_dim(before, start_row, block_length, 0)
            next_mask = lax.dynamic_slice_in_dim(following_rows, start_row, block_length, 0)
            stacked_rows = jnp.concatenate([previous_mask[:, None] * activation_broad[:block_length], activation_broad[DILATION_BINS:DILATION_BINS + block_length], next_mask[:, None] * activation_broad[2 * DILATION_BINS:]], axis=1)
            return low_back(jnp.dot(stacked_rows, conv_flat, precision=HIGHEST))
        conv_out = lax.map(jax.checkpoint(conv_block), block_ids).reshape(ROWS, H)
        mean_two = lax.optimization_barrier(jnp.mean(conv_out, axis=0))
        var_two = lax.optimization_barrier(jnp.mean(conv_out * conv_out, axis=0)) - mean_two * mean_two
        inv_two = lax.rsqrt(var_two + EPSILON)

        def point_block(block_index):
            start_row = (block_index * block_length).astype(jnp.int32)
            piece = lax.dynamic_slice_in_dim(conv_out, start_row, block_length, 0)
            act_two = low(gelu(g_two * ((piece - mean_two) * inv_two) + b_two))
            return low_back(jnp.dot(act_two, point_w, precision=HIGHEST))
        branch = lax.map(jax.checkpoint(point_block), block_ids).reshape(ROWS, C)
        return (block_input + branch, (mean_one, var_one, mean_two, var_two))
    x_float = activations.astype(jnp.float32)
    result, pullback, stats = jax.vjp(forward, x_float, conv_weight.astype(jnp.float32), point_weight.astype(jnp.float32), gain_one, bias_one, gain_two, bias_two, has_aux=True)
    out_cot = out_grad.astype(jnp.float32) * species_weight[species]
    grads = pullback(out_cot)
    mean_one, var_one, mean_two, var_two = stats
    unbias = ROWS / (ROWS - 1.0)
    running_one_new = MOMENTUM * running_one + (1.0 - MOMENTUM) * jnp.stack([mean_one, var_one * unbias])
    running_two_new = MOMENTUM * running_two + (1.0 - MOMENTUM) * jnp.stack([mean_two, var_two * unbias])
    return (result.astype(jnp.bfloat16), grads[0].astype(jnp.bfloat16), grads[1], grads[2], grads[3], grads[4], grads[5], grads[6], running_one_new, running_two_new)
```

```python
import functools

import jax
import jax.numpy as jnp
from jax import lax
from jax.experimental import pallas as pl
from jax.experimental.pallas import tpu as pltpu
from jax.sharding import PartitionSpec as P

DIL = 11
SEQ_LEN = 1024
EPSILON = 0.001
MOMENTUM = 0.9
PAD = 16
HALF_SLOPE = 0.851
BF = jnp.bfloat16
F32 = jnp.float32
MESH = pl.DeviceIdType.MESH


def gelu_all(u):
    t = jnp.tanh(u)
    s = 0.5 * t + 0.5
    return (u * s) * (1.0 / HALF_SLOPE), s + u * (0.5 - 0.5 * t * t)


def colsum(v):
    return jnp.sum(v.reshape(v.shape[0] // 8, 8, v.shape[1]), axis=0)


def squash(v):
    return jnp.sum(v, axis=0, keepdims=True)


class Kernel:
    def __init__(self, mesh, rows, channels, hidden, packed):
        self.ndp, self.nsub = mesh.shape["dp"], mesh.shape["sub"]
        self.rows, self.C, self.H = rows, channels, hidden
        self.packed = packed
        self.total = rows * self.ndp * self.nsub
        self.chips = self.ndp * self.nsub // 2
        self.nz = self.ndp // 2
        self.cw, self.hw = channels // self.ndp, hidden // self.nsub

    def scratch(self):
        R, C, H = self.rows, self.C, self.H
        V, D = pltpu.VMEM, pltpu.SemaphoreType.DMA
        s = dict(
            x=V((R, C), BF),
            og=V((R, C), BF),
            act=V((R, C), BF),
            slope=V((R, C), BF),
            big=V((R + 2 * PAD, 3 * H), F32),
            conv=V((R, H), F32),
            p2g=V((R, H), F32),
            act2=V((R, H), BF),
            bg=V((R, C), BF),
            back=V((R, 3 * H), BF),
            outv=V((R, C), BF),
            mb=V((R, 128), F32),
            ma=V((R, 128), F32),
            hs=V((2, PAD, H), F32),
            hc=V((2, PAD, H), F32),
            acc1=V((2, 8, C), F32),
            acc2=V((2, 8, H), F32),
            c1=V((2, 2, C), F32),
            c2=V((2, 2, H), F32),
            c3=V((2, 2, H), F32),
            c4=V((2, 2, C), F32),
            s1=V((self.chips, 2, C), F32),
            s2=V((self.chips, 2, H), F32),
            s3=V((self.chips, 2, H), F32),
            s4=V((self.chips, 2, C), F32),
            ar_send=D((4, 2)),
            ar_recv=D((4, 2)),
            xsem=D((4,)),
            ogsem=D,
            osem=D((8,)),
            isem=D((8,)),
            halo_send=D((2, 2)),
            halo_recv=D((2, 2)),
        )
        if self.packed:
            nz, n = self.nz, self.cw
            s.update(
                wf=V((C, 3 * H), BF),
                pf=V((H, C), BF),
                g=V((3, 2, 2, 2, nz, n, 128), BF),
                ag_send=D((3, 3)),
                ag_z=D((3,)),
                ag_xy=D((3, 3)),
                ag_core=D((3, 4)),
                rs=V((3, 2, 2, 2, nz, n, 128), BF),
                rc=V((3, 2, 2, nz, n, 128), BF),
                rd=V((3, nz, n, 128), BF),
                rxy=V((3, 2, nz, n, 128), BF),
                rz=V((3, nz, n, 128), BF),
                rs_send=D((3, 4)),
                rs_core=D((3,)),
                rs_d=D((3,)),
                rs_xy=D((3, 2)),
                rs_z=D((3,)),
            )
        return s

    def place(self):
        self.dp, self.sub = lax.axis_index("dp"), lax.axis_index("sub")
        self.z, self.y = self.dp // 2, lax.rem(self.dp, 2)
        self.x, self.c = self.sub // 2, lax.rem(self.sub, 2)
        n = self.ndp * self.nsub
        me = self.dp * self.nsub + self.sub
        nxt, prv = lax.rem(me + 1, n), lax.rem(me + n - 1, n)
        self.core_nbr = (self.dp, self.x * 2 + 1 - self.c)
        self.x_nbr = (self.dp, (self.nsub // 2 - 1 - self.x) * 2 + self.c)
        self.y_nbr = (self.z * 2 + 1 - self.y, self.sub)
        self.next = (nxt // self.nsub, lax.rem(nxt, self.nsub))
        self.prev = (prv // self.nsub, lax.rem(prv, self.nsub))
        self.chip = self.dp * (self.nsub // 2) + self.x

    def chip_device(self, chip):
        half = self.nsub // 2
        return (chip // half, lax.rem(chip, half) * 2 + self.c)

    def z_device(self, d):
        return (lax.rem(self.z + d, self.nz) * 2 + self.y, self.sub)

    def greet(self):
        b = pltpu.get_barrier_semaphore()

        def hello(device):
            pl.semaphore_signal(b, inc=1, device_id=device, device_id_type=MESH)

        hello(self.core_nbr)
        n = self.ndp * self.nsub
        me = self.dp * self.nsub + self.sub
        far = lax.rem(me + jnp.where(self.c == 1, 1, n - 1), n)
        hello((far // self.nsub, lax.rem(far, self.nsub)))

        def one(d, carry):
            hello(self.chip_device(lax.rem(self.chip + d, self.chips)))
            return carry

        lax.fori_loop(1, self.chips, one, 0)

    def greeted(self):
        pl.semaphore_wait(pltpu.get_barrier_semaphore(), self.chips + 1)

    def copy_to(self, src, dst, send, recv, device):
        return pltpu.make_async_remote_copy(
            src, dst, send, recv, device_id=device, device_id_type=MESH
        )

    def ar_begin(self, r, i, top, low):
        cs = (r.c1, r.c2, r.c3, r.c4)[i]
        cs[self.c, 0:1, :] = top
        cs[self.c, 1:2, :] = low
        mine = cs.at[self.c]
        self.copy_to(mine, mine, r.ar_send.at[i, 0], r.ar_recv.at[i, 0], self.core_nbr).start()

    def ar_middle(self, r, i):
        cs, sl = (r.c1, r.c2, r.c3, r.c4)[i], (r.s1, r.s2, r.s3, r.s4)[i]
        pltpu.make_async_copy(cs.at[0], cs.at[0], r.ar_recv.at[i, 0]).wait()
        sl[self.chip] = cs[0] + cs[1]
        mine = sl.at[self.chip]

        def one(d, carry):
            device = self.chip_device(lax.rem(self.chip + d, self.chips))
            self.copy_to(mine, mine, r.ar_send.at[i, 1], r.ar_recv.at[i, 1], device).start()
            return carry

        lax.fori_loop(1, self.chips, one, 0)

    def ar_end(self, r, i):
        sl = (r.s1, r.s2, r.s3, r.s4)[i]
        most = sl.at[pl.ds(0, self.chips - 1)]
        pltpu.make_async_copy(most, most, r.ar_recv.at[i, 1]).wait()
        if self.chips <= 16:
            total = sl[0]
            for k in range(1, self.chips):
                total = total + sl[k]
        else:
            total = lax.fori_loop(1, self.chips, lambda k, t: t + sl[k], sl[0])
        return total[0:1, :], total[1:2, :]

    def ar_drain(self, r, i):
        cs, sl = (r.c1, r.c2, r.c3, r.c4)[i], (r.s1, r.s2, r.s3, r.s4)[i]
        pltpu.make_async_copy(cs.at[0], cs.at[0], r.ar_send.at[i, 0]).wait()
        most = sl.at[pl.ds(0, self.chips - 1)]
        pltpu.make_async_copy(most, most, r.ar_send.at[i, 1]).wait()

    def mine(self, r, k):
        return r.g.at[k, self.y, self.x, self.c]

    def ag_start(self, r, conv, point):
        for k in range(3):
            r.g[k, self.y, self.x, self.c, self.z] = jnp.concatenate(
                [conv[k], point[:, 32 * k : 32 * k + 32]], axis=1
            )
            slot = r.g.at[k, self.y, self.x, self.c, self.z]
            for d in range(1, self.nz):
                self.copy_to(slot, slot, r.ag_send.at[k, 0], r.ag_z.at[k], self.z_device(d)).start()

    def to_core(self, r, k, j, grp):
        self.copy_to(grp, grp, r.ag_send.at[k, 2], r.ag_core.at[k, j], self.core_nbr).start()

    def ag_plane(self, r, k):
        grp = self.mine(r, k)
        part = grp.at[pl.ds(0, self.nz - 1)]
        pltpu.make_async_copy(part, part, r.ag_z.at[k]).wait()
        self.copy_to(grp, grp, r.ag_send.at[k, 1], r.ag_xy.at[k, 0], self.y_nbr).start()
        self.copy_to(grp, grp, r.ag_send.at[k, 1], r.ag_xy.at[k, 1], self.x_nbr).start()
        self.to_core(r, k, 0, grp)

    def ag_diagonal(self, r, k):
        by_y = r.g.at[k, 1 - self.y, self.x, self.c]
        by_x = r.g.at[k, self.y, 1 - self.x, self.c]
        first, second = (by_y, by_x) if k % 2 == 0 else (by_x, by_y)
        f, s = (0, 1) if k % 2 == 0 else (1, 0)
        to = self.x_nbr if k % 2 == 0 else self.y_nbr
        pltpu.make_async_copy(first, first, r.ag_xy.at[k, f]).wait()
        self.copy_to(first, first, r.ag_send.at[k, 1], r.ag_xy.at[k, 2], to).start()
        self.to_core(r, k, 1, first)
        pltpu.make_async_copy(second, second, r.ag_xy.at[k, s]).wait()
        self.to_core(r, k, 2, second)

    def ag_last(self, r, k):
        grp = r.g.at[k, 1 - self.y, 1 - self.x, self.c]
        pltpu.make_async_copy(grp, grp, r.ag_xy.at[k, 2]).wait()
        self.to_core(r, k, 3, grp)

    def ag_unpack(self, r, k):
        for j in range(4):
            grp = self.mine(r, k)
            pltpu.make_async_copy(grp, grp, r.ag_core.at[k, j]).wait()
        n, H = self.cw, self.H
        for z in range(self.nz):
            for y in range(2):
                dp = z * 2 + y
                parts = [r.g[k, y, s // 2, s % 2, z] for s in range(4)]
                r.wf[dp * n : dp * n + n, k * H : k * H + H] = jnp.concatenate(
                    [p[:, 0:96] for p in parts], axis=1
                )
                for s in range(4):
                    at = dp * n + 32 * k
                    r.pf[s * 96 : s * 96 + 96, at : at + 32] = parts[s][:, 96:128]

    def ag_drain(self, r):
        for k in range(3):
            grp = self.mine(r, k)
            part = grp.at[pl.ds(0, self.nz - 1)]
            pltpu.make_async_copy(part, part, r.ag_send.at[k, 0]).wait()
            for _ in range(3):
                pltpu.make_async_copy(grp, grp, r.ag_send.at[k, 1]).wait()
            for _ in range(4):
                pltpu.make_async_copy(grp, grp, r.ag_send.at[k, 2]).wait()

    def rs_core(self, r, k):
        for y in range(2):
            for x in range(2):
                self.copy_to(
                    r.rs.at[k, y, x, 1 - self.c],
                    r.rc.at[k, y, x],
                    r.rs_send.at[k, 0],
                    r.rs_core.at[k],
                    self.core_nbr,
                ).start()

    def add(self, r, k, y, x, *others):
        for z in range(self.nz):
            v = r.rs[k, y, x, self.c, z].astype(F32)
            for o in others:
                v = v + o[z].astype(F32)
            r.rs[k, y, x, self.c, z] = v.astype(BF)

    def rs_diagonal(self, r, k):
        pltpu.make_async_copy(r.rc.at[k], r.rc.at[k], r.rs_core.at[k]).wait()
        for y in range(2):
            for x in range(2):
                self.add(r, k, y, x, r.rc.at[k, y, x])
        to = self.x_nbr if k % 2 == 0 else self.y_nbr
        src = r.rs.at[k, 1 - self.y, 1 - self.x, self.c]
        self.copy_to(src, r.rd.at[k], r.rs_send.at[k, 1], r.rs_d.at[k], to).start()

    def rs_plane(self, r, k):
        pltpu.make_async_copy(r.rd.at[k], r.rd.at[k], r.rs_d.at[k]).wait()
        if k % 2 == 0:
            self.add(r, k, 1 - self.y, self.x, r.rd.at[k])
        else:
            self.add(r, k, self.y, 1 - self.x, r.rd.at[k])
        by_y = r.rs.at[k, 1 - self.y, self.x, self.c]
        by_x = r.rs.at[k, self.y, 1 - self.x, self.c]
        self.copy_to(by_y, r.rxy.at[k, 0], r.rs_send.at[k, 2], r.rs_xy.at[k, 0], self.y_nbr).start()
        self.copy_to(by_x, r.rxy.at[k, 1], r.rs_send.at[k, 2], r.rs_xy.at[k, 1], self.x_nbr).start()

    def rs_column(self, r, k):
        for j in range(2):
            pltpu.make_async_copy(r.rxy.at[k, j], r.rxy.at[k, j], r.rs_xy.at[k, j]).wait()
        self.add(r, k, self.y, self.x, r.rxy.at[k, 0], r.rxy.at[k, 1])
        for d in range(1, self.nz):
            to = lax.rem(self.z + d, self.nz)
            src = r.rs.at[k, self.y, self.x, self.c, to]
            self.copy_to(src, r.rz.at[k, self.z], r.rs_send.at[k, 3], r.rs_z.at[k], self.z_device(d)).start()
        r.rz[k, self.z] = r.rs[k, self.y, self.x, self.c, self.z]

    def rs_end(self, r, k):
        part = r.rz.at[k, pl.ds(0, self.nz - 1)]
        pltpu.make_async_copy(part, part, r.rs_z.at[k]).wait()
        v = r.rz[k, 0].astype(F32)
        for z in range(1, self.nz):
            v = v + r.rz[k, z].astype(F32)
        r.conv_grad[k] = v[:, 0:96]
        r.point_grad[:, 32 * k : 32 * k + 32] = v[:, 96:128]

    def rs_drain(self, r):
        for k in range(3):
            grp = r.rd.at[k]
            pltpu.make_async_copy(r.rc.at[k], r.rc.at[k], r.rs_send.at[k, 0]).wait()
            pltpu.make_async_copy(grp, grp, r.rs_send.at[k, 1]).wait()
            for _ in range(2):
                pltpu.make_async_copy(grp, grp, r.rs_send.at[k, 2]).wait()
            part = r.rz.at[k, pl.ds(0, self.nz - 1)]
            pltpu.make_async_copy(part, part, r.rs_send.at[k, 3]).wait()

    def halo_begin(self, r, i, low_lanes, high_lanes):
        R, H = self.rows, self.H
        buf = r.hs if i == 0 else r.hc
        wide = lambda m: jnp.concatenate([m] * (H // 128), axis=1)
        buf[0] = r.big[PAD : 2 * PAD, low_lanes : low_lanes + H] * wide(r.mb[0:PAD])
        buf[1] = r.big[R : R + PAD, high_lanes : high_lanes + H] * wide(r.ma[R - PAD : R])
        self.copy_to(
            buf.at[0], r.halo.at[i, 0], r.halo_send.at[i, 0], r.halo_recv.at[i, 0], self.prev
        ).start()
        self.copy_to(
            buf.at[1], r.halo.at[i, 1], r.halo_send.at[i, 1], r.halo_recv.at[i, 1], self.next
        ).start()

    def halo_end(self, r, i, low_lanes, high_lanes):
        R, H = self.rows, self.H
        for j in range(2):
            pltpu.make_async_copy(r.halo.at[i, j], r.halo.at[i, j], r.halo_recv.at[i, j]).wait()
        r.big[R + PAD : R + 2 * PAD, low_lanes : low_lanes + H] = r.halo[i, 0]
        r.big[0:PAD, high_lanes : high_lanes + H] = r.halo[i, 1]

    def halo_drain(self, r, i):
        for j in range(2):
            pltpu.make_async_copy(r.halo.at[i, j], r.halo.at[i, j], r.halo_send.at[i, j]).wait()


def loop(rows, tile, f):
    def one(i, carry):
        f(pl.multiple_of(i * tile, tile))
        return carry

    lax.fori_loop(0, rows // tile, one, 0)


def row_tile(start, tile):
    return start + lax.broadcasted_iota(jnp.int32, (tile, 128), 0)


def wide(m, n):
    return jnp.concatenate([m] * (n // 128), axis=1)


class Refs:
    pass


def kernel(k, n_in, n_out, names, *refs):
    r = Refs()
    ins, outs, scr = refs[:n_in], refs[n_in : n_in + n_out], refs[n_in + n_out :]
    for name, ref in zip(names, scr):
        setattr(r, name, ref)
    (x_hbm, og_hbm, species, first, sw, conv_w, point_w, g1, b1, g2, b2, run1, run2) = ins
    (out_hbm, ig_hbm, r.conv_grad, r.point_grad, gg1, gb1, gg2, gb2, new1, new2) = outs
    R, C, H, N = k.rows, k.C, k.H, k.total
    k.place()
    k.greet()
    Q = R // 4
    xcopies = [
        pltpu.make_async_copy(x_hbm.at[pl.ds(q * Q, Q)], r.x.at[pl.ds(q * Q, Q)], r.xsem.at[q])
        for q in range(4)
    ]
    for cp in xcopies:
        cp.start()
    ogcopy = pltpu.make_async_copy(og_hbm, r.og, r.ogsem)
    ogcopy.start()
    k.greeted()
    if k.packed:
        k.ag_start(r, conv_w, point_w)

    r.acc1[...] = jnp.zeros_like(r.acc1)
    for q in range(4):
        xcopies[q].wait()
        v = r.x[q * Q : q * Q + Q, :].astype(F32)
        r.acc1[0] += colsum(v)
        r.acc1[1] += colsum(v * v)
    k.ar_begin(r, 0, squash(r.acc1[0]), squash(r.acc1[1]))

    fs = first[0]
    starts = [fs + SEQ_LEN * j for j in range(R // SEQ_LEN)]

    def masks(at):
        row = row_tile(at, 128)
        before = jnp.ones((128, 128), F32)
        after = jnp.ones((128, 128), F32)
        for s in starts:
            before = jnp.where((row >= s) & (row < s + DIL), 0.0, before)
            after = jnp.where((row >= s - DIL) & (row < s), 0.0, after)
        r.mb[pl.ds(at, 128), :] = before
        r.ma[pl.ds(at, 128), :] = after

    loop(R, 128, masks)
    k.ar_middle(r, 0)
    if k.packed:
        for j in range(3):
            k.ag_plane(r, j)
    sum1, sq1 = k.ar_end(r, 0)
    mean1 = sum1 / N
    var1 = sq1 / N - mean1 * mean1
    inv1 = lax.rsqrt(var1 + EPSILON)
    scale1 = (HALF_SLOPE * g1[...]) * inv1
    shift1 = HALF_SLOPE * b1[...] - mean1 * scale1

    def act_tile(at):
        rows = pl.ds(at, 256)
        a, s = gelu_all(r.x[rows, :].astype(F32) * scale1 + shift1)
        r.act[rows, :] = a.astype(BF)
        r.slope[rows, :] = s.astype(BF)

    loop(R, 256, act_tile)
    if k.packed:
        for j in range(3):
            k.ag_diagonal(r, j)
        for j in range(3):
            k.ag_last(r, j)
        for j in range(3):
            k.ag_unpack(r, j)
        wf, pf = r.wf, r.pf
    else:
        wf, pf = conv_w, point_w

    for at in (0, R - Q):
        r.big[PAD + at : PAD + at + Q, :] = jnp.dot(
            r.act[at : at + Q, :], wf[...], preferred_element_type=F32
        )
    k.halo_begin(r, 0, 2 * H, 0)
    for at in range(Q, R - Q, Q):
        r.big[PAD + at : PAD + at + Q, :] = jnp.dot(
            r.act[at : at + Q, :], wf[...], preferred_element_type=F32
        )
    k.halo_end(r, 0, 2 * H, 0)
    r.acc2[...] = jnp.zeros_like(r.acc2)
    T = 256

    def gather_taps(at):
        rows = pl.ds(at, T)
        lo = r.big[pl.ds(at, T + 2 * PAD), 0:H][PAD - DIL : PAD - DIL + T]
        mid = r.big[pl.ds(at + PAD, T), H : 2 * H]
        hi = r.big[pl.ds(at, T + 2 * PAD), 2 * H : 3 * H][PAD + DIL : PAD + DIL + T]
        v = lo * wide(r.mb[rows, :], H) + mid + hi * wide(r.ma[rows, :], H)
        r.conv[rows, :] = v
        r.acc2[0] += colsum(v)
        r.acc2[1] += colsum(v * v)

    loop(R, T, gather_taps)
    k.ar_begin(r, 1, squash(r.acc2[0]), squash(r.acc2[1]))
    k.ar_middle(r, 1)

    ogcopy.wait()
    at_start = [species[0]] + [species[s] for s in starts]
    weights = [jnp.where(sp == 0, sw[0:1, :], sw[1:2, :]) for sp in at_start]

    def row_weight(at, tile):
        row = row_tile(at, tile)
        w = jnp.broadcast_to(weights[0], (tile, C))
        for s, v in zip(starts, weights[1:]):
            w = jnp.where(wide(row, C) >= s, v, w)
        return w

    def branch_grad(at):
        rows = pl.ds(at, 128)
        r.bg[rows, :] = (r.og[rows, :].astype(F32) * row_weight(at, 128)).astype(BF)

    loop(R, 128, branch_grad)

    def act_two_grad(at):
        rows = pl.ds(at, 1024)
        r.p2g[rows, :] = lax.dot_general(
            r.bg[rows, :], pf[...], (((1,), (1,)), ((), ())), preferred_element_type=F32
        )

    loop(R, 1024, act_two_grad)
    sum2, sq2 = k.ar_end(r, 1)
    mean2 = sum2 / N
    var2 = sq2 / N - mean2 * mean2
    inv2 = lax.rsqrt(var2 + EPSILON)
    minv2 = mean2 * inv2
    gain2, bias2 = HALF_SLOPE * g2[...], HALF_SLOPE * b2[...]
    r.acc2[...] = jnp.zeros_like(r.acc2)

    def second_norm(at):
        rows = pl.ds(at, 256)
        zh = r.conv[rows, :] * inv2 - minv2
        a, s = gelu_all(zh * gain2 + bias2)
        r.act2[rows, :] = a.astype(BF)
        p = r.p2g[rows, :] * s
        r.p2g[rows, :] = p
        r.acc2[0] += colsum(p)
        r.acc2[1] += colsum(p * zh)

    loop(R, 256, second_norm)
    k.ar_begin(r, 2, squash(r.acc2[0]), squash(r.acc2[1]))
    k.ar_middle(r, 2)

    ocopies = []
    for q in range(2):
        rows = pl.ds(q * 1024, 1024)
        br = jnp.dot(r.act2[rows, :], pf[...], preferred_element_type=F32)
        r.outv[rows, :] = (r.x[rows, :].astype(F32) + br).astype(BF)
        cp = pltpu.make_async_copy(r.outv.at[rows], out_hbm.at[rows], r.osem.at[q])
        cp.start()
        ocopies.append(cp)
    pg = lax.dot_general(
        r.act2[...], r.bg[...], (((0,), (0,)), ((), ())), preferred_element_type=F32
    )
    if k.packed:
        pgb = pg.astype(BF)
        for j in range(3):
            for z in range(k.nz):
                for y in range(2):
                    for s in range(4):
                        lane = (z * 2 + y) * 96 + 32 * j
                        r.rs[j, y, s // 2, s % 2, z, :, 96:128] = pgb[
                            s * 96 : s * 96 + 96, lane : lane + 32
                        ]
    else:
        r.point_grad[...] = pg
    bsum, gsum = k.ar_end(r, 2)
    gb2[...] = bsum
    gg2[...] = gsum
    a2 = inv2 * g2[...]
    lin2 = -a2 * (gsum / N) * inv2
    off2 = -a2 * (bsum / N) + a2 * (gsum / N) * minv2

    def cot(at):
        rows = pl.ds(at, 256)
        r.big[pl.ds(at + PAD, 256), 0:H] = (
            r.p2g[rows, :] * a2 + r.conv[rows, :] * lin2 + off2
        )

    loop(R, 256, cot)
    k.halo_begin(r, 1, 0, 0)
    k.halo_end(r, 1, 0, 0)
    T2 = 128

    def shifted(at):
        rows = pl.ds(at, T2)
        v = r.big[pl.ds(at, T2 + 2 * PAD), 0:H]
        r.back[rows, 0:H] = (v[PAD + DIL : PAD + DIL + T2] * wide(r.ma[rows, :], H)).astype(BF)
        r.back[rows, H : 2 * H] = v[PAD : PAD + T2].astype(BF)
        r.back[rows, 2 * H : 3 * H] = (v[PAD - DIL : PAD - DIL + T2] * wide(r.mb[rows, :], H)).astype(BF)

    loop(R, T2, shifted)

    M = 384
    for m in range(0, C, M):
        cg = lax.dot_general(
            r.act[:, m : m + M], r.back[...], (((0,), (0,)), ((), ())), preferred_element_type=F32
        )
        if k.packed:
            cgb = cg.astype(BF)
            for j in range(3):
                for d in range(M // 96):
                    dp = m // 96 + d
                    for s in range(4):
                        lane = j * H + s * 96
                        r.rs[j, dp % 2, s // 2, s % 2, dp // 2, :, 0:96] = cgb[
                            d * 96 : d * 96 + 96, lane : lane + 96
                        ]
        else:
            for j in range(3):
                r.conv_grad[j, m : m + M, :] = cg[:, j * H : j * H + H]
    if k.packed:
        for j in range(3):
            k.rs_core(r, j)
        for j in range(3):
            k.rs_diagonal(r, j)

    minv1 = mean1 * inv1
    r.acc1[...] = jnp.zeros_like(r.acc1)
    for q in range(4):
        rows = slice(q * Q, q * Q + Q)
        ag = lax.dot_general(
            r.back[rows, :], wf[...], (((1,), (1,)), ((), ())), preferred_element_type=F32
        )
        p = ag * r.slope[rows, :].astype(F32)
        r.big[rows, 0:C] = p
        r.acc1[0] += colsum(p)
        r.acc1[1] += colsum(p * (r.x[rows, :].astype(F32) * inv1 - minv1))
    k.ar_begin(r, 3, squash(r.acc1[0]), squash(r.acc1[1]))
    k.ar_middle(r, 3)
    if k.packed:
        for j in range(3):
            k.rs_plane(r, j)
    unbias = N / (N - 1.0)
    new1[0:1, :] = MOMENTUM * run1[0:1, :] + (1.0 - MOMENTUM) * mean1
    new1[1:2, :] = MOMENTUM * run1[1:2, :] + (1.0 - MOMENTUM) * (var1 * unbias)
    new2[0:1, :] = MOMENTUM * run2[0:1, :] + (1.0 - MOMENTUM) * mean2
    new2[1:2, :] = MOMENTUM * run2[1:2, :] + (1.0 - MOMENTUM) * (var2 * unbias)
    bsum1, gsum1 = k.ar_end(r, 3)
    gb1[...] = bsum1
    gg1[...] = gsum1
    a1 = inv1 * g1[...]
    lin1 = -a1 * (gsum1 / N) * inv1
    off1 = -a1 * (bsum1 / N) + a1 * (gsum1 / N) * minv1

    icopies = []
    for q in range(4):

        def last(at):
            rows = pl.ds(at, 128)
            v = r.og[rows, :].astype(F32) * row_weight(at, 128)
            v = v + r.big[rows, 0:C] * a1 + r.x[rows, :].astype(F32) * lin1 + off1
            r.og[rows, :] = v.astype(BF)

        lax.fori_loop(
            0, Q // 128, lambda i, c: (last(pl.multiple_of(q * Q + i * 128, 128)), c)[1], 0
        )
        rows = pl.ds(q * Q, Q)
        cp = pltpu.make_async_copy(r.og.at[rows], ig_hbm.at[rows], r.isem.at[q])
        cp.start()
        icopies.append(cp)
    if k.packed:
        for j in range(3):
            k.rs_column(r, j)
        for j in range(3):
            k.rs_end(r, j)
        k.ag_drain(r)
        k.rs_drain(r)
    for i in range(4):
        k.ar_drain(r, i)
    for i in range(2):
        k.halo_drain(r, i)
    for cp in ocopies + icopies:
        cp.wait()


def body(
    mesh,
    activations,
    out_grad,
    species,
    first_start,
    species_weight,
    conv_weight,
    point_weight,
    gain_one,
    bias_one,
    gain_two,
    bias_two,
    running_one,
    running_two,
):
    rows, C = activations.shape
    ndp, nsub = mesh.shape["dp"], mesh.shape["sub"]
    cw, hw = conv_weight.shape[1:]
    taps, H = conv_weight.shape[0], hw * nsub
    packed = cw == 96 and hw == 96 and nsub == 4 and ndp % 2 == 0
    if not packed:
        conv_weight = lax.all_gather(conv_weight, "dp", axis=1, tiled=True)
        conv_weight = lax.all_gather(conv_weight, "sub", axis=2, tiled=True)
        conv_weight = jnp.transpose(conv_weight, (1, 0, 2)).reshape(C, taps * H)
        point_weight = lax.all_gather(point_weight, "dp", axis=1, tiled=True)
        point_weight = lax.all_gather(point_weight, "sub", axis=0, tiled=True)
    k = Kernel(mesh, rows, C, H, packed)
    scratch = k.scratch()
    scratch["halo"] = pltpu.VMEM((2, 2, PAD, H), F32)
    any_, vmem, smem = (
        pl.BlockSpec(memory_space=pl.ANY),
        pl.BlockSpec(memory_space=pltpu.VMEM),
        pl.BlockSpec(memory_space=pltpu.SMEM),
    )
    row = lambda v: v.reshape(1, -1)
    sds = jax.ShapeDtypeStruct
    out_shape = (
        sds((rows, C), BF),
        sds((rows, C), BF),
        sds((taps, cw, hw) if packed else (taps, C, H), F32),
        sds((hw, cw) if packed else (H, C), F32),
        sds((1, C), F32),
        sds((1, C), F32),
        sds((1, H), F32),
        sds((1, H), F32),
        sds((2, C), F32),
        sds((2, H), F32),
    )
    outs = pl.pallas_call(
        functools.partial(kernel, k, 13, 10, list(scratch)),
        out_shape=out_shape,
        in_specs=[any_, any_, smem, smem] + [vmem] * 9,
        out_specs=[any_, any_] + [vmem] * 8,
        scratch_shapes=list(scratch.values()),
        compiler_params=pltpu.CompilerParams(
            collective_id=0, has_side_effects=True, vmem_limit_bytes=62 * 2**20
        ),
    )(
        activations,
        out_grad,
        species,
        first_start,
        species_weight,
        conv_weight,
        point_weight,
        row(gain_one),
        row(bias_one),
        row(gain_two),
        row(bias_two),
        running_one,
        running_two,
    )
    output, input_grad, conv_grad, point_grad, gg1, gb1, gg2, gb2, new1, new2 = outs
    if not packed:
        conv_grad = lax.psum_scatter(conv_grad, "dp", scatter_dimension=1, tiled=True)
        point_grad = lax.psum_scatter(point_grad, "dp", scatter_dimension=1, tiled=True)
        conv_grad = lax.psum_scatter(conv_grad, "sub", scatter_dimension=2, tiled=True)
        point_grad = lax.psum_scatter(point_grad, "sub", scatter_dimension=0, tiled=True)
    flat = lambda v: v.reshape(-1)
    return (
        output,
        input_grad,
        conv_grad,
        point_grad,
        flat(gg1),
        flat(gb1),
        flat(gg2),
        flat(gb2),
        new1,
        new2,
    )


def solution(mesh):
    in_specs = (
        P(("dp", "sub"), None),
        P(("dp", "sub"), None),
        P(("dp", "sub")),
        P(("dp", "sub")),
        P(),
        P(None, "dp", "sub"),
        P("sub", "dp"),
        P(),
        P(),
        P(),
        P(),
        P(),
        P(),
    )
    out_specs = (
        P(("dp", "sub"), None),
        P(("dp", "sub"), None),
        P(None, "dp", "sub"),
        P("sub", "dp"),
        P(),
        P(),
        P(),
        P(),
        P(),
        P(),
    )
    return jax.shard_map(
        functools.partial(body, mesh), mesh=mesh, in_specs=in_specs, out_specs=out_specs, check_vma=False
    )
```

```python
import functools

import jax
import jax.numpy as jnp
from jax import lax
from jax.experimental import pallas as pl
from jax.experimental.pallas import tpu as pltpu
from jax.sharding import PartitionSpec as P

DIL = 11
SEQ_LEN = 1024
EPSILON = 0.001
MOMENTUM = 0.9
PAD = 16
HALF_SLOPE = 0.851
BF = jnp.bfloat16
F32 = jnp.float32
MESH = pl.DeviceIdType.MESH
PARTS = ((0, 48), (48, 48), (96, 48), (144, 48), (192, 32), (224, 80))
CONV_ROWS, SLOT_ROWS = 224, 304
SIDE = 112


def gelu_all(u):
    t = jnp.tanh(u)
    s = 0.5 * t + 0.5
    return (u * s) * (1.0 / HALF_SLOPE), s + u * (0.5 - 0.5 * t * t)


def colsum(v):
    return jnp.sum(v.reshape(v.shape[0] // 8, 8, v.shape[1]), axis=0)


def squash(v):
    return jnp.sum(v, axis=0, keepdims=True)


def loop(first, last, tile, f):
    def one(i, carry):
        f(pl.multiple_of(first + i * tile, tile))
        return carry

    lax.fori_loop(0, (last - first) // tile, one, 0)


def row_tile(start, tile):
    return start + lax.broadcasted_iota(jnp.int32, (tile, 128), 0)


def wide(m, n):
    return jnp.concatenate([m] * (n // 128), axis=1)


class Kernel:
    def __init__(self, mesh, rows, channels, hidden, packed):
        self.ndp, self.nsub = mesh.shape["dp"], mesh.shape["sub"]
        self.rows, self.C, self.H = rows, channels, hidden
        self.packed = packed
        self.total = rows * self.ndp * self.nsub
        self.chips = self.ndp * self.nsub // 2
        self.nz = self.ndp // 2
        self.cw, self.hw = channels // self.ndp, hidden // self.nsub
        self.half = self.cw // 2
        self.sent, self.coming, self.local = [], {}, {}

    def scratch(self):
        R, C, H = self.rows, self.C, self.H
        V, D = pltpu.VMEM, pltpu.SemaphoreType.DMA
        s = dict(
            x=V((R, C), BF),
            og=V((R, C), BF),
            act=V((R, C), BF),
            slope=V((R, C), BF),
            big=V((R + 2 * PAD, 3 * H), F32),
            conv=V((R, H), F32),
            p2g=V((R, H), F32),
            act2=V((R, H), BF),
            back=V((R, 3 * H), BF),
            mb=V((R, 128), F32),
            ma=V((R, 128), F32),
            hs=V((2, PAD, H), F32),
            halo=V((2, PAD, H), F32),
            es=V((2, PAD, 2 * H + 128), F32),
            edge=V((2, PAD, 2 * H + 128), F32),
            acc1=V((2, 8, C), F32),
            acc2=V((2, 8, H), F32),
            c0=V((2, 2, C), F32),
            c1=V((2, 2, H), F32),
            c2=V((2, 2, H), F32),
            c3=V((2, 2, C), F32),
            s0=V((self.chips, 2, C), F32),
            s1=V((self.chips, 2, H), F32),
            s2=V((self.chips, 2, H), F32),
            s3=V((self.chips, 2, C), F32),
            wf=V((C, 3 * H), BF),
            pf=V((H, C), BF),
            sw=V((2, C), F32),
            g1=V((C,), F32),
            b1=V((C,), F32),
            g2=V((H,), F32),
            b2=V((H,), F32),
            run1=V((2, C), F32),
            run2=V((2, H), F32),
            species=pltpu.SMEM((R,), jnp.int32),
            first=pltpu.SMEM((1,), jnp.int32),
            ar_send=D((4, 2)),
            ar_recv=D((4, 2)),
            insem=D((24,)),
            halo_send=D((2, 2)),
            halo_recv=D((2, 2)),
        )
        if self.packed:
            nz = self.nz
            s.update(
                cshard=V((3, self.cw, self.hw), BF),
                pshard=V((self.hw, self.cw), BF),
                ag_send=D((len(PARTS), 3)),
                ag_z=D((len(PARTS),)),
                ag_own=D((len(PARTS), 2)),
                ag_oth=D((len(PARTS), 2)),
                ag_d=D((len(PARTS),)),
                ag_core=D((len(PARTS), 4)),
                ra=V((2, 2, 2, 2, 2, SIDE, 128), F32),
                rs=V((2, 2, 2, 2, 2, SIDE, 128), BF),
                rc=V((2, 2, 2, 2, 2, SIDE, 128), BF),
                st=V((2, 2, 2, 2, 2, SIDE, 128), BF),
                rd=V((2, 2, 2, SIDE, 128), BF),
                rxy=V((2, 2, 2, 2, SIDE, 128), BF),
                rz=V((2, 3, SIDE, 128), BF),
                rs_send=D((2, 2, 3)),
                rs_core=D((2, 2)),
                rs_d=D((2, 2)),
                rs_xy=D((2, 2, 2)),
                rz_send=D((2,)),
                rs_z=D((2,)),
                pa=V((2, 2, nz, 80, 128), F32),
                ps=V((2, 2, nz, 80, 128), BF),
                pc=V((2, 2, nz, 80, 128), BF),
                pt=V((2, 2, nz, 80, 128), BF),
                pd=V((nz, 80, 128), BF),
                pxy=V((2, nz, 80, 128), BF),
                pz=V((3, 80, 128), BF),
                p_send=D((4,)),
                p_recv=D((5,)),
            )
            s.update({f"w{j}": V((2, 2, 2, nz, n, 128), BF) for j, (_, n) in enumerate(PARTS)})
        return s

    def place(self):
        self.dp, self.sub = lax.axis_index("dp"), lax.axis_index("sub")
        self.z, self.y = self.dp // 2, lax.rem(self.dp, 2)
        self.x, self.c = self.sub // 2, lax.rem(self.sub, 2)
        n = self.ndp * self.nsub
        me = self.dp * self.nsub + self.sub
        nxt, prv = lax.rem(me + 1, n), lax.rem(me + n - 1, n)
        far = lax.rem(me + jnp.where(self.c == 1, 1, n - 1), n)
        self.core_nbr = (self.dp, self.x * 2 + 1 - self.c)
        self.x_nbr = (self.dp, (1 - self.x) * 2 + self.c)
        self.y_nbr = (self.z * 2 + 1 - self.y, self.sub)
        self.next = (nxt // self.nsub, lax.rem(nxt, self.nsub))
        self.prev = (prv // self.nsub, lax.rem(prv, self.nsub))
        self.far = (far // self.nsub, lax.rem(far, self.nsub))
        self.chip = self.dp * (self.nsub // 2) + self.x

    def z_device(self, d):
        return (lax.rem(self.z + d, self.nz) * 2 + self.y, self.sub)

    def each_chip(self, f):
        if self.chips == 16 and self.nsub == 4:
            z, y, x = self.z, self.y, self.x
            zs = (z, z + 1 - 2 * lax.rem(z, 2), lax.rem(z + 2, 4), 3 - z)
            for d in range(15, 0, -1):
                yy = 1 - y if (d // 2) % 2 else y
                xx = 1 - x if d % 2 else x
                f((zs[d // 4] * 2 + yy, xx * 2 + self.c))
        else:
            side = self.nsub // 2

            def one(d, carry):
                chip = lax.rem(self.chip + d, self.chips)
                f((chip // side, lax.rem(chip, side) * 2 + self.c))
                return carry

            lax.fori_loop(1, self.chips, one, 0)

    def greet(self):
        b = pltpu.get_barrier_semaphore()

        def hello(device):
            pl.semaphore_signal(b, inc=1, device_id=device, device_id_type=MESH)

        self.each_chip(hello)
        hello(self.far)
        hello(self.core_nbr)

    def greeted(self):
        pl.semaphore_wait(pltpu.get_barrier_semaphore(), self.chips + 1)

    def put(self, src, dst, send, recv, device, key=None, ref=None):
        pltpu.make_async_remote_copy(
            src, dst, send, recv, device_id=device, device_id_type=MESH
        ).start()
        self.sent.append((src, send))
        if key is not None:
            self.coming[key] = (dst if ref is None else ref, recv)

    def arrived(self, *keys):
        for key in keys:
            ref, sem = self.coming.pop(key)
            pltpu.make_async_copy(ref, ref, sem).wait()

    def fetch(self, key, src, dst, sem):
        self.local[key] = cp = pltpu.make_async_copy(src, dst, sem)
        cp.start()

    def have(self, *keys):
        for key in keys:
            self.local.pop(key).wait()

    def drain(self):
        self.have(*list(self.local))
        self.arrived(*list(self.coming))
        for ref, sem in self.sent:
            pltpu.make_async_copy(ref, ref, sem).wait()


    def ar_begin(self, r, i, top, low):
        cs = getattr(r, f"c{i}")
        cs[self.c, 0:1, :] = top
        cs[self.c, 1:2, :] = low
        mine = cs.at[self.c]
        self.put(mine, mine, r.ar_send.at[i, 0], r.ar_recv.at[i, 0], self.core_nbr, ("c", i))

    def ar_middle(self, r, i):
        cs, sl = getattr(r, f"c{i}"), getattr(r, f"s{i}")
        self.arrived(("c", i))
        sl[self.chip] = cs[0] + cs[1]
        mine = sl.at[self.chip]
        most = sl.at[pl.ds(0, self.chips - 1)]
        send, recv = r.ar_send.at[i, 1], r.ar_recv.at[i, 1]

        def one(device):
            pltpu.make_async_remote_copy(
                mine, mine, send, recv, device_id=device, device_id_type=MESH
            ).start()

        self.each_chip(one)
        self.sent.append((most, send))
        self.coming["s", i] = (most, recv)

    def ar_end(self, r, i):
        sl = getattr(r, f"s{i}")
        self.arrived(("s", i))
        if self.chips <= 16:
            total = sl[0]
            for k in range(1, self.chips):
                total = total + sl[k]
        else:
            total = lax.fori_loop(1, self.chips, lambda k, t: t + sl[k], sl[0])
        return total[0:1, :], total[1:2, :]

    def group(self, ref, flip_y=False, flip_x=False):
        y = 1 - self.y if flip_y else self.y
        x = 1 - self.x if flip_x else self.x
        return ref.at[y, x, self.c]

    def ag_pack(self, r):
        rest, tail = r.cshard[2][32:96], r.pshard[80:96, :]
        narrow = jnp.concatenate([rest[:, 32 * i : 32 * i + 32] for i in range(3)], axis=0)
        for j in range(2):
            v = jnp.concatenate([r.cshard[j], narrow[96 * j : 96 * j + 96]], axis=1)
            for h in range(2):
                g = (r.w0, r.w1, r.w2, r.w3)[2 * j + h]
                g[self.y, self.x, self.c, 0] = v[48 * h : 48 * h + 48]
        r.w4[self.y, self.x, self.c, 0, :, 0:96] = r.cshard[2][0:32]
        g5 = r.w5.at[self.y, self.x, self.c, 0]
        g5[:, 0:96] = r.pshard[0:80, :]
        g5[0:48, 96:128] = jnp.concatenate([tail[:, 32 * i : 32 * i + 32] for i in range(3)], axis=0)

    def ag_start(self, r, j):
        grp = self.group(getattr(r, f"w{j}"))
        slot, some = grp.at[0], grp.at[pl.ds(1, self.nz - 1)]
        for d in range(1, self.nz):
            pltpu.make_async_remote_copy(
                slot, grp.at[self.nz - d], r.ag_send.at[j, 0], r.ag_z.at[j],
                device_id=self.z_device(d), device_id_type=MESH,
            ).start()
        self.sent.append((some, r.ag_send.at[j, 0]))
        self.coming["z", j] = (some, r.ag_z.at[j])
        self.put(slot, slot, r.ag_send.at[j, 1], r.ag_own.at[j, 0], self.y_nbr, ("yo", j))
        self.put(slot, slot, r.ag_send.at[j, 1], r.ag_own.at[j, 1], self.x_nbr, ("xo", j))

    def to_core(self, r, j, i, grp):
        self.put(grp, grp, r.ag_send.at[j, 2], r.ag_core.at[j, i], self.core_nbr, ("core", j, i))

    def ag_plane(self, r, j):
        self.arrived(("z", j))
        grp = self.group(getattr(r, f"w{j}"))
        some = grp.at[pl.ds(1, self.nz - 1)]
        self.put(some, some, r.ag_send.at[j, 1], r.ag_oth.at[j, 0], self.y_nbr, ("yr", j))
        self.put(some, some, r.ag_send.at[j, 1], r.ag_oth.at[j, 1], self.x_nbr, ("xr", j))
        self.to_core(r, j, 0, grp)

    def ag_diagonal(self, r, j):
        g = getattr(r, f"w{j}")
        by_y, by_x = self.group(g, flip_y=True), self.group(g, flip_x=True)
        h = j % 2
        first, second = (by_y, by_x) if h == 0 else (by_x, by_y)
        self.arrived(("yx"[h] + "o", j), ("yx"[h] + "r", j))
        self.put(
            first, first, r.ag_send.at[j, 1], r.ag_d.at[j], (self.x_nbr, self.y_nbr)[h], ("d", j)
        )
        self.to_core(r, j, 1, first)
        self.arrived(("xy"[h] + "o", j), ("xy"[h] + "r", j))
        self.to_core(r, j, 2, second)

    def ag_last(self, r, j):
        self.arrived(("d", j))
        self.to_core(r, j, 3, self.group(getattr(r, f"w{j}"), True, True))

    def each_slot(self):
        for z in range(self.nz):
            at = lax.rem(z - self.z + self.nz, self.nz)
            for y in range(2):
                yield z, y, at

    def ag_unpack(self, r, k):
        H, cw, hw = self.H, self.cw, self.hw
        for j in ((0, 1), (2, 3), (4,), (5,))[k]:
            self.arrived(*[("core", j, i) for i in range(4)])
        for z, y, at in self.each_slot():
            low = (z * 2 + y) * cw
            slot = lambda j, s: r.__dict__[f"w{j}"].at[y, s // 2, s % 2, at]
            if k < 2:
                for h in range(2):
                    r.wf[low + 48 * h : low + 48 * h + 48, k * H : k * H + H] = jnp.concatenate(
                        [slot(2 * k + h, s)[:, 0:96] for s in range(4)], axis=1
                    )
            elif k == 2:
                r.wf[low : low + 32, 2 * H : 3 * H] = jnp.concatenate(
                    [slot(4, s)[:, 0:96] for s in range(4)], axis=1
                )
                for i, pieces in enumerate(
                    (((0, 0, 48), (1, 0, 16)), ((1, 16, 48), (2, 0, 32)), ((2, 32, 48), (3, 0, 48)))
                ):
                    row = low + 32
                    for j, a, b in pieces:
                        for s in range(4):
                            lane = 2 * H + s * hw + 32 * i
                            r.wf[row : row + b - a, lane : lane + 32] = slot(j, s)[a:b, 96:128]
                        row += b - a
            else:
                for s in range(4):
                    p = slot(5, s)
                    r.pf[s * hw : s * hw + 80, low : low + cw] = p[:, 0:96]
                    for i in range(3):
                        r.pf[s * hw + 80 : s * hw + 96, low + 32 * i : low + 32 * i + 32] = p[
                            16 * i : 16 * i + 16, 96:128
                        ]

    def rs_pack(self, r, cg, m):
        H, cw, hw = self.H, self.cw, self.hw
        mine = self.c == 0
        for zl in range(2):
            for y in range(2):
                low = (zl * 2 + y) * cw
                tile = lambda t, s: cg[low : low + cw, t * H + s * hw : t * H + s * hw + hw]
                for x in range(2):
                    both = []
                    for c in range(2):
                        s = x * 2 + c
                        t2 = tile(2, s)
                        rest = jnp.concatenate([t2[32:96, 32 * i : 32 * i + 32] for i in range(3)], axis=0)
                        both.append((
                            jnp.concatenate([tile(0, s), rest[0:96]], axis=1),
                            jnp.concatenate([tile(1, s), rest[96:192]], axis=1),
                            jnp.concatenate([t2[0:32], jnp.zeros((32, 32), F32)], axis=1),
                        ))
                    for a, b, at in ((both[0], both[1], 0),):
                        own = [jnp.where(mine, p, q) for p, q in zip(a, b)]
                        other = [jnp.where(mine, q, p).astype(BF) for p, q in zip(a, b)]
                    r.ra[m, 0, y, x, zl, 0:96, :] = own[0]
                    r.ra[m, 0, y, x, zl, 96:112, :] = own[1][0:16]
                    r.ra[m, 1, y, x, zl, 0:80, :] = own[1][16:96]
                    r.ra[m, 1, y, x, zl, 80:112, :] = own[2]
                    r.rs[m, 0, y, x, zl, 0:96, :] = other[0]
                    r.rs[m, 0, y, x, zl, 96:112, :] = other[1][0:16]
                    r.rs[m, 1, y, x, zl, 0:80, :] = other[1][16:96]
                    r.rs[m, 1, y, x, zl, 80:112, :] = other[2]

    def rs_core(self, r, m):
        for h in range(2):
            self.put(r.rs.at[m, h], r.rc.at[m, h], r.rs_send.at[m, h, 0], r.rs_core.at[m, h], self.core_nbr, ("rc", m, h))

    def rs_diagonal(self, r, m, h):
        self.arrived(("rc", m, h))
        for y in range(2):
            for x in range(2):
                for zl in range(2):
                    r.ra[m, h, y, x, zl] += r.rc[m, h, y, x, zl].astype(F32)
        y, x = 1 - self.y, 1 - self.x
        r.st[m, h, y, x] = r.ra[m, h, y, x].astype(BF)
        self.put(
            r.st.at[m, h, y, x], r.rd.at[m, h], r.rs_send.at[m, h, 1], r.rs_d.at[m, h],
            (self.x_nbr, self.y_nbr)[h], ("rd", m, h),
        )

    def rs_plane(self, r, m, h):
        self.arrived(("rd", m, h))
        via_y, via_x = (1 - self.y, self.x), (self.y, 1 - self.x)
        y, x = (via_y, via_x)[h]
        r.ra[m, h, y, x] += r.rd[m, h].astype(F32)
        for i, ((y, x), to) in enumerate(((via_y, self.y_nbr), (via_x, self.x_nbr))):
            r.st[m, h, y, x] = r.ra[m, h, y, x].astype(BF)
            self.put(r.st.at[m, h, y, x], r.rxy.at[m, h, i], r.rs_send.at[m, h, 2], r.rs_xy.at[m, h, i], to, ("rp", m, h, i))

    def rs_column(self, r, h):
        y, x = self.y, self.x
        for m in range(2):
            self.arrived(("rp", m, h, 0), ("rp", m, h, 1))
            r.ra[m, h, y, x] += r.rxy[m, h, 0].astype(F32) + r.rxy[m, h, 1].astype(F32)
            r.st[m, h, y, x] = r.ra[m, h, y, x].astype(BF)
        for d in range(1, self.nz):
            to = lax.rem(self.z + d, self.nz)
            pltpu.make_async_remote_copy(
                r.st.at[to // 2, h, y, x, lax.rem(to, 2)], r.rz.at[h, self.nz - d - 1],
                r.rz_send.at[h], r.rs_z.at[h], device_id=self.z_device(d), device_id_type=MESH,
            ).start()
        self.sent.append((r.rz.at[h], r.rz_send.at[h]))
        self.coming["rz", h] = (r.rz.at[h], r.rs_z.at[h])

    def rs_end(self, r):
        v = []
        for h in range(2):
            self.arrived(("rz", h))
            t = r.ra[self.z // 2, h, self.y, self.x, lax.rem(self.z, 2)]
            for i in range(3):
                t = t + r.rz[h, i].astype(F32)
            v.append(t)
        v = jnp.concatenate(v, axis=0)
        r.conv_grad[0] = v[0:96, 0:96]
        r.conv_grad[1] = v[96:192, 0:96]
        r.conv_grad[2, 0:32, :] = v[192:224, 0:96]
        for i in range(3):
            r.conv_grad[2, 32:96, 32 * i : 32 * i + 32] = v[64 * i : 64 * i + 64, 96:128]

    def pg_pack(self, r, pg):
        cw, hw = self.cw, self.hw
        mine = self.c == 0
        for z in range(self.nz):
            for y in range(2):
                lane = (z * 2 + y) * cw
                for x in range(2):
                    both = []
                    for c in range(2):
                        t = pg[(x * 2 + c) * hw : (x * 2 + c) * hw + hw, lane : lane + cw]
                        rest = jnp.concatenate([t[80:96, 32 * i : 32 * i + 32] for i in range(3)] + [jnp.zeros((32, 32), F32)], axis=0)
                        both.append(jnp.concatenate([t[0:80], rest], axis=1))
                    r.pa[y, x, z] = jnp.where(mine, both[0], both[1])
                    r.ps[y, x, z] = jnp.where(mine, both[1], both[0]).astype(BF)

    def pg_core(self, r):
        self.put(r.ps, r.pc, r.p_send.at[0], r.p_recv.at[0], self.core_nbr, "pc")

    def pg_diagonal(self, r):
        self.arrived("pc")
        for y in range(2):
            for x in range(2):
                r.pa[y, x] += r.pc[y, x].astype(F32)
        y, x = 1 - self.y, 1 - self.x
        r.pt[y, x] = r.pa[y, x].astype(BF)
        self.put(r.pt.at[y, x], r.pd, r.p_send.at[1], r.p_recv.at[1], self.x_nbr, "pd")

    def pg_plane(self, r):
        self.arrived("pd")
        via_y, via_x = (1 - self.y, self.x), (self.y, 1 - self.x)
        r.pa[via_y[0], via_y[1]] += r.pd[...].astype(F32)
        for i, ((y, x), to) in enumerate(((via_y, self.y_nbr), (via_x, self.x_nbr))):
            r.pt[y, x] = r.pa[y, x].astype(BF)
            self.put(r.pt.at[y, x], r.pxy.at[i], r.p_send.at[2], r.p_recv.at[2 + i], to, ("pp", i))

    def pg_column(self, r):
        y, x = self.y, self.x
        self.arrived(("pp", 0), ("pp", 1))
        r.pa[y, x] += r.pxy[0].astype(F32) + r.pxy[1].astype(F32)
        r.pt[y, x] = r.pa[y, x].astype(BF)
        for d in range(1, self.nz):
            to = lax.rem(self.z + d, self.nz)
            pltpu.make_async_remote_copy(
                r.pt.at[y, x, to], r.pz.at[self.nz - d - 1], r.p_send.at[3], r.p_recv.at[4],
                device_id=self.z_device(d), device_id_type=MESH,
            ).start()
        self.sent.append((r.pz, r.p_send.at[3]))
        self.coming["pz"] = (r.pz, r.p_recv.at[4])

    def pg_end(self, r):
        self.arrived("pz")
        v = r.pa[self.y, self.x, self.z]
        for i in range(3):
            v = v + r.pz[i].astype(F32)
        r.point_grad[0:80, :] = v[:, 0:96]
        for i in range(3):
            r.point_grad[80:96, 32 * i : 32 * i + 32] = v[16 * i : 16 * i + 16, 96:128]

    def halo_begin(self, r):
        R, H = self.rows, self.H
        r.hs[0] = r.big[PAD : 2 * PAD, 2 * H : 3 * H] * wide(r.mb[0:PAD], H)
        r.hs[1] = r.big[R : R + PAD, 0:H] * wide(r.ma[R - PAD : R], H)
        for j, to in enumerate((self.prev, self.next)):
            self.put(r.hs.at[j], r.halo.at[j], r.halo_send.at[0, j], r.halo_recv.at[0, j], to, ("h", j))

    def halo_end(self, r):
        R, H = self.rows, self.H
        self.arrived(("h", 0), ("h", 1))
        r.big[R + PAD : R + 2 * PAD, 2 * H : 3 * H] = r.halo[0]
        r.big[0:PAD, 0:H] = r.halo[1]

    def edges_begin(self, r):
        R, H = self.rows, self.H
        for j, (at, m, to) in enumerate(((0, r.mb, self.prev), (R - PAD, r.ma, self.next))):
            mask = m[at : at + PAD]
            r.es[j, :, 0:H] = r.p2g[at : at + PAD, :] * wide(mask, H)
            r.es[j, :, H : 2 * H] = r.conv[at : at + PAD, :] * wide(mask, H)
            r.es[j, :, 2 * H :] = mask
            self.put(r.es.at[j], r.edge.at[j], r.halo_send.at[1, j], r.halo_recv.at[1, j], to, ("e", j))

    def edges_end(self, r, a2, lin2, off2):
        R, H = self.rows, self.H
        self.arrived(("e", 0), ("e", 1))
        for j, at in ((0, R + PAD), (1, 0)):
            r.big[at : at + PAD, 0:H] = (
                r.edge[j, :, 0:H] * a2 + r.edge[j, :, H : 2 * H] * lin2 + wide(r.edge[j, :, 2 * H :], H) * off2
            )


class Refs:
    pass


def kernel(k, n_in, n_out, names, *refs):
    r = Refs()
    for name, ref in zip(names, refs[n_in + n_out :]):
        setattr(r, name, ref)
    k.sent, k.coming, k.local = [], {}, {}
    k.place()
    work(k, r, refs[:n_in], refs[n_in : n_in + n_out])
    k.drain()


def work(k, r, ins, outs):
    (x_hbm, og_hbm, species, first, sw, conv_w, point_w, g1, b1, g2, b2, run1, run2) = ins
    (out, ig, r.conv_grad, r.point_grad, gg1, gb1, gg2, gb2, new1, new2) = outs
    R, C, H, N = k.rows, k.C, k.H, k.total
    Q = R // 4
    r.bg = ig
    k.greet()
    if k.packed:
        k.fetch("cw", conv_w, r.cshard, r.insem.at[5])
        k.fetch("pw", point_w, r.pshard, r.insem.at[6])
    for q in range(4):
        rows = pl.ds(q * Q, Q)
        k.fetch(("x", q), x_hbm.at[rows], r.x.at[rows], r.insem.at[q])
    small = dict(first=first, g1=g1, b1=b1, g2=g2, b2=b2, sw=sw, run1=run1, run2=run2, species=species)
    for i, (name, ref) in enumerate(small.items()):
        k.fetch(name, ref, getattr(r, name), r.insem.at[7 + i])
    k.fetch("og", og_hbm, r.og, r.insem.at[4])
    if not k.packed:
        k.fetch("cw", conv_w, r.wf, r.insem.at[5])
        k.fetch("pw", point_w, r.pf, r.insem.at[6])
    else:
        k.have("cw", "pw")
        k.ag_pack(r)

    def sums(q):
        k.have(("x", q))
        v = r.x[q * Q : q * Q + Q, :].astype(F32)
        r.acc1[0] += colsum(v)
        r.acc1[1] += colsum(v * v)

    r.acc1[...] = jnp.zeros_like(r.acc1)
    for q in range(2):
        sums(q)
    k.greeted()
    if k.packed:
        for j in range(5):
            k.ag_start(r, j)
    for q in range(2, 4):
        sums(q)
    k.ar_begin(r, 0, squash(r.acc1[0]), squash(r.acc1[1]))

    k.have("first")
    fs = r.first[0]
    starts = [fs + SEQ_LEN * j for j in range(R // SEQ_LEN)]
    k.ar_middle(r, 0)
    if k.packed:
        k.ag_start(r, 5)

    def masks(at):
        row = row_tile(at, 128)
        before = jnp.ones((128, 128), F32)
        after = jnp.ones((128, 128), F32)
        for s in starts:
            before = jnp.where((row >= s) & (row < s + DIL), 0.0, before)
            after = jnp.where((row >= s - DIL) & (row < s), 0.0, after)
        r.mb[pl.ds(at, 128), :] = before
        r.ma[pl.ds(at, 128), :] = after

    loop(0, R, 128, masks)
    if k.packed:
        for j in range(5):
            k.ag_plane(r, j)
    k.have("g1", "b1")
    sum1, sq1 = k.ar_end(r, 0)
    mean1 = sum1 / N
    var1 = sq1 / N - mean1 * mean1
    inv1 = lax.rsqrt(var1 + EPSILON)
    gain1 = r.g1[...].reshape(1, C)
    scale1 = (HALF_SLOPE * gain1) * inv1
    shift1 = HALF_SLOPE * r.b1[...].reshape(1, C) - mean1 * scale1

    def act_tile(at):
        rows = pl.ds(at, 256)
        a, s = gelu_all(r.x[rows, :].astype(F32) * scale1 + shift1)
        r.act[rows, :] = a.astype(BF)
        r.slope[rows, :] = s.astype(BF)

    steps = (
        lambda: (k.ag_diagonal(r, 0), k.ag_diagonal(r, 1)),
        lambda: (k.ag_diagonal(r, 2), k.ag_plane(r, 5)),
        lambda: (k.ag_diagonal(r, 3), k.ag_diagonal(r, 4)),
        lambda: (k.ag_last(r, 0), k.ag_last(r, 1)),
    )
    for q in range(4):
        loop(q * Q, q * Q + Q, 256, act_tile)
        if k.packed:
            steps[q]()
    if k.packed:
        k.ag_last(r, 2)
        k.ag_unpack(r, 0)
        k.ag_last(r, 3)
        k.ag_last(r, 4)
        k.ag_unpack(r, 1)
    else:
        k.have("cw", "pw")

    def product(at, rows, lanes):
        r.big[PAD + at : PAD + at + rows, lanes] = jnp.dot(
            r.act[at : at + rows, :], r.wf[:, lanes], preferred_element_type=F32
        )

    product(0, R // 2, slice(0, 2 * H))
    if k.packed:
        k.ag_diagonal(r, 5)
    product(R // 2, R // 2, slice(0, 2 * H))
    if k.packed:
        k.ag_unpack(r, 2)
    product(0, R // 2, slice(2 * H, 3 * H))
    product(R // 2, R // 2, slice(2 * H, 3 * H))
    k.halo_begin(r)
    if k.packed:
        k.ag_last(r, 5)
    r.acc2[...] = jnp.zeros_like(r.acc2)
    T = 256

    def gather_taps(at):
        rows = pl.ds(at, T)
        lo = r.big[pl.ds(at, T + 2 * PAD), 0:H][PAD - DIL : PAD - DIL + T]
        mid = r.big[pl.ds(at + PAD, T), H : 2 * H]
        hi = r.big[pl.ds(at, T + 2 * PAD), 2 * H : 3 * H][PAD + DIL : PAD + DIL + T]
        v = lo * wide(r.mb[rows, :], H) + mid + hi * wide(r.ma[rows, :], H)
        r.conv[rows, :] = v
        r.acc2[0] += colsum(v)
        r.acc2[1] += colsum(v * v)

    loop(T, R - T, T, gather_taps)
    k.halo_end(r)
    gather_taps(0)
    gather_taps(R - T)
    k.ar_begin(r, 1, squash(r.acc2[0]), squash(r.acc2[1]))
    k.ar_middle(r, 1)

    k.have("og", "sw", "species", "g2", "b2", "run1", "run2")
    at_start = [r.species[0]] + [r.species[s] for s in starts]
    weights = [jnp.where(sp == 0, r.sw[0:1, :], r.sw[1:2, :]) for sp in at_start]

    def row_weight(at, tile):
        row = row_tile(at, tile)
        w = jnp.broadcast_to(weights[0], (tile, C))
        for s, v in zip(starts, weights[1:]):
            w = jnp.where(wide(row, C) >= s, v, w)
        return w

    def branch_grad(at):
        rows = pl.ds(at, 128)
        r.bg[rows, :] = (r.og[rows, :].astype(F32) * row_weight(at, 128)).astype(BF)

    loop(0, R, 128, branch_grad)
    if k.packed:
        k.ag_unpack(r, 3)

    def act_two_grad(at):
        rows = pl.ds(at, 1024)
        r.p2g[rows, :] = lax.dot_general(
            r.bg[rows, :], r.pf[...], (((1,), (1,)), ((), ())), preferred_element_type=F32
        )

    loop(0, R, 1024, act_two_grad)
    sum2, sq2 = k.ar_end(r, 1)
    mean2 = sum2 / N
    var2 = sq2 / N - mean2 * mean2
    inv2 = lax.rsqrt(var2 + EPSILON)
    minv2 = mean2 * inv2
    gain2 = r.g2[...].reshape(1, H)
    gain2h, bias2h = HALF_SLOPE * gain2, HALF_SLOPE * r.b2[...].reshape(1, H)
    r.acc2[...] = jnp.zeros_like(r.acc2)

    def second_norm(at):
        rows = pl.ds(at, 256)
        zh = r.conv[rows, :] * inv2 - minv2
        a, s = gelu_all(zh * gain2h + bias2h)
        r.act2[rows, :] = a.astype(BF)
        p = r.p2g[rows, :] * s
        r.p2g[rows, :] = p
        r.acc2[0] += colsum(p)
        r.acc2[1] += colsum(p * zh)

    loop(0, R, 256, second_norm)
    k.ar_begin(r, 2, squash(r.acc2[0]), squash(r.acc2[1]))
    k.edges_begin(r)
    k.ar_middle(r, 2)

    for q in range(2):
        rows = pl.ds(q * 1024, 1024)
        br = jnp.dot(r.act2[rows, :], r.pf[...], preferred_element_type=F32)
        out[rows, :] = (r.x[rows, :].astype(F32) + br).astype(BF)
    pg = lax.dot_general(
        r.act2[...], r.bg[...], (((0,), (0,)), ((), ())), preferred_element_type=F32
    )
    if k.packed:
        k.pg_pack(r, pg)
        k.pg_core(r)
    else:
        r.point_grad[...] = pg
    bsum, gsum = k.ar_end(r, 2)
    gb2[...] = bsum.reshape(H)
    gg2[...] = gsum.reshape(H)
    a2 = inv2 * gain2
    lin2 = -a2 * (gsum / N) * inv2
    off2 = -a2 * (bsum / N) + a2 * (gsum / N) * minv2

    def cot(at):
        rows = pl.ds(at, 256)
        r.big[pl.ds(at + PAD, 256), 0:H] = (
            r.p2g[rows, :] * a2 + r.conv[rows, :] * lin2 + off2
        )

    loop(0, R, 256, cot)
    if k.packed:
        k.pg_diagonal(r)
    k.edges_end(r, a2, lin2, off2)
    T2 = 128

    def shifted(at):
        rows = pl.ds(at, T2)
        v = r.big[pl.ds(at, T2 + 2 * PAD), 0:H]
        r.back[rows, 0:H] = (v[PAD + DIL : PAD + DIL + T2] * wide(r.ma[rows, :], H)).astype(BF)
        r.back[rows, H : 2 * H] = v[PAD : PAD + T2].astype(BF)
        r.back[rows, 2 * H : 3 * H] = (v[PAD - DIL : PAD - DIL + T2] * wide(r.mb[rows, :], H)).astype(BF)

    loop(0, R, T2, shifted)

    M = C // 2
    for i, m in enumerate(range(0, C, M)):
        cg = lax.dot_general(
            r.act[:, m : m + M], r.back[...], (((0,), (0,)), ((), ())), preferred_element_type=F32
        )
        if k.packed:
            k.rs_pack(r, cg, i)
            k.rs_core(r, i)
            if i == 0:
                k.pg_plane(r)
        else:
            for j in range(3):
                r.conv_grad[j, m : m + M, :] = cg[:, j * H : j * H + H]

    minv1 = mean1 * inv1
    r.acc1[...] = jnp.zeros_like(r.acc1)
    steps = (
        lambda: (k.rs_diagonal(r, 0, 0), k.rs_diagonal(r, 0, 1)),
        lambda: (k.rs_diagonal(r, 1, 0), k.rs_diagonal(r, 1, 1), k.pg_column(r)),
        lambda: (k.rs_plane(r, 0, 0), k.rs_plane(r, 0, 1)),
        lambda: None,
    )
    for q in range(4):
        rows = slice(q * Q, q * Q + Q)
        ag = lax.dot_general(
            r.back[rows, :], r.wf[...], (((1,), (1,)), ((), ())), preferred_element_type=F32
        )
        p = ag * r.slope[rows, :].astype(F32)
        r.big[rows, 0:C] = p
        r.acc1[0] += colsum(p)
        r.acc1[1] += colsum(p * (r.x[rows, :].astype(F32) * inv1 - minv1))
        if k.packed:
            steps[q]()
    k.ar_begin(r, 3, squash(r.acc1[0]), squash(r.acc1[1]))
    k.ar_middle(r, 3)
    if k.packed:
        k.rs_plane(r, 1, 0)
        k.rs_plane(r, 1, 1)
    unbias = N / (N - 1.0)
    new1[0:1, :] = MOMENTUM * r.run1[0:1, :] + (1.0 - MOMENTUM) * mean1
    new1[1:2, :] = MOMENTUM * r.run1[1:2, :] + (1.0 - MOMENTUM) * (var1 * unbias)
    new2[0:1, :] = MOMENTUM * r.run2[0:1, :] + (1.0 - MOMENTUM) * mean2
    new2[1:2, :] = MOMENTUM * r.run2[1:2, :] + (1.0 - MOMENTUM) * (var2 * unbias)
    if k.packed:
        k.pg_end(r)
    bsum1, gsum1 = k.ar_end(r, 3)
    gb1[...] = bsum1.reshape(C)
    gg1[...] = gsum1.reshape(C)
    a1 = inv1 * gain1
    lin1 = -a1 * (gsum1 / N) * inv1
    off1 = -a1 * (bsum1 / N) + a1 * (gsum1 / N) * minv1

    def last(at):
        rows = pl.ds(at, 128)
        v = r.og[rows, :].astype(F32) * row_weight(at, 128)
        v = v + r.big[rows, 0:C] * a1 + r.x[rows, :].astype(F32) * lin1 + off1
        ig[rows, :] = v.astype(BF)

    loop(0, R // 2, 128, last)
    if k.packed:
        k.rs_column(r, 0)
    if k.packed:
        k.rs_column(r, 1)
    loop(R // 2, R, 128, last)
    if k.packed:
        k.rs_end(r)


def hand_out(n, large, *refs):
    ins, outs, sems = refs[:n], refs[n : 2 * n], refs[2 * n]
    copies = [pltpu.make_async_copy(ins[i], outs[i], sems.at[i]) for i in range(n)]
    for cp in copies:
        cp.start()
    for cp in copies:
        cp.wait()


def body(
    mesh,
    activations,
    out_grad,
    species,
    first_start,
    species_weight,
    conv_weight,
    point_weight,
    gain_one,
    bias_one,
    gain_two,
    bias_two,
    running_one,
    running_two,
):
    rows, C = activations.shape
    ndp, nsub = mesh.shape["dp"], mesh.shape["sub"]
    cw, hw = conv_weight.shape[1:]
    taps, H = conv_weight.shape[0], hw * nsub
    packed = cw == 96 and hw == 96 and nsub == 4 and ndp % 2 == 0
    if not packed:
        conv_weight = lax.all_gather(conv_weight, "dp", axis=1, tiled=True)
        conv_weight = lax.all_gather(conv_weight, "sub", axis=2, tiled=True)
        conv_weight = jnp.transpose(conv_weight, (1, 0, 2)).reshape(C, taps * H)
        point_weight = lax.all_gather(point_weight, "dp", axis=1, tiled=True)
        point_weight = lax.all_gather(point_weight, "sub", axis=0, tiled=True)
    k = Kernel(mesh, rows, C, H, packed)
    scratch = k.scratch()
    here = pl.BlockSpec(memory_space=pl.ANY)
    vmem = pl.BlockSpec(memory_space=pltpu.VMEM)
    shapes = [
        ((rows, C), BF),
        ((rows, C), BF),
        ((taps, cw, hw) if packed else (taps, C, H), F32),
        ((hw, cw) if packed else (H, C), F32),
        ((C,), F32),
        ((C,), F32),
        ((H,), F32),
        ((H,), F32),
        ((2, C), F32),
        ((2, H), F32),
    ]
    held = [packed or i not in (2, 3) for i in range(len(shapes))]
    outs = pl.pallas_call(
        functools.partial(kernel, k, 13, len(shapes), list(scratch)),
        out_shape=[
            pltpu.VMEM(*s) if in_vmem else jax.ShapeDtypeStruct(*s) for s, in_vmem in zip(shapes, held)
        ],
        in_specs=[here] * 13,
        out_specs=[vmem] * len(shapes),
        scratch_shapes=list(scratch.values()),
        compiler_params=pltpu.CompilerParams(
            collective_id=0, has_side_effects=True, vmem_limit_bytes=(55 if packed else 54) * 2**20
        ),
    )(
        activations,
        out_grad,
        species,
        first_start,
        species_weight,
        conv_weight,
        point_weight,
        gain_one,
        bias_one,
        gain_two,
        bias_two,
        running_one,
        running_two,
    )
    keep = [i for i in range(len(shapes)) if held[i]]
    n = len(keep)
    given = pl.pallas_call(
        functools.partial(hand_out, n, 2),
        out_shape=[jax.ShapeDtypeStruct(*shapes[i]) for i in keep],
        in_specs=[vmem] * n,
        out_specs=[here] * n,
        scratch_shapes=[pltpu.SemaphoreType.DMA((n,))],
        compiler_params=pltpu.CompilerParams(vmem_limit_bytes=2**20),
    )(*[pltpu.with_memory_space_constraint(outs[i], pltpu.VMEM) for i in keep])
    outs = list(outs)
    for i, v in zip(keep, given):
        outs[i] = v
    if not packed:
        conv_grad, point_grad = outs[2], outs[3]
        conv_grad = lax.psum_scatter(conv_grad, "dp", scatter_dimension=1, tiled=True)
        point_grad = lax.psum_scatter(point_grad, "dp", scatter_dimension=1, tiled=True)
        outs[2] = lax.psum_scatter(conv_grad, "sub", scatter_dimension=2, tiled=True)
        outs[3] = lax.psum_scatter(point_grad, "sub", scatter_dimension=0, tiled=True)
    return tuple(outs)


def solution(mesh):
    in_specs = (
        P(("dp", "sub"), None),
        P(("dp", "sub"), None),
        P(("dp", "sub")),
        P(("dp", "sub")),
        P(),
        P(None, "dp", "sub"),
        P("sub", "dp"),
        P(),
        P(),
        P(),
        P(),
        P(),
        P(),
    )
    out_specs = (
        P(("dp", "sub"), None),
        P(("dp", "sub"), None),
        P(None, "dp", "sub"),
        P("sub", "dp"),
        P(),
        P(),
        P(),
        P(),
        P(),
        P(),
    )
    return jax.shard_map(
        functools.partial(body, mesh), mesh=mesh, in_specs=in_specs, out_specs=out_specs, check_vma=False
    )
```

```python
import functools

import jax
import jax.numpy as jnp
from jax import lax
from jax.experimental import pallas as pl
from jax.experimental.pallas import tpu as pltpu
from jax.sharding import PartitionSpec as P

DIL = 11
SEQ_LEN = 1024
EPSILON = 0.001
MOMENTUM = 0.9
PAD = 16
HALF_SLOPE = 0.851
BF = jnp.bfloat16
F32 = jnp.float32
MESH = pl.DeviceIdType.MESH
PARTS = ((0, 48), (48, 48), (96, 48), (144, 48), (192, 32), (224, 80))
CONV_ROWS, SLOT_ROWS = 224, 304
SIDE = 112


def gelu_all(u):
    t = jnp.tanh(u)
    s = 0.5 * t + 0.5
    return (u * s) * (1.0 / HALF_SLOPE), s + u * (0.5 - 0.5 * t * t)


def colsum(v):
    return jnp.sum(v.reshape(v.shape[0] // 8, 8, v.shape[1]), axis=0)


def squash(v):
    return jnp.sum(v, axis=0, keepdims=True)


def loop(first, last, tile, f):
    def one(i, carry):
        f(pl.multiple_of(first + i * tile, tile))
        return carry

    lax.fori_loop(0, (last - first) // tile, one, 0)


def row_tile(start, tile):
    return start + lax.broadcasted_iota(jnp.int32, (tile, 128), 0)


def wide(m, n):
    return jnp.concatenate([m] * (n // 128), axis=1)


def lanes_of(rows):
    return lax.broadcasted_iota(jnp.int32, (rows, 128), 1)


def join(pieces):
    lane = lanes_of(pieces[0].shape[0])
    return [jnp.where(lane < 96 - 32 * i, pieces[i], pieces[i + 1]) for i in range(3)]


def split(tiles):
    lane = lanes_of(tiles[0].shape[0])
    return [
        tiles[0],
        jnp.where(lane >= 96, tiles[0], tiles[1]),
        jnp.where(lane >= 64, tiles[1], tiles[2]),
        tiles[2],
    ]


def free(i, lane):
    at = (96 * i + 96) % 128
    return (lane >= at) & (lane < at + 32)


def narrow(v, i):
    return pltpu.roll(v, 96 - 32 * i, 1)


def widen(blocks, i):
    lane = lanes_of(blocks[0].shape[0])
    moved = [pltpu.roll(b, 32 + 32 * j, 1) for j, b in enumerate(blocks)]
    inside = lambda j: (lane >= (96 * i + 32 * j) % 128) & (lane < (96 * i + 32 * j) % 128 + 32)
    return jnp.where(inside(0), moved[0], jnp.where(inside(1), moved[1], moved[2]))


class Kernel:
    def __init__(self, mesh, rows, channels, hidden, packed):
        self.ndp, self.nsub = mesh.shape["dp"], mesh.shape["sub"]
        self.rows, self.C, self.H = rows, channels, hidden
        self.packed = packed
        self.total = rows * self.ndp * self.nsub
        self.chips = self.ndp * self.nsub // 2
        self.nz = self.ndp // 2
        self.cw, self.hw = channels // self.ndp, hidden // self.nsub
        self.half = self.cw // 2
        self.sent, self.coming, self.local = [], {}, {}

    def scratch(self):
        R, C, H = self.rows, self.C, self.H
        V, D = pltpu.VMEM, pltpu.SemaphoreType.DMA
        s = dict(
            x=V((R, C), BF),
            og=V((R, C), BF),
            act=V((R, C), BF),
            slope=V((R, C), BF),
            big=V((R + 2 * PAD, 3 * H), F32),
            conv=V((R, H), F32),
            p2g=V((R, H), F32),
            act2=V((R, H), BF),
            back=V((R, 3 * H), BF),
            mb=V((R, 128), F32),
            ma=V((R, 128), F32),
            hs=V((2, PAD, H), F32),
            halo=V((2, PAD, H), F32),
            es=V((2, PAD, 2 * H + 128), F32),
            edge=V((2, PAD, 2 * H + 128), F32),
            acc1=V((2, 8, C), F32),
            acc2=V((2, 8, H), F32),
            c0=V((2, 2, C), F32),
            c1=V((2, 2, H), F32),
            c2=V((2, 2, H), F32),
            c3=V((2, 2, C), F32),
            s0=V((self.chips, 2, C), F32),
            s1=V((self.chips, 2, H), F32),
            s2=V((self.chips, 2, H), F32),
            s3=V((self.chips, 2, C), F32),
            wf=V((C, 3 * H), BF),
            pf=V((H, C), BF),
            sw=V((2, C), F32),
            g1=V((C,), F32),
            b1=V((C,), F32),
            g2=V((H,), F32),
            b2=V((H,), F32),
            run1=V((2, C), F32),
            run2=V((2, H), F32),
            species=pltpu.SMEM((R,), jnp.int32),
            first=pltpu.SMEM((1,), jnp.int32),
            ar_send=D((4, 2)),
            ar_recv=D((4, 2)),
            insem=D((24,)),
            halo_send=D((2, 2)),
            halo_recv=D((2, 2)),
        )
        if self.packed:
            nz = self.nz
            s.update(
                cshard=V((3, self.cw, self.hw), BF),
                pshard=V((self.hw, self.cw), BF),
                ag_send=D((len(PARTS), 3)),
                ag_z=D((len(PARTS),)),
                ag_own=D((len(PARTS), 2)),
                ag_oth=D((len(PARTS), 2)),
                ag_d=D((len(PARTS),)),
                ag_core=D((len(PARTS), 4)),
                ra=V((2, 2, 2, 2, 2, SIDE, 128), F32),
                rs=V((2, 2, 2, 2, 2, SIDE, 128), BF),
                rc=V((2, 2, 2, 2, 2, SIDE, 128), BF),
                st=V((2, 2, 2, 2, 2, SIDE, 128), BF),
                rd=V((2, 2, 2, SIDE, 128), BF),
                rxy=V((2, 2, 2, 2, SIDE, 128), BF),
                rz=V((2, 3, SIDE, 128), BF),
                rs_send=D((2, 2, 3)),
                rs_core=D((2, 2)),
                rs_d=D((2, 2)),
                rs_xy=D((2, 2, 2)),
                rz_send=D((2,)),
                rs_z=D((2,)),
                pa=V((2, 2, nz, 80, 128), F32),
                ps=V((2, 2, nz, 80, 128), BF),
                pc=V((2, 2, nz, 80, 128), BF),
                pt=V((2, 2, nz, 80, 128), BF),
                pd=V((nz, 80, 128), BF),
                pxy=V((2, nz, 80, 128), BF),
                pz=V((3, 80, 128), BF),
                p_send=D((4,)),
                p_recv=D((5,)),
            )
            s.update({f"w{j}": V((2, 2, 2, nz, n, 128), BF) for j, (_, n) in enumerate(PARTS)})
        return s

    def place(self):
        self.dp, self.sub = lax.axis_index("dp"), lax.axis_index("sub")
        self.z, self.y = self.dp // 2, lax.rem(self.dp, 2)
        self.x, self.c = self.sub // 2, lax.rem(self.sub, 2)
        n = self.ndp * self.nsub
        me = self.dp * self.nsub + self.sub
        nxt, prv = lax.rem(me + 1, n), lax.rem(me + n - 1, n)
        far = lax.rem(me + jnp.where(self.c == 1, 1, n - 1), n)
        self.core_nbr = (self.dp, self.x * 2 + 1 - self.c)
        self.x_nbr = (self.dp, (1 - self.x) * 2 + self.c)
        self.y_nbr = (self.z * 2 + 1 - self.y, self.sub)
        self.next = (nxt // self.nsub, lax.rem(nxt, self.nsub))
        self.prev = (prv // self.nsub, lax.rem(prv, self.nsub))
        self.far = (far // self.nsub, lax.rem(far, self.nsub))
        self.chip = self.dp * (self.nsub // 2) + self.x

    def z_device(self, d):
        return (lax.rem(self.z + d, self.nz) * 2 + self.y, self.sub)

    def each_chip(self, f):
        if self.chips == 16 and self.nsub == 4:
            z, y, x = self.z, self.y, self.x
            zs = (z, z + 1 - 2 * lax.rem(z, 2), lax.rem(z + 2, 4), 3 - z)
            for d in range(15, 0, -1):
                yy = 1 - y if (d // 2) % 2 else y
                xx = 1 - x if d % 2 else x
                f((zs[d // 4] * 2 + yy, xx * 2 + self.c))
        else:
            side = self.nsub // 2

            def one(d, carry):
                chip = lax.rem(self.chip + d, self.chips)
                f((chip // side, lax.rem(chip, side) * 2 + self.c))
                return carry

            lax.fori_loop(1, self.chips, one, 0)

    def greet(self):
        b = pltpu.get_barrier_semaphore()

        def hello(device):
            pl.semaphore_signal(b, inc=1, device_id=device, device_id_type=MESH)

        self.each_chip(hello)
        hello(self.far)
        hello(self.core_nbr)

    def greeted(self):
        pl.semaphore_wait(pltpu.get_barrier_semaphore(), self.chips + 1)

    def put(self, src, dst, send, recv, device, key=None, ref=None):
        pltpu.make_async_remote_copy(
            src, dst, send, recv, device_id=device, device_id_type=MESH
        ).start()
        self.sent.append((src, send))
        if key is not None:
            self.coming[key] = (dst if ref is None else ref, recv)

    def arrived(self, *keys):
        for key in keys:
            ref, sem = self.coming.pop(key)
            pltpu.make_async_copy(ref, ref, sem).wait()

    def fetch(self, key, src, dst, sem):
        self.local[key] = cp = pltpu.make_async_copy(src, dst, sem)
        cp.start()

    def have(self, *keys):
        for key in keys:
            self.local.pop(key).wait()

    def drain(self):
        self.have(*list(self.local))
        self.arrived(*list(self.coming))
        for ref, sem in self.sent:
            pltpu.make_async_copy(ref, ref, sem).wait()


    def ar_begin(self, r, i, top, low):
        cs = getattr(r, f"c{i}")
        cs[self.c, 0:1, :] = top
        cs[self.c, 1:2, :] = low
        mine = cs.at[self.c]
        self.put(mine, mine, r.ar_send.at[i, 0], r.ar_recv.at[i, 0], self.core_nbr, ("c", i))

    def ar_middle(self, r, i):
        cs, sl = getattr(r, f"c{i}"), getattr(r, f"s{i}")
        self.arrived(("c", i))
        sl[self.chip] = cs[0] + cs[1]
        mine = sl.at[self.chip]
        most = sl.at[pl.ds(0, self.chips - 1)]
        send, recv = r.ar_send.at[i, 1], r.ar_recv.at[i, 1]

        def one(device):
            pltpu.make_async_remote_copy(
                mine, mine, send, recv, device_id=device, device_id_type=MESH
            ).start()

        self.each_chip(one)
        self.sent.append((most, send))
        self.coming["s", i] = (most, recv)

    def ar_end(self, r, i):
        sl = getattr(r, f"s{i}")
        self.arrived(("s", i))
        if self.chips <= 16:
            total = sl[0]
            for k in range(1, self.chips):
                total = total + sl[k]
        else:
            total = lax.fori_loop(1, self.chips, lambda k, t: t + sl[k], sl[0])
        return total[0:1, :], total[1:2, :]

    def group(self, ref, flip_y=False, flip_x=False):
        y = 1 - self.y if flip_y else self.y
        x = 1 - self.x if flip_x else self.x
        return ref.at[y, x, self.c]

    def ag_pack(self, r):
        lane = lanes_of(96)
        full = lambda v: jnp.concatenate([v.astype(F32), jnp.zeros((96, 32), F32)], axis=1)
        place = lambda v, i: pltpu.roll(v, lax.rem(96 * i, 128), 1).astype(BF)
        here = (self.y, self.x, self.c, 0)
        t2, p = full(r.cshard[2]), full(r.pshard[...])
        rest = jnp.concatenate([narrow(t2, i)[32:96] for i in range(3)], axis=0)
        for j in range(2):
            v = place(jnp.where(lane < 96, full(r.cshard[j]), rest[96 * j : 96 * j + 96]), self.sub)
            for h in range(2):
                (r.w0, r.w1, r.w2, r.w3)[2 * j + h][here] = v[48 * h : 48 * h + 48]
        r.w4[here] = place(t2[0:32], self.sub)
        rest = jnp.concatenate([narrow(p[80:96], i) for i in range(3)] + [jnp.zeros((32, 128), F32)], axis=0)
        r.w5[here] = place(jnp.where(lane[0:80] < 96, p[0:80], rest), self.dp)

    def ag_start(self, r, j):
        grp = self.group(getattr(r, f"w{j}"))
        slot, some = grp.at[0], grp.at[pl.ds(1, self.nz - 1)]
        for d in range(1, self.nz):
            pltpu.make_async_remote_copy(
                slot, grp.at[self.nz - d], r.ag_send.at[j, 0], r.ag_z.at[j],
                device_id=self.z_device(d), device_id_type=MESH,
            ).start()
        self.sent.append((some, r.ag_send.at[j, 0]))
        self.coming["z", j] = (some, r.ag_z.at[j])
        self.put(slot, slot, r.ag_send.at[j, 1], r.ag_own.at[j, 0], self.y_nbr, ("yo", j))
        self.put(slot, slot, r.ag_send.at[j, 1], r.ag_own.at[j, 1], self.x_nbr, ("xo", j))

    def to_core(self, r, j, i, grp):
        self.put(grp, grp, r.ag_send.at[j, 2], r.ag_core.at[j, i], self.core_nbr, ("core", j, i))

    def ag_plane(self, r, j):
        self.arrived(("z", j))
        grp = self.group(getattr(r, f"w{j}"))
        some = grp.at[pl.ds(1, self.nz - 1)]
        self.put(some, some, r.ag_send.at[j, 1], r.ag_oth.at[j, 0], self.y_nbr, ("yr", j))
        self.put(some, some, r.ag_send.at[j, 1], r.ag_oth.at[j, 1], self.x_nbr, ("xr", j))
        self.to_core(r, j, 0, grp)

    def ag_diagonal(self, r, j):
        g = getattr(r, f"w{j}")
        by_y, by_x = self.group(g, flip_y=True), self.group(g, flip_x=True)
        h = j % 2
        first, second = (by_y, by_x) if h == 0 else (by_x, by_y)
        self.arrived(("yx"[h] + "o", j), ("yx"[h] + "r", j))
        self.put(
            first, first, r.ag_send.at[j, 1], r.ag_d.at[j], (self.x_nbr, self.y_nbr)[h], ("d", j)
        )
        self.to_core(r, j, 1, first)
        self.arrived(("xy"[h] + "o", j), ("xy"[h] + "r", j))
        self.to_core(r, j, 2, second)

    def ag_last(self, r, j):
        self.arrived(("d", j))
        self.to_core(r, j, 3, self.group(getattr(r, f"w{j}"), True, True))

    def each_slot(self):
        for z in range(self.nz):
            at = lax.rem(z - self.z + self.nz, self.nz)
            for y in range(2):
                yield z, y, at

    def ag_unpack(self, r, k):
        H, cw, hw = self.H, self.cw, self.hw
        for j in ((0, 1), (2, 3), (4,), (5,))[k]:
            self.arrived(*[("core", j, i) for i in range(4)])

        def slot(j, y, s, at):
            return getattr(r, f"w{j}").at[y, s // 2, s % 2, at]

        def keep(ref, row, lane, tiles):
            for i, t in enumerate(tiles):
                ref[row : row + t.shape[0], lane + 128 * i : lane + 128 * i + 128] = t.astype(BF)

        if k < 3:
            for z, y, at in self.each_slot():
                low = (z * 2 + y) * cw
                if k < 2:
                    for h in range(2):
                        tiles = join([slot(2 * k + h, y, s, at)[...].astype(F32) for s in range(4)])
                        keep(r.wf, low + 48 * h, k * H, tiles)
                else:
                    keep(r.wf, low, 2 * H, join([slot(4, y, s, at)[...].astype(F32) for s in range(4)]))
                    pieces = []
                    for s in range(4):
                        parts = [slot(j, y, s, at) for j in range(4)]
                        cut = lambda j, a, b: parts[j][a:b, :].astype(F32)
                        pieces.append(widen((
                            jnp.concatenate([cut(0, 0, 48), cut(1, 0, 16)], axis=0),
                            jnp.concatenate([cut(1, 16, 48), cut(2, 0, 32)], axis=0),
                            jnp.concatenate([cut(2, 32, 48), cut(3, 0, 48)], axis=0),
                        ), s))
                    keep(r.wf, low + 32, 2 * H, join(pieces))
        else:
            ats = {z: at for z, _, at in self.each_slot()}
            for s in range(4):
                for q in range(2):
                    got = [slot(5, dp % 2, s, ats[dp // 2])[...].astype(F32) for dp in range(4 * q, 4 * q + 4)]
                    keep(r.pf, s * hw, 4 * q * cw, join([v[0:80] for v in got]))
                    rest = [widen([v[16 * i : 16 * i + 16] for i in range(3)], dp) for dp, v in enumerate(got)]
                    keep(r.pf, s * hw + 80, 4 * q * cw, join(rest))

    def rs_pack(self, r, cg, m):
        H, cw = self.H, self.cw
        mine = self.c == 0
        lane = lanes_of(96)
        for zl in range(2):
            for y in range(2):
                low = (zl * 2 + y) * cw
                taps = [
                    split([cg[low : low + cw, t * H + 128 * i : t * H + 128 * i + 128] for i in range(3)])
                    for t in range(3)
                ]
                for x in range(2):
                    both = []
                    for s in (2 * x, 2 * x + 1):
                        t2 = taps[2][s]
                        rest = jnp.concatenate([narrow(t2[32:96], i) for i in range(3)], axis=0)
                        gap = free(s, lane)
                        both.append((
                            jnp.where(gap, rest[0:96], taps[0][s]),
                            jnp.where(gap, rest[96:192], taps[1][s]),
                            t2[0:32],
                        ))
                    own = [jnp.where(mine, p, q) for p, q in zip(*both)]
                    other = [jnp.where(mine, q, p).astype(BF) for p, q in zip(*both)]
                    for ref, v in ((r.ra, own), (r.rs, other)):
                        ref[m, 0, y, x, zl, 0:96, :] = v[0]
                        ref[m, 0, y, x, zl, 96:112, :] = v[1][0:16]
                        ref[m, 1, y, x, zl, 0:80, :] = v[1][16:96]
                        ref[m, 1, y, x, zl, 80:112, :] = v[2]

    def rs_core(self, r, m):
        for h in range(2):
            self.put(r.rs.at[m, h], r.rc.at[m, h], r.rs_send.at[m, h, 0], r.rs_core.at[m, h], self.core_nbr, ("rc", m, h))

    def rs_diagonal(self, r, m, h):
        self.arrived(("rc", m, h))
        for y in range(2):
            for x in range(2):
                for zl in range(2):
                    r.ra[m, h, y, x, zl] += r.rc[m, h, y, x, zl].astype(F32)
        y, x = 1 - self.y, 1 - self.x
        r.st[m, h, y, x] = r.ra[m, h, y, x].astype(BF)
        self.put(
            r.st.at[m, h, y, x], r.rd.at[m, h], r.rs_send.at[m, h, 1], r.rs_d.at[m, h],
            (self.x_nbr, self.y_nbr)[h], ("rd", m, h),
        )

    def rs_plane(self, r, m, h):
        self.arrived(("rd", m, h))
        via_y, via_x = (1 - self.y, self.x), (self.y, 1 - self.x)
        y, x = (via_y, via_x)[h]
        r.ra[m, h, y, x] += r.rd[m, h].astype(F32)
        for i, ((y, x), to) in enumerate(((via_y, self.y_nbr), (via_x, self.x_nbr))):
            r.st[m, h, y, x] = r.ra[m, h, y, x].astype(BF)
            self.put(r.st.at[m, h, y, x], r.rxy.at[m, h, i], r.rs_send.at[m, h, 2], r.rs_xy.at[m, h, i], to, ("rp", m, h, i))

    def rs_column(self, r, m, h):
        y, x = self.y, self.x
        self.arrived(("rp", m, h, 0), ("rp", m, h, 1))
        r.ra[m, h, y, x] += r.rxy[m, h, 0].astype(F32) + r.rxy[m, h, 1].astype(F32)
        r.st[m, h, y, x] = r.ra[m, h, y, x].astype(BF)
        for zl in range(2):
            to = 2 * m + zl
            d = lax.rem(self.z - to + self.nz, self.nz)

            @pl.when(d != 0)
            def _():
                pltpu.make_async_remote_copy(
                    r.st.at[m, h, y, x, zl], r.rz.at[h, d - 1], r.rz_send.at[h], r.rs_z.at[h],
                    device_id=(to * 2 + self.y, self.sub), device_id_type=MESH,
                ).start()

        if m == 1:
            self.sent.append((r.rz.at[h], r.rz_send.at[h]))
            self.coming["rz", h] = (r.rz.at[h], r.rs_z.at[h])

    def rs_end(self, r):
        v = []
        for h in range(2):
            self.arrived(("rz", h))
            t = r.ra[self.z // 2, h, self.y, self.x, lax.rem(self.z, 2)]
            for i in range(3):
                t = t + r.rz[h, i].astype(F32)
            v.append(t)
        v = pltpu.roll(jnp.concatenate(v, axis=0), lax.rem(128 - lax.rem(96 * self.sub, 128), 128), 1)
        r.conv_grad[0] = v[0:96, 0:96]
        r.conv_grad[1] = v[96:192, 0:96]
        r.conv_grad[2, 0:32, :] = v[192:224, 0:96]
        r.conv_grad[2, 32:96, :] = widen([v[64 * i : 64 * i + 64] for i in range(3)], 0)[:, 0:96]

    def pg_pack(self, r, pg):
        cw, hw = self.cw, self.hw
        mine = self.c == 0
        lane = lanes_of(80)
        pieces = []
        for s in range(4):
            rows = slice(s * hw, s * hw + hw)
            pieces.append([
                p
                for q in range(2)
                for p in split([pg[rows, 4 * q * cw + 128 * i : 4 * q * cw + 128 * i + 128] for i in range(3)])
            ])
        for dp in range(self.ndp):
            for x in range(2):
                both = []
                for s in (2 * x, 2 * x + 1):
                    p = pieces[s][dp]
                    rest = jnp.concatenate([narrow(p[80:96], i) for i in range(3)] + [p[0:32]], axis=0)
                    both.append(jnp.where(free(dp, lane), rest, p[0:80]))
                r.pa[dp % 2, x, dp // 2] = jnp.where(mine, both[0], both[1])
                r.ps[dp % 2, x, dp // 2] = jnp.where(mine, both[1], both[0]).astype(BF)

    def pg_core(self, r):
        self.put(r.ps, r.pc, r.p_send.at[0], r.p_recv.at[0], self.core_nbr, "pc")

    def pg_diagonal(self, r):
        self.arrived("pc")
        for y in range(2):
            for x in range(2):
                r.pa[y, x] += r.pc[y, x].astype(F32)
        y, x = 1 - self.y, 1 - self.x
        r.pt[y, x] = r.pa[y, x].astype(BF)
        self.put(r.pt.at[y, x], r.pd, r.p_send.at[1], r.p_recv.at[1], self.x_nbr, "pd")

    def pg_plane(self, r):
        self.arrived("pd")
        via_y, via_x = (1 - self.y, self.x), (self.y, 1 - self.x)
        r.pa[via_y[0], via_y[1]] += r.pd[...].astype(F32)
        for i, ((y, x), to) in enumerate(((via_y, self.y_nbr), (via_x, self.x_nbr))):
            r.pt[y, x] = r.pa[y, x].astype(BF)
            self.put(r.pt.at[y, x], r.pxy.at[i], r.p_send.at[2], r.p_recv.at[2 + i], to, ("pp", i))

    def pg_column(self, r):
        y, x = self.y, self.x
        self.arrived(("pp", 0), ("pp", 1))
        r.pa[y, x] += r.pxy[0].astype(F32) + r.pxy[1].astype(F32)
        r.pt[y, x] = r.pa[y, x].astype(BF)
        for d in range(1, self.nz):
            to = lax.rem(self.z + d, self.nz)
            pltpu.make_async_remote_copy(
                r.pt.at[y, x, to], r.pz.at[self.nz - d - 1], r.p_send.at[3], r.p_recv.at[4],
                device_id=self.z_device(d), device_id_type=MESH,
            ).start()
        self.sent.append((r.pz, r.p_send.at[3]))
        self.coming["pz"] = (r.pz, r.p_recv.at[4])

    def pg_end(self, r):
        self.arrived("pz")
        v = r.pa[self.y, self.x, self.z]
        for i in range(3):
            v = v + r.pz[i].astype(F32)
        v = pltpu.roll(v, lax.rem(128 - lax.rem(96 * self.dp, 128), 128), 1)
        r.point_grad[0:80, :] = v[:, 0:96]
        r.point_grad[80:96, :] = widen([v[16 * i : 16 * i + 16] for i in range(3)], 0)[:, 0:96]

    def halo_up(self, r):
        R, H = self.rows, self.H
        r.hs[1] = r.big[R : R + PAD, 0:H] * wide(r.ma[R - PAD : R], H)
        self.put(r.hs.at[1], r.halo.at[1], r.halo_send.at[0, 1], r.halo_recv.at[0, 1], self.next, ("h", 1))

    def halo_down(self, r):
        H = self.H
        r.hs[0] = r.big[PAD : 2 * PAD, 2 * H : 3 * H] * wide(r.mb[0:PAD], H)
        self.put(r.hs.at[0], r.halo.at[0], r.halo_send.at[0, 0], r.halo_recv.at[0, 0], self.prev, ("h", 0))

    def halo_end(self, r):
        R, H = self.rows, self.H
        self.arrived(("h", 0), ("h", 1))
        r.big[R + PAD : R + 2 * PAD, 2 * H : 3 * H] = r.halo[0]
        r.big[0:PAD, 0:H] = r.halo[1]

    def edges_begin(self, r):
        R, H = self.rows, self.H
        for j, (at, m, to) in enumerate(((0, r.mb, self.prev), (R - PAD, r.ma, self.next))):
            mask = m[at : at + PAD]
            r.es[j, :, 0:H] = r.p2g[at : at + PAD, :] * wide(mask, H)
            r.es[j, :, H : 2 * H] = r.conv[at : at + PAD, :] * wide(mask, H)
            r.es[j, :, 2 * H :] = mask
            self.put(r.es.at[j], r.edge.at[j], r.halo_send.at[1, j], r.halo_recv.at[1, j], to, ("e", j))

    def edges_end(self, r, a2, lin2, off2):
        R, H = self.rows, self.H
        self.arrived(("e", 0), ("e", 1))
        for j, at in ((0, R + PAD), (1, 0)):
            r.big[at : at + PAD, 0:H] = (
                r.edge[j, :, 0:H] * a2 + r.edge[j, :, H : 2 * H] * lin2 + wide(r.edge[j, :, 2 * H :], H) * off2
            )


class Refs:
    pass


def kernel(k, n_in, n_out, names, *refs):
    r = Refs()
    for name, ref in zip(names, refs[n_in + n_out :]):
        setattr(r, name, ref)
    k.sent, k.coming, k.local = [], {}, {}
    k.place()
    work(k, r, refs[:n_in], refs[n_in : n_in + n_out])
    k.drain()


def work(k, r, ins, outs):
    (x_hbm, og_hbm, species, first, sw, conv_w, point_w, g1, b1, g2, b2, run1, run2) = ins
    (out, ig, r.conv_grad, r.point_grad, gg1, gb1, gg2, gb2, new1, new2) = outs
    R, C, H, N = k.rows, k.C, k.H, k.total
    Q = R // 4
    r.bg = ig
    k.greet()
    if k.packed:
        k.fetch("cw", conv_w, r.cshard, r.insem.at[5])
        k.fetch("pw", point_w, r.pshard, r.insem.at[6])
    for q in range(4):
        rows = pl.ds(q * Q, Q)
        k.fetch(("x", q), x_hbm.at[rows], r.x.at[rows], r.insem.at[q])
    small = dict(first=first, g1=g1, b1=b1, g2=g2, b2=b2, sw=sw, run1=run1, run2=run2, species=species)
    for i, (name, ref) in enumerate(small.items()):
        k.fetch(name, ref, getattr(r, name), r.insem.at[7 + i])
    k.fetch("og", og_hbm, r.og, r.insem.at[4])
    if not k.packed:
        k.fetch("cw", conv_w, r.wf, r.insem.at[5])
        k.fetch("pw", point_w, r.pf, r.insem.at[6])
    else:
        k.have("cw", "pw")
        k.ag_pack(r)

    def sums(q):
        k.have(("x", q))
        v = r.x[q * Q : q * Q + Q, :].astype(F32)
        r.acc1[0] += colsum(v)
        r.acc1[1] += colsum(v * v)

    r.acc1[...] = jnp.zeros_like(r.acc1)
    for q in range(2):
        sums(q)
    k.greeted()
    if k.packed:
        for j in range(5):
            k.ag_start(r, j)
    for q in range(2, 4):
        sums(q)
    k.ar_begin(r, 0, squash(r.acc1[0]), squash(r.acc1[1]))

    k.have("first")
    fs = r.first[0]
    starts = [fs + SEQ_LEN * j for j in range(R // SEQ_LEN)]
    k.ar_middle(r, 0)
    def masks(at):
        row = row_tile(at, 128)
        before = jnp.ones((128, 128), F32)
        after = jnp.ones((128, 128), F32)
        for s in starts:
            before = jnp.where((row >= s) & (row < s + DIL), 0.0, before)
            after = jnp.where((row >= s - DIL) & (row < s), 0.0, after)
        r.mb[pl.ds(at, 128), :] = before
        r.ma[pl.ds(at, 128), :] = after

    loop(0, R, 128, masks)
    if k.packed:
        for j in range(5):
            k.ag_plane(r, j)
        k.ag_start(r, 5)
    k.have("g1", "b1")
    sum1, sq1 = k.ar_end(r, 0)
    mean1 = sum1 / N
    var1 = sq1 / N - mean1 * mean1
    inv1 = lax.rsqrt(var1 + EPSILON)
    gain1 = r.g1[...].reshape(1, C)
    scale1 = (HALF_SLOPE * gain1) * inv1
    shift1 = HALF_SLOPE * r.b1[...].reshape(1, C) - mean1 * scale1

    def act_tile(at):
        rows = pl.ds(at, 256)
        u = r.x[rows, :].astype(F32) * scale1 + shift1
        a, s = gelu_all(u)
        r.act[rows, :] = a.astype(BF)
        r.slope[rows, :] = s.astype(BF)

    steps = (
        lambda: (k.ag_diagonal(r, 0), k.ag_diagonal(r, 1)),
        lambda: (k.ag_diagonal(r, 2), k.ag_diagonal(r, 3)),
        lambda: (k.ag_diagonal(r, 4), k.ag_plane(r, 5)),
        lambda: (k.ag_last(r, 0), k.ag_last(r, 1)),
    )
    for q in range(4):
        loop(q * Q, q * Q + Q, 256, act_tile)
        if k.packed:
            steps[q]()
    if k.packed:
        k.ag_last(r, 2)
        k.ag_last(r, 3)
        k.ag_unpack(r, 0)
        k.ag_last(r, 4)
        k.ag_unpack(r, 1)
    else:
        k.have("cw", "pw")

    def product(at, rows, lanes):
        r.big[PAD + at : PAD + at + rows, lanes] = jnp.dot(
            r.act[at : at + rows, :], r.wf[:, lanes], preferred_element_type=F32
        )

    product(0, R // 2, slice(0, 2 * H))
    product(R // 2, R // 2, slice(0, 2 * H))
    if k.packed:
        k.ag_unpack(r, 2)
    k.halo_up(r)
    product(0, R // 2, slice(2 * H, 3 * H))
    k.halo_down(r)
    product(R // 2, R // 2, slice(2 * H, 3 * H))
    if k.packed:
        k.ag_diagonal(r, 5)
    r.acc2[...] = jnp.zeros_like(r.acc2)
    T = 256

    def gather_taps(at):
        rows = pl.ds(at, T)
        lo = r.big[pl.ds(at, T + 2 * PAD), 0:H][PAD - DIL : PAD - DIL + T]
        mid = r.big[pl.ds(at + PAD, T), H : 2 * H]
        hi = r.big[pl.ds(at, T + 2 * PAD), 2 * H : 3 * H][PAD + DIL : PAD + DIL + T]
        v = lo * wide(r.mb[rows, :], H) + mid + hi * wide(r.ma[rows, :], H)
        r.conv[rows, :] = v
        r.acc2[0] += colsum(v)
        r.acc2[1] += colsum(v * v)

    loop(T, R - T, T, gather_taps)
    k.halo_end(r)
    gather_taps(0)
    gather_taps(R - T)
    k.ar_begin(r, 1, squash(r.acc2[0]), squash(r.acc2[1]))
    k.ar_middle(r, 1)
    if k.packed:
        k.ag_last(r, 5)

    k.have("og", "sw", "species", "g2", "b2", "run1", "run2")
    at_start = [r.species[0]] + [r.species[s] for s in starts]
    weights = [jnp.where(sp == 0, r.sw[0:1, :], r.sw[1:2, :]) for sp in at_start]

    def row_weight(at, tile):
        row = row_tile(at, tile)
        w = jnp.broadcast_to(weights[0], (tile, C))
        for s, v in zip(starts, weights[1:]):
            w = jnp.where(wide(row, C) >= s, v, w)
        return w

    def branch_grad(at):
        rows = pl.ds(at, 128)
        r.bg[rows, :] = (r.og[rows, :].astype(F32) * row_weight(at, 128)).astype(BF)

    loop(0, R, 128, branch_grad)
    if k.packed:
        k.ag_unpack(r, 3)

    def act_two_grad(at):
        rows = pl.ds(at, 1024)
        r.p2g[rows, :] = lax.dot_general(
            r.bg[rows, :], r.pf[...], (((1,), (1,)), ((), ())), preferred_element_type=F32
        )

    loop(0, R, 1024, act_two_grad)
    sum2, sq2 = k.ar_end(r, 1)
    mean2 = sum2 / N
    var2 = sq2 / N - mean2 * mean2
    inv2 = lax.rsqrt(var2 + EPSILON)
    minv2 = mean2 * inv2
    gain2 = r.g2[...].reshape(1, H)
    gain2h, bias2h = HALF_SLOPE * gain2, HALF_SLOPE * r.b2[...].reshape(1, H)
    r.acc2[...] = jnp.zeros_like(r.acc2)

    def second_norm(at):
        rows = pl.ds(at, 256)
        zh = r.conv[rows, :] * inv2 - minv2
        a, s = gelu_all(zh * gain2h + bias2h)
        r.act2[rows, :] = a.astype(BF)
        p = r.p2g[rows, :] * s
        r.p2g[rows, :] = p
        r.acc2[0] += colsum(p)
        r.acc2[1] += colsum(p * zh)

    loop(0, R, 256, second_norm)
    k.ar_begin(r, 2, squash(r.acc2[0]), squash(r.acc2[1]))
    k.edges_begin(r)
    k.ar_middle(r, 2)

    def block_output():
        for q in range(2):
            rows = pl.ds(q * 1024, 1024)
            br = jnp.dot(r.act2[rows, :], r.pf[...], preferred_element_type=F32)
            out[rows, :] = (r.x[rows, :].astype(F32) + br).astype(BF)

    pg = lax.dot_general(
        r.act2[...], r.bg[...], (((0,), (0,)), ((), ())), preferred_element_type=F32
    )
    if k.packed:
        k.pg_pack(r, pg)
        k.pg_core(r)
    else:
        r.point_grad[...] = pg
    bsum, gsum = k.ar_end(r, 2)
    gb2[...] = bsum.reshape(H)
    gg2[...] = gsum.reshape(H)
    a2 = inv2 * gain2
    lin2 = -a2 * (gsum / N) * inv2
    off2 = -a2 * (bsum / N) + a2 * (gsum / N) * minv2

    def cot(at):
        rows = pl.ds(at, 256)
        r.big[pl.ds(at + PAD, 256), 0:H] = (
            r.p2g[rows, :] * a2 + r.conv[rows, :] * lin2 + off2
        )

    loop(0, R, 256, cot)
    if k.packed:
        k.pg_diagonal(r)
    k.edges_end(r, a2, lin2, off2)
    T2 = 128

    def shifted(at):
        rows = pl.ds(at, T2)
        v = r.big[pl.ds(at, T2 + 2 * PAD), 0:H]
        r.back[rows, 0:H] = (v[PAD + DIL : PAD + DIL + T2] * wide(r.ma[rows, :], H)).astype(BF)
        r.back[rows, H : 2 * H] = v[PAD : PAD + T2].astype(BF)
        r.back[rows, 2 * H : 3 * H] = (v[PAD - DIL : PAD - DIL + T2] * wide(r.mb[rows, :], H)).astype(BF)

    loop(0, R, T2, shifted)

    M = C // 2
    for i, m in enumerate(range(0, C, M)):
        cg = lax.dot_general(
            r.act[:, m : m + M], r.back[...], (((0,), (0,)), ((), ())), preferred_element_type=F32
        )
        if k.packed:
            k.rs_pack(r, cg, i)
            k.rs_core(r, i)
            if i == 0:
                k.pg_plane(r)
        else:
            for j in range(3):
                r.conv_grad[j, m : m + M, :] = cg[:, j * H : j * H + H]

    minv1 = mean1 * inv1
    r.acc1[...] = jnp.zeros_like(r.acc1)
    both = lambda f, m: (f(r, m, 0), f(r, m, 1))
    steps = (
        lambda: both(k.rs_diagonal, 1),
        lambda: k.pg_column(r),
        lambda: both(k.rs_plane, 0),
        lambda: None,
    )
    if k.packed:
        both(k.rs_diagonal, 0)
    for q in range(4):
        rows = slice(q * Q, q * Q + Q)
        ag = lax.dot_general(
            r.back[rows, :], r.wf[...], (((1,), (1,)), ((), ())), preferred_element_type=F32
        )
        p = ag * r.slope[rows, :].astype(F32)
        r.big[rows, 0:C] = p
        r.acc1[0] += colsum(p)
        r.acc1[1] += colsum(p * (r.x[rows, :].astype(F32) * inv1 - minv1))
        if k.packed:
            steps[q]()
    k.ar_begin(r, 3, squash(r.acc1[0]), squash(r.acc1[1]))
    k.ar_middle(r, 3)
    if k.packed:
        both(k.rs_plane, 1)
    block_output()
    if k.packed:
        both(k.rs_column, 0)
    unbias = N / (N - 1.0)
    new1[0:1, :] = MOMENTUM * r.run1[0:1, :] + (1.0 - MOMENTUM) * mean1
    new1[1:2, :] = MOMENTUM * r.run1[1:2, :] + (1.0 - MOMENTUM) * (var1 * unbias)
    new2[0:1, :] = MOMENTUM * r.run2[0:1, :] + (1.0 - MOMENTUM) * mean2
    new2[1:2, :] = MOMENTUM * r.run2[1:2, :] + (1.0 - MOMENTUM) * (var2 * unbias)
    bsum1, gsum1 = k.ar_end(r, 3)
    gb1[...] = bsum1.reshape(C)
    gg1[...] = gsum1.reshape(C)
    a1 = inv1 * gain1
    lin1 = -a1 * (gsum1 / N) * inv1
    off1 = -a1 * (bsum1 / N) + a1 * (gsum1 / N) * minv1

    def last(at):
        rows = pl.ds(at, 128)
        v = r.og[rows, :].astype(F32) * row_weight(at, 128)
        v = v + r.big[rows, 0:C] * a1 + r.x[rows, :].astype(F32) * lin1 + off1
        ig[rows, :] = v.astype(BF)

    if k.packed:
        both(k.rs_column, 1)
    loop(0, R // 2, 128, last)
    loop(R // 2, R, 128, last)
    if k.packed:
        k.pg_end(r)
        k.rs_end(r)


def hand_out(n, large, *refs):
    ins, outs, sems = refs[:n], refs[n : 2 * n], refs[2 * n]
    copies = [pltpu.make_async_copy(ins[i], outs[i], sems.at[i]) for i in range(n)]
    for cp in copies:
        cp.start()
    for cp in copies:
        cp.wait()


def body(
    mesh,
    activations,
    out_grad,
    species,
    first_start,
    species_weight,
    conv_weight,
    point_weight,
    gain_one,
    bias_one,
    gain_two,
    bias_two,
    running_one,
    running_two,
):
    rows, C = activations.shape
    ndp, nsub = mesh.shape["dp"], mesh.shape["sub"]
    cw, hw = conv_weight.shape[1:]
    taps, H = conv_weight.shape[0], hw * nsub
    packed = cw == 96 and hw == 96 and nsub == 4 and ndp % 2 == 0
    if not packed:
        conv_weight = lax.all_gather(conv_weight, "dp", axis=1, tiled=True)
        conv_weight = lax.all_gather(conv_weight, "sub", axis=2, tiled=True)
        conv_weight = jnp.transpose(conv_weight, (1, 0, 2)).reshape(C, taps * H)
        point_weight = lax.all_gather(point_weight, "dp", axis=1, tiled=True)
        point_weight = lax.all_gather(point_weight, "sub", axis=0, tiled=True)
    k = Kernel(mesh, rows, C, H, packed)
    scratch = k.scratch()
    here = pl.BlockSpec(memory_space=pl.ANY)
    vmem = pl.BlockSpec(memory_space=pltpu.VMEM)
    shapes = [
        ((rows, C), BF),
        ((rows, C), BF),
        ((taps, cw, hw) if packed else (taps, C, H), F32),
        ((hw, cw) if packed else (H, C), F32),
        ((C,), F32),
        ((C,), F32),
        ((H,), F32),
        ((H,), F32),
        ((2, C), F32),
        ((2, H), F32),
    ]
    held = [packed or i not in (2, 3) for i in range(len(shapes))]
    outs = pl.pallas_call(
        functools.partial(kernel, k, 13, len(shapes), list(scratch)),
        out_shape=[
            pltpu.VMEM(*s) if in_vmem else jax.ShapeDtypeStruct(*s) for s, in_vmem in zip(shapes, held)
        ],
        in_specs=[here] * 13,
        out_specs=[vmem] * len(shapes),
        scratch_shapes=list(scratch.values()),
        compiler_params=pltpu.CompilerParams(
            collective_id=0, has_side_effects=True, vmem_limit_bytes=(55 if packed else 54) * 2**20
        ),
    )(
        activations,
        out_grad,
        species,
        first_start,
        species_weight,
        conv_weight,
        point_weight,
        gain_one,
        bias_one,
        gain_two,
        bias_two,
        running_one,
        running_two,
    )
    keep = [i for i in range(len(shapes)) if held[i]]
    n = len(keep)
    given = pl.pallas_call(
        functools.partial(hand_out, n, 2),
        out_shape=[jax.ShapeDtypeStruct(*shapes[i]) for i in keep],
        in_specs=[vmem] * n,
        out_specs=[here] * n,
        scratch_shapes=[pltpu.SemaphoreType.DMA((n,))],
        compiler_params=pltpu.CompilerParams(vmem_limit_bytes=2**20),
    )(*[pltpu.with_memory_space_constraint(outs[i], pltpu.VMEM) for i in keep])
    outs = list(outs)
    for i, v in zip(keep, given):
        outs[i] = v
    if not packed:
        conv_grad, point_grad = outs[2], outs[3]
        conv_grad = lax.psum_scatter(conv_grad, "dp", scatter_dimension=1, tiled=True)
        point_grad = lax.psum_scatter(point_grad, "dp", scatter_dimension=1, tiled=True)
        outs[2] = lax.psum_scatter(conv_grad, "sub", scatter_dimension=2, tiled=True)
        outs[3] = lax.psum_scatter(point_grad, "sub", scatter_dimension=0, tiled=True)
    return tuple(outs)


def solution(mesh):
    in_specs = (
        P(("dp", "sub"), None),
        P(("dp", "sub"), None),
        P(("dp", "sub")),
        P(("dp", "sub")),
        P(),
        P(None, "dp", "sub"),
        P("sub", "dp"),
        P(),
        P(),
        P(),
        P(),
        P(),
        P(),
    )
    out_specs = (
        P(("dp", "sub"), None),
        P(("dp", "sub"), None),
        P(None, "dp", "sub"),
        P("sub", "dp"),
        P(),
        P(),
        P(),
        P(),
        P(),
        P(),
    )
    return jax.shard_map(
        functools.partial(body, mesh), mesh=mesh, in_specs=in_specs, out_specs=out_specs, check_vma=False
    )
```

```python
import functools

import jax
import jax.numpy as jnp
from jax import lax
from jax.experimental import pallas as pl
from jax.experimental.pallas import tpu as pltpu
from jax.sharding import PartitionSpec as P

DIL = 11
SEQ_LEN = 1024
EPSILON = 0.001
MOMENTUM = 0.9
PAD = 16
HALF_SLOPE = 0.851
BF = jnp.bfloat16
F32 = jnp.float32
MESH = pl.DeviceIdType.MESH
PARTS = ((0, 48), (48, 48), (96, 48), (144, 48), (192, 32), (224, 80))
CONV_ROWS, SLOT_ROWS = 224, 304
SIDE = 112


def gelu_all(u):
    t = jnp.tanh(u)
    s = 0.5 * t + 0.5
    return (u * s) * (1.0 / HALF_SLOPE), s + u * (0.5 - 0.5 * t * t)


def colsum(v):
    return jnp.sum(v.reshape(v.shape[0] // 8, 8, v.shape[1]), axis=0)


def squash(v):
    return jnp.sum(v, axis=0, keepdims=True)


def loop(first, last, tile, f):
    def one(i, carry):
        f(pl.multiple_of(first + i * tile, tile))
        return carry

    lax.fori_loop(0, (last - first) // tile, one, 0)


def row_tile(start, tile):
    return start + lax.broadcasted_iota(jnp.int32, (tile, 128), 0)


def wide(m, n):
    return jnp.concatenate([m] * (n // 128), axis=1)


def lanes_of(rows):
    return lax.broadcasted_iota(jnp.int32, (rows, 128), 1)


def join(pieces):
    lane = lanes_of(pieces[0].shape[0])
    return [jnp.where(lane < 96 - 32 * i, pieces[i], pieces[i + 1]) for i in range(3)]


def split(tiles):
    lane = lanes_of(tiles[0].shape[0])
    return [
        tiles[0],
        jnp.where(lane >= 96, tiles[0], tiles[1]),
        jnp.where(lane >= 64, tiles[1], tiles[2]),
        tiles[2],
    ]


def free(i, lane):
    at = (96 * i + 96) % 128
    return (lane >= at) & (lane < at + 32)


def narrow(v, i):
    return pltpu.roll(v, 96 - 32 * i, 1)


def widen(blocks, i):
    lane = lanes_of(blocks[0].shape[0])
    moved = [pltpu.roll(b, 32 + 32 * j, 1) for j, b in enumerate(blocks)]
    inside = lambda j: (lane >= (96 * i + 32 * j) % 128) & (lane < (96 * i + 32 * j) % 128 + 32)
    return jnp.where(inside(0), moved[0], jnp.where(inside(1), moved[1], moved[2]))


class Kernel:
    def __init__(self, mesh, rows, channels, hidden, packed):
        self.ndp, self.nsub = mesh.shape["dp"], mesh.shape["sub"]
        self.rows, self.C, self.H = rows, channels, hidden
        self.packed = packed
        self.total = rows * self.ndp * self.nsub
        self.chips = self.ndp * self.nsub // 2
        self.nz = self.ndp // 2
        self.cw, self.hw = channels // self.ndp, hidden // self.nsub
        self.half = self.cw // 2
        self.sent, self.coming, self.local = [], {}, {}

    def scratch(self):
        R, C, H = self.rows, self.C, self.H
        V, D = pltpu.VMEM, pltpu.SemaphoreType.DMA
        s = dict(
            x=V((R, C), BF),
            og=V((R, C), BF),
            act=V((R, C), BF),
            slope=V((R, C), BF),
            big=V((R + 2 * PAD, 3 * H), F32),
            conv=V((R, H), F32),
            p2g=V((R, H), F32),
            act2=V((R, H), BF),
            back=V((R, 3 * H), BF),
            mb=V((R, 128), F32),
            ma=V((R, 128), F32),
            hs=V((2, PAD, H), F32),
            halo=V((2, PAD, H), F32),
            es=V((2, PAD, 2 * H + 128), F32),
            edge=V((2, PAD, 2 * H + 128), F32),
            acc1=V((2, 8, C), F32),
            acc2=V((2, 8, H), F32),
            c0=V((2, 2, C), F32),
            c1=V((2, 2, H), F32),
            c2=V((2, 2, H), F32),
            c3=V((2, 2, C), F32),
            s0=V((self.chips, 2, C), F32),
            s1=V((self.chips, 2, H), F32),
            s2=V((self.chips, 2, H), F32),
            s3=V((self.chips, 2, C), F32),
            wf=V((C, 3 * H), BF),
            pf=V((H, C), BF),
            sw=V((2, C), F32),
            g1=V((C,), F32),
            b1=V((C,), F32),
            g2=V((H,), F32),
            b2=V((H,), F32),
            run1=V((2, C), F32),
            run2=V((2, H), F32),
            species=pltpu.SMEM((R,), jnp.int32),
            first=pltpu.SMEM((1,), jnp.int32),
            ar_send=D((4, 2)),
            ar_recv=D((4, 2)),
            insem=D((24,)),
            halo_send=D((2, 2)),
            halo_recv=D((2, 2)),
        )
        if self.packed:
            nz = self.nz
            s.update(
                cshard=V((3, self.cw, self.hw), BF),
                pshard=V((self.hw, self.cw), BF),
                ag_send=D((len(PARTS), 3)),
                ag_z=D((len(PARTS),)),
                ag_own=D((len(PARTS), 2)),
                ag_oth=D((len(PARTS), 2)),
                ag_d=D((len(PARTS),)),
                ag_core=D((len(PARTS), 4)),
                ra=V((nz, 2, 2, 2, SIDE, 128), F32),
                rs=V((nz, 2, 2, 2, SIDE, 128), BF),
                rc=V((nz, 2, 2, 2, SIDE, 128), BF),
                st=V((nz, 2, 2, 2, SIDE, 128), BF),
                rd=V((nz, 2, SIDE, 128), BF),
                rxy=V((nz, 2, 2, SIDE, 128), BF),
                rz=V((2, 3, SIDE, 128), BF),
                rs_send=D((nz, 2, 3)),
                rs_core=D((nz, 2)),
                rs_d=D((nz, 2)),
                rs_xy=D((nz, 2, 2)),
                rz_send=D((2,)),
                rs_z=D((2,)),
                pa=V((2, 2, nz, 80, 128), F32),
                ps=V((2, 2, nz, 80, 128), BF),
                pc=V((2, 2, nz, 80, 128), BF),
                pt=V((2, 2, nz, 80, 128), BF),
                pd=V((nz, 80, 128), BF),
                pxy=V((2, nz, 80, 128), BF),
                pz=V((3, 80, 128), BF),
                p_send=D((4,)),
                p_recv=D((5,)),
            )
            s.update({f"w{j}": V((2, 2, 2, nz, n, 128), BF) for j, (_, n) in enumerate(PARTS)})
        return s

    def place(self):
        self.dp, self.sub = lax.axis_index("dp"), lax.axis_index("sub")
        self.z, self.y = self.dp // 2, lax.rem(self.dp, 2)
        self.x, self.c = self.sub // 2, lax.rem(self.sub, 2)
        n = self.ndp * self.nsub
        me = self.dp * self.nsub + self.sub
        nxt, prv = lax.rem(me + 1, n), lax.rem(me + n - 1, n)
        far = lax.rem(me + jnp.where(self.c == 1, 1, n - 1), n)
        self.core_nbr = (self.dp, self.x * 2 + 1 - self.c)
        self.x_nbr = (self.dp, (1 - self.x) * 2 + self.c)
        self.y_nbr = (self.z * 2 + 1 - self.y, self.sub)
        self.next = (nxt // self.nsub, lax.rem(nxt, self.nsub))
        self.prev = (prv // self.nsub, lax.rem(prv, self.nsub))
        self.far = (far // self.nsub, lax.rem(far, self.nsub))
        self.chip = self.dp * (self.nsub // 2) + self.x

    def z_device(self, d):
        return (lax.rem(self.z + d, self.nz) * 2 + self.y, self.sub)

    def each_chip(self, f):
        if self.chips == 16 and self.nsub == 4:
            z, y, x = self.z, self.y, self.x
            zs = (z, z + 1 - 2 * lax.rem(z, 2), lax.rem(z + 2, 4), 3 - z)
            for d in range(15, 0, -1):
                yy = 1 - y if (d // 2) % 2 else y
                xx = 1 - x if d % 2 else x
                f((zs[d // 4] * 2 + yy, xx * 2 + self.c))
        else:
            side = self.nsub // 2

            def one(d, carry):
                chip = lax.rem(self.chip + d, self.chips)
                f((chip // side, lax.rem(chip, side) * 2 + self.c))
                return carry

            lax.fori_loop(1, self.chips, one, 0)

    def greet(self):
        b = pltpu.get_barrier_semaphore()

        def hello(device):
            pl.semaphore_signal(b, inc=1, device_id=device, device_id_type=MESH)

        self.each_chip(hello)
        hello(self.far)
        hello(self.core_nbr)

    def greeted(self):
        pl.semaphore_wait(pltpu.get_barrier_semaphore(), self.chips + 1)

    def put(self, src, dst, send, recv, device, key=None, ref=None):
        pltpu.make_async_remote_copy(
            src, dst, send, recv, device_id=device, device_id_type=MESH
        ).start()
        self.sent.append((src, send))
        if key is not None:
            self.coming[key] = (dst if ref is None else ref, recv)

    def arrived(self, *keys):
        for key in keys:
            ref, sem = self.coming.pop(key)
            pltpu.make_async_copy(ref, ref, sem).wait()

    def fetch(self, key, src, dst, sem):
        self.local[key] = cp = pltpu.make_async_copy(src, dst, sem)
        cp.start()

    def have(self, *keys):
        for key in keys:
            self.local.pop(key).wait()

    def drain(self):
        self.have(*list(self.local))
        self.arrived(*list(self.coming))
        for ref, sem in self.sent:
            pltpu.make_async_copy(ref, ref, sem).wait()


    def ar_begin(self, r, i, top, low):
        cs = getattr(r, f"c{i}")
        cs[self.c, 0:1, :] = top
        cs[self.c, 1:2, :] = low
        mine = cs.at[self.c]
        self.put(mine, mine, r.ar_send.at[i, 0], r.ar_recv.at[i, 0], self.core_nbr, ("c", i))

    def ar_middle(self, r, i):
        cs, sl = getattr(r, f"c{i}"), getattr(r, f"s{i}")
        self.arrived(("c", i))
        sl[self.chip] = cs[0] + cs[1]
        mine = sl.at[self.chip]
        most = sl.at[pl.ds(0, self.chips - 1)]
        send, recv = r.ar_send.at[i, 1], r.ar_recv.at[i, 1]

        def one(device):
            pltpu.make_async_remote_copy(
                mine, mine, send, recv, device_id=device, device_id_type=MESH
            ).start()

        self.each_chip(one)
        self.sent.append((most, send))
        self.coming["s", i] = (most, recv)

    def ar_end(self, r, i):
        sl = getattr(r, f"s{i}")
        self.arrived(("s", i))
        if self.chips <= 16:
            total = sl[0]
            for k in range(1, self.chips):
                total = total + sl[k]
        else:
            total = lax.fori_loop(1, self.chips, lambda k, t: t + sl[k], sl[0])
        return total[0:1, :], total[1:2, :]

    def group(self, ref, flip_y=False, flip_x=False):
        y = 1 - self.y if flip_y else self.y
        x = 1 - self.x if flip_x else self.x
        return ref.at[y, x, self.c]

    def ag_pack(self, r):
        lane = lanes_of(96)
        full = lambda v: jnp.concatenate([v.astype(F32), jnp.zeros((96, 32), F32)], axis=1)
        place = lambda v, i: pltpu.roll(v, lax.rem(96 * i, 128), 1).astype(BF)
        here = (self.y, self.x, self.c, 0)
        t2, p = full(r.cshard[2]), full(r.pshard[...])
        rest = jnp.concatenate([narrow(t2, i)[32:96] for i in range(3)], axis=0)
        for j in range(2):
            v = place(jnp.where(lane < 96, full(r.cshard[j]), rest[96 * j : 96 * j + 96]), self.sub)
            for h in range(2):
                (r.w0, r.w1, r.w2, r.w3)[2 * j + h][here] = v[48 * h : 48 * h + 48]
        r.w4[here] = place(t2[0:32], self.sub)
        rest = jnp.concatenate([narrow(p[80:96], i) for i in range(3)] + [jnp.zeros((32, 128), F32)], axis=0)
        r.w5[here] = place(jnp.where(lane[0:80] < 96, p[0:80], rest), self.dp)

    def ag_start(self, r, j):
        grp = self.group(getattr(r, f"w{j}"))
        slot, some = grp.at[0], grp.at[pl.ds(1, self.nz - 1)]
        for d in range(1, self.nz):
            pltpu.make_async_remote_copy(
                slot, grp.at[self.nz - d], r.ag_send.at[j, 0], r.ag_z.at[j],
                device_id=self.z_device(d), device_id_type=MESH,
            ).start()
        self.sent.append((some, r.ag_send.at[j, 0]))
        self.coming["z", j] = (some, r.ag_z.at[j])
        self.put(slot, slot, r.ag_send.at[j, 1], r.ag_own.at[j, 0], self.y_nbr, ("yo", j))
        self.put(slot, slot, r.ag_send.at[j, 1], r.ag_own.at[j, 1], self.x_nbr, ("xo", j))

    def to_core(self, r, j, i, grp):
        self.put(grp, grp, r.ag_send.at[j, 2], r.ag_core.at[j, i], self.core_nbr, ("core", j, i))

    def ag_plane(self, r, j):
        self.arrived(("z", j))
        grp = self.group(getattr(r, f"w{j}"))
        some = grp.at[pl.ds(1, self.nz - 1)]
        self.put(some, some, r.ag_send.at[j, 1], r.ag_oth.at[j, 0], self.y_nbr, ("yr", j))
        self.put(some, some, r.ag_send.at[j, 1], r.ag_oth.at[j, 1], self.x_nbr, ("xr", j))
        self.to_core(r, j, 0, grp)

    def ag_diagonal(self, r, j):
        g = getattr(r, f"w{j}")
        by_y, by_x = self.group(g, flip_y=True), self.group(g, flip_x=True)
        h = j % 2
        first, second = (by_y, by_x) if h == 0 else (by_x, by_y)
        self.arrived(("yx"[h] + "o", j), ("yx"[h] + "r", j))
        self.put(
            first, first, r.ag_send.at[j, 1], r.ag_d.at[j], (self.x_nbr, self.y_nbr)[h], ("d", j)
        )
        self.to_core(r, j, 1, first)
        self.arrived(("xy"[h] + "o", j), ("xy"[h] + "r", j))
        self.to_core(r, j, 2, second)

    def ag_last(self, r, j):
        self.arrived(("d", j))
        self.to_core(r, j, 3, self.group(getattr(r, f"w{j}"), True, True))

    def each_slot(self):
        for z in range(self.nz):
            at = lax.rem(z - self.z + self.nz, self.nz)
            for y in range(2):
                yield z, y, at

    def ag_unpack(self, r, k):
        H, cw, hw = self.H, self.cw, self.hw
        for j in ((0, 1), (2, 3), (4,), (5,))[k]:
            self.arrived(*[("core", j, i) for i in range(4)])

        def slot(j, y, s, at):
            return getattr(r, f"w{j}").at[y, s // 2, s % 2, at]

        def keep(ref, row, lane, tiles):
            for i, t in enumerate(tiles):
                ref[row : row + t.shape[0], lane + 128 * i : lane + 128 * i + 128] = t.astype(BF)

        if k < 3:
            for z, y, at in self.each_slot():
                low = (z * 2 + y) * cw
                if k < 2:
                    for h in range(2):
                        tiles = join([slot(2 * k + h, y, s, at)[...].astype(F32) for s in range(4)])
                        keep(r.wf, low + 48 * h, k * H, tiles)
                else:
                    keep(r.wf, low, 2 * H, join([slot(4, y, s, at)[...].astype(F32) for s in range(4)]))
                    pieces = []
                    for s in range(4):
                        parts = [slot(j, y, s, at) for j in range(4)]
                        cut = lambda j, a, b: parts[j][a:b, :].astype(F32)
                        pieces.append(widen((
                            jnp.concatenate([cut(0, 0, 48), cut(1, 0, 16)], axis=0),
                            jnp.concatenate([cut(1, 16, 48), cut(2, 0, 32)], axis=0),
                            jnp.concatenate([cut(2, 32, 48), cut(3, 0, 48)], axis=0),
                        ), s))
                    keep(r.wf, low + 32, 2 * H, join(pieces))
        else:
            ats = {z: at for z, _, at in self.each_slot()}
            for s in range(4):
                for q in range(2):
                    got = [slot(5, dp % 2, s, ats[dp // 2])[...].astype(F32) for dp in range(4 * q, 4 * q + 4)]
                    keep(r.pf, s * hw, 4 * q * cw, join([v[0:80] for v in got]))
                    rest = [widen([v[16 * i : 16 * i + 16] for i in range(3)], dp) for dp, v in enumerate(got)]
                    keep(r.pf, s * hw + 80, 4 * q * cw, join(rest))

    def rs_pack(self, r, cg, m, first):
        H, cw = self.H, self.cw
        mine = self.c == 0
        lane = lanes_of(96)
        for y in range(2):
            low = first + y * cw
            taps = [
                split([cg[low : low + cw, t * H + 128 * i : t * H + 128 * i + 128] for i in range(3)])
                for t in range(3)
            ]
            for x in range(2):
                both = []
                for s in (2 * x, 2 * x + 1):
                    t2 = taps[2][s]
                    rest = jnp.concatenate([narrow(t2[32:96], i) for i in range(3)], axis=0)
                    gap = free(s, lane)
                    both.append((
                        jnp.where(gap, rest[0:96], taps[0][s]),
                        jnp.where(gap, rest[96:192], taps[1][s]),
                        t2[0:32],
                    ))
                own = [jnp.where(mine, p, q) for p, q in zip(*both)]
                other = [jnp.where(mine, q, p).astype(BF) for p, q in zip(*both)]
                for ref, v in ((r.ra, own), (r.rs, other)):
                    ref[m, 0, y, x, 0:96, :] = v[0]
                    ref[m, 0, y, x, 96:112, :] = v[1][0:16]
                    ref[m, 1, y, x, 0:80, :] = v[1][16:96]
                    ref[m, 1, y, x, 80:112, :] = v[2]

    def rs_core(self, r, m):
        for h in range(2):
            self.put(r.rs.at[m, h], r.rc.at[m, h], r.rs_send.at[m, h, 0], r.rs_core.at[m, h], self.core_nbr, ("rc", m, h))

    def rs_diagonal(self, r, m, h):
        self.arrived(("rc", m, h))
        for y in range(2):
            for x in range(2):
                r.ra[m, h, y, x] += r.rc[m, h, y, x].astype(F32)
        y, x = 1 - self.y, 1 - self.x
        r.st[m, h, y, x] = r.ra[m, h, y, x].astype(BF)
        self.put(
            r.st.at[m, h, y, x], r.rd.at[m, h], r.rs_send.at[m, h, 1], r.rs_d.at[m, h],
            (self.x_nbr, self.y_nbr)[h], ("rd", m, h),
        )

    def rs_plane(self, r, m, h):
        self.arrived(("rd", m, h))
        via_y, via_x = (1 - self.y, self.x), (self.y, 1 - self.x)
        y, x = (via_y, via_x)[h]
        r.ra[m, h, y, x] += r.rd[m, h].astype(F32)
        for i, ((y, x), to) in enumerate(((via_y, self.y_nbr), (via_x, self.x_nbr))):
            r.st[m, h, y, x] = r.ra[m, h, y, x].astype(BF)
            self.put(r.st.at[m, h, y, x], r.rxy.at[m, h, i], r.rs_send.at[m, h, 2], r.rs_xy.at[m, h, i], to, ("rp", m, h, i))

    def rs_column(self, r, m, h):
        y, x = self.y, self.x
        self.arrived(("rp", m, h, 0), ("rp", m, h, 1))
        r.ra[m, h, y, x] += r.rxy[m, h, 0].astype(F32) + r.rxy[m, h, 1].astype(F32)
        r.st[m, h, y, x] = r.ra[m, h, y, x].astype(BF)
        d = lax.rem(self.z - m + self.nz, self.nz)

        @pl.when(d != 0)
        def _():
            pltpu.make_async_remote_copy(
                r.st.at[m, h, y, x], r.rz.at[h, d - 1], r.rz_send.at[h], r.rs_z.at[h],
                device_id=(m * 2 + self.y, self.sub), device_id_type=MESH,
            ).start()

        if m == self.nz - 1:
            self.sent.append((r.rz.at[h], r.rz_send.at[h]))
            self.coming["rz", h] = (r.rz.at[h], r.rs_z.at[h])

    def rs_end(self, r):
        v = []
        for h in range(2):
            self.arrived(("rz", h))
            t = r.ra[self.z, h, self.y, self.x]
            for i in range(3):
                t = t + r.rz[h, i].astype(F32)
            v.append(t)
        v = pltpu.roll(jnp.concatenate(v, axis=0), lax.rem(128 - lax.rem(96 * self.sub, 128), 128), 1)
        r.conv_grad[0] = v[0:96, 0:96]
        r.conv_grad[1] = v[96:192, 0:96]
        r.conv_grad[2, 0:32, :] = v[192:224, 0:96]
        r.conv_grad[2, 32:96, :] = widen([v[64 * i : 64 * i + 64] for i in range(3)], 0)[:, 0:96]

    def pg_pack(self, r, pg):
        cw, hw = self.cw, self.hw
        mine = self.c == 0
        lane = lanes_of(80)
        pieces = []
        for s in range(4):
            rows = slice(s * hw, s * hw + hw)
            pieces.append([
                p
                for q in range(2)
                for p in split([pg[rows, 4 * q * cw + 128 * i : 4 * q * cw + 128 * i + 128] for i in range(3)])
            ])
        for dp in range(self.ndp):
            for x in range(2):
                both = []
                for s in (2 * x, 2 * x + 1):
                    p = pieces[s][dp]
                    rest = jnp.concatenate([narrow(p[80:96], i) for i in range(3)] + [p[0:32]], axis=0)
                    both.append(jnp.where(free(dp, lane), rest, p[0:80]))
                r.pa[dp % 2, x, dp // 2] = jnp.where(mine, both[0], both[1])
                r.ps[dp % 2, x, dp // 2] = jnp.where(mine, both[1], both[0]).astype(BF)

    def pg_core(self, r):
        self.put(r.ps, r.pc, r.p_send.at[0], r.p_recv.at[0], self.core_nbr, "pc")

    def pg_diagonal(self, r):
        self.arrived("pc")
        for y in range(2):
            for x in range(2):
                r.pa[y, x] += r.pc[y, x].astype(F32)
        y, x = 1 - self.y, 1 - self.x
        r.pt[y, x] = r.pa[y, x].astype(BF)
        self.put(r.pt.at[y, x], r.pd, r.p_send.at[1], r.p_recv.at[1], self.x_nbr, "pd")

    def pg_plane(self, r):
        self.arrived("pd")
        via_y, via_x = (1 - self.y, self.x), (self.y, 1 - self.x)
        r.pa[via_y[0], via_y[1]] += r.pd[...].astype(F32)
        for i, ((y, x), to) in enumerate(((via_y, self.y_nbr), (via_x, self.x_nbr))):
            r.pt[y, x] = r.pa[y, x].astype(BF)
            self.put(r.pt.at[y, x], r.pxy.at[i], r.p_send.at[2], r.p_recv.at[2 + i], to, ("pp", i))

    def pg_column(self, r):
        y, x = self.y, self.x
        self.arrived(("pp", 0), ("pp", 1))
        r.pa[y, x] += r.pxy[0].astype(F32) + r.pxy[1].astype(F32)
        r.pt[y, x] = r.pa[y, x].astype(BF)
        for d in range(1, self.nz):
            to = lax.rem(self.z + d, self.nz)
            pltpu.make_async_remote_copy(
                r.pt.at[y, x, to], r.pz.at[self.nz - d - 1], r.p_send.at[3], r.p_recv.at[4],
                device_id=self.z_device(d), device_id_type=MESH,
            ).start()
        self.sent.append((r.pz, r.p_send.at[3]))
        self.coming["pz"] = (r.pz, r.p_recv.at[4])

    def pg_end(self, r):
        self.arrived("pz")
        v = r.pa[self.y, self.x, self.z]
        for i in range(3):
            v = v + r.pz[i].astype(F32)
        v = pltpu.roll(v, lax.rem(128 - lax.rem(96 * self.dp, 128), 128), 1)
        r.point_grad[0:80, :] = v[:, 0:96]
        r.point_grad[80:96, :] = widen([v[16 * i : 16 * i + 16] for i in range(3)], 0)[:, 0:96]

    def halo_up(self, r):
        R, H = self.rows, self.H
        r.hs[1] = r.big[R : R + PAD, 0:H] * wide(r.ma[R - PAD : R], H)
        self.put(r.hs.at[1], r.halo.at[1], r.halo_send.at[0, 1], r.halo_recv.at[0, 1], self.next, ("h", 1))

    def halo_down(self, r):
        H = self.H
        r.hs[0] = r.big[PAD : 2 * PAD, 2 * H : 3 * H] * wide(r.mb[0:PAD], H)
        self.put(r.hs.at[0], r.halo.at[0], r.halo_send.at[0, 0], r.halo_recv.at[0, 0], self.prev, ("h", 0))

    def halo_end(self, r):
        R, H = self.rows, self.H
        self.arrived(("h", 0), ("h", 1))
        r.big[R + PAD : R + 2 * PAD, 2 * H : 3 * H] = r.halo[0]
        r.big[0:PAD, 0:H] = r.halo[1]

    def edges_begin(self, r):
        R, H = self.rows, self.H
        for j, (at, m, to) in enumerate(((0, r.mb, self.prev), (R - PAD, r.ma, self.next))):
            mask = m[at : at + PAD]
            r.es[j, :, 0:H] = r.p2g[at : at + PAD, :] * wide(mask, H)
            r.es[j, :, H : 2 * H] = r.conv[at : at + PAD, :] * wide(mask, H)
            r.es[j, :, 2 * H :] = mask
            self.put(r.es.at[j], r.edge.at[j], r.halo_send.at[1, j], r.halo_recv.at[1, j], to, ("e", j))

    def edges_end(self, r, a2, lin2, off2):
        R, H = self.rows, self.H
        self.arrived(("e", 0), ("e", 1))
        for j, at in ((0, R + PAD), (1, 0)):
            r.big[at : at + PAD, 0:H] = (
                r.edge[j, :, 0:H] * a2 + r.edge[j, :, H : 2 * H] * lin2 + wide(r.edge[j, :, 2 * H :], H) * off2
            )


class Refs:
    pass


def kernel(k, n_in, n_out, names, *refs):
    r = Refs()
    for name, ref in zip(names, refs[n_in + n_out :]):
        setattr(r, name, ref)
    k.sent, k.coming, k.local = [], {}, {}
    k.place()
    work(k, r, refs[:n_in], refs[n_in : n_in + n_out])
    k.drain()


def work(k, r, ins, outs):
    (x_hbm, og_hbm, species, first, sw, conv_w, point_w, g1, b1, g2, b2, run1, run2) = ins
    (out, ig, r.conv_grad, r.point_grad, gg1, gb1, gg2, gb2, new1, new2) = outs
    R, C, H, N = k.rows, k.C, k.H, k.total
    Q = R // 4
    r.bg = ig
    k.greet()
    if k.packed:
        k.fetch("cw", conv_w, r.cshard, r.insem.at[5])
        k.fetch("pw", point_w, r.pshard, r.insem.at[6])
    for q in range(4):
        rows = pl.ds(q * Q, Q)
        k.fetch(("x", q), x_hbm.at[rows], r.x.at[rows], r.insem.at[q])
    small = dict(first=first, g1=g1, b1=b1, g2=g2, b2=b2, sw=sw, run1=run1, run2=run2, species=species)
    for i, (name, ref) in enumerate(small.items()):
        k.fetch(name, ref, getattr(r, name), r.insem.at[7 + i])
    k.fetch("og", og_hbm, r.og, r.insem.at[4])
    if not k.packed:
        k.fetch("cw", conv_w, r.wf, r.insem.at[5])
        k.fetch("pw", point_w, r.pf, r.insem.at[6])
    else:
        k.have("cw", "pw")
        k.ag_pack(r)

    def sums(q):
        k.have(("x", q))
        v = r.x[q * Q : q * Q + Q, :].astype(F32)
        r.acc1[0] += colsum(v)
        r.acc1[1] += colsum(v * v)

    r.acc1[...] = jnp.zeros_like(r.acc1)
    for q in range(2):
        sums(q)
    k.greeted()
    if k.packed:
        for j in range(5):
            k.ag_start(r, j)
    for q in range(2, 4):
        sums(q)
    k.ar_begin(r, 0, squash(r.acc1[0]), squash(r.acc1[1]))

    k.have("first")
    fs = r.first[0]
    starts = [fs + SEQ_LEN * j for j in range(R // SEQ_LEN)]
    k.ar_middle(r, 0)
    def masks(at):
        row = row_tile(at, 128)
        before = jnp.ones((128, 128), F32)
        after = jnp.ones((128, 128), F32)
        for s in starts:
            before = jnp.where((row >= s) & (row < s + DIL), 0.0, before)
            after = jnp.where((row >= s - DIL) & (row < s), 0.0, after)
        r.mb[pl.ds(at, 128), :] = before
        r.ma[pl.ds(at, 128), :] = after

    loop(0, R, 128, masks)
    if k.packed:
        for j in range(5):
            k.ag_plane(r, j)
        k.ag_start(r, 5)
    k.have("g1", "b1")
    sum1, sq1 = k.ar_end(r, 0)
    mean1 = sum1 / N
    var1 = sq1 / N - mean1 * mean1
    inv1 = lax.rsqrt(var1 + EPSILON)
    gain1 = r.g1[...].reshape(1, C)
    scale1 = (HALF_SLOPE * gain1) * inv1
    shift1 = HALF_SLOPE * r.b1[...].reshape(1, C) - mean1 * scale1

    def act_tile(at):
        rows = pl.ds(at, 256)
        u = r.x[rows, :].astype(F32) * scale1 + shift1
        a, s = gelu_all(u)
        r.act[rows, :] = a.astype(BF)
        r.slope[rows, :] = s.astype(BF)

    steps = (
        lambda: (k.ag_diagonal(r, 0), k.ag_diagonal(r, 1)),
        lambda: (k.ag_diagonal(r, 2), k.ag_diagonal(r, 3)),
        lambda: (k.ag_diagonal(r, 4), k.ag_plane(r, 5)),
        lambda: (k.ag_last(r, 0), k.ag_last(r, 1)),
    )
    for q in range(4):
        loop(q * Q, q * Q + Q, 256, act_tile)
        if k.packed:
            steps[q]()
    if k.packed:
        k.ag_last(r, 2)
        k.ag_last(r, 3)
        k.ag_unpack(r, 0)
        k.ag_last(r, 4)
        k.ag_unpack(r, 1)
    else:
        k.have("cw", "pw")

    def product(at, rows, lanes):
        r.big[PAD + at : PAD + at + rows, lanes] = jnp.dot(
            r.act[at : at + rows, :], r.wf[:, lanes], preferred_element_type=F32
        )

    product(0, R // 2, slice(0, 2 * H))
    product(R // 2, R // 2, slice(0, 2 * H))
    if k.packed:
        k.ag_unpack(r, 2)
    k.halo_up(r)
    product(0, R // 2, slice(2 * H, 3 * H))
    k.halo_down(r)
    product(R // 2, R // 2, slice(2 * H, 3 * H))
    if k.packed:
        k.ag_diagonal(r, 5)
    r.acc2[...] = jnp.zeros_like(r.acc2)
    T = 256

    def gather_taps(at):
        rows = pl.ds(at, T)
        lo = r.big[pl.ds(at, T + 2 * PAD), 0:H][PAD - DIL : PAD - DIL + T]
        mid = r.big[pl.ds(at + PAD, T), H : 2 * H]
        hi = r.big[pl.ds(at, T + 2 * PAD), 2 * H : 3 * H][PAD + DIL : PAD + DIL + T]
        v = lo * wide(r.mb[rows, :], H) + mid + hi * wide(r.ma[rows, :], H)
        r.conv[rows, :] = v
        r.acc2[0] += colsum(v)
        r.acc2[1] += colsum(v * v)

    loop(T, R - T, T, gather_taps)
    k.halo_end(r)
    gather_taps(0)
    gather_taps(R - T)
    k.ar_begin(r, 1, squash(r.acc2[0]), squash(r.acc2[1]))
    k.ar_middle(r, 1)
    if k.packed:
        k.ag_last(r, 5)

    k.have("og", "sw", "species", "g2", "b2", "run1", "run2")
    at_start = [r.species[0]] + [r.species[s] for s in starts]
    weights = [jnp.where(sp == 0, r.sw[0:1, :], r.sw[1:2, :]) for sp in at_start]

    def row_weight(at, tile):
        row = row_tile(at, tile)
        w = jnp.broadcast_to(weights[0], (tile, C))
        for s, v in zip(starts, weights[1:]):
            w = jnp.where(wide(row, C) >= s, v, w)
        return w

    def branch_grad(at):
        rows = pl.ds(at, 128)
        r.bg[rows, :] = (r.og[rows, :].astype(F32) * row_weight(at, 128)).astype(BF)

    loop(0, R, 128, branch_grad)
    if k.packed:
        k.ag_unpack(r, 3)

    def act_two_grad(at):
        rows = pl.ds(at, 1024)
        r.p2g[rows, :] = lax.dot_general(
            r.bg[rows, :], r.pf[...], (((1,), (1,)), ((), ())), preferred_element_type=F32
        )

    loop(0, R, 1024, act_two_grad)
    sum2, sq2 = k.ar_end(r, 1)
    mean2 = sum2 / N
    var2 = sq2 / N - mean2 * mean2
    inv2 = lax.rsqrt(var2 + EPSILON)
    minv2 = mean2 * inv2
    gain2 = r.g2[...].reshape(1, H)
    gain2h, bias2h = HALF_SLOPE * gain2, HALF_SLOPE * r.b2[...].reshape(1, H)
    r.acc2[...] = jnp.zeros_like(r.acc2)

    def second_norm(at):
        rows = pl.ds(at, 256)
        zh = r.conv[rows, :] * inv2 - minv2
        a, s = gelu_all(zh * gain2h + bias2h)
        r.act2[rows, :] = a.astype(BF)
        p = r.p2g[rows, :] * s
        r.p2g[rows, :] = p
        r.acc2[0] += colsum(p)
        r.acc2[1] += colsum(p * zh)

    loop(0, R, 256, second_norm)
    k.ar_begin(r, 2, squash(r.acc2[0]), squash(r.acc2[1]))
    k.edges_begin(r)
    k.ar_middle(r, 2)

    def block_output():
        for q in range(2):
            rows = pl.ds(q * 1024, 1024)
            br = jnp.dot(r.act2[rows, :], r.pf[...], preferred_element_type=F32)
            out[rows, :] = (r.x[rows, :].astype(F32) + br).astype(BF)

    pg = lax.dot_general(
        r.act2[...], r.bg[...], (((0,), (0,)), ((), ())), preferred_element_type=F32
    )
    if k.packed:
        k.pg_pack(r, pg)
        k.pg_core(r)
    else:
        r.point_grad[...] = pg
    bsum, gsum = k.ar_end(r, 2)
    gb2[...] = bsum.reshape(H)
    gg2[...] = gsum.reshape(H)
    a2 = inv2 * gain2
    lin2 = -a2 * (gsum / N) * inv2
    off2 = -a2 * (bsum / N) + a2 * (gsum / N) * minv2

    def cot(at):
        rows = pl.ds(at, 256)
        r.big[pl.ds(at + PAD, 256), 0:H] = (
            r.p2g[rows, :] * a2 + r.conv[rows, :] * lin2 + off2
        )

    loop(0, R, 256, cot)
    if k.packed:
        k.pg_diagonal(r)
    k.edges_end(r, a2, lin2, off2)
    T2 = 128

    def shifted(at):
        rows = pl.ds(at, T2)
        v = r.big[pl.ds(at, T2 + 2 * PAD), 0:H]
        r.back[rows, 0:H] = (v[PAD + DIL : PAD + DIL + T2] * wide(r.ma[rows, :], H)).astype(BF)
        r.back[rows, H : 2 * H] = v[PAD : PAD + T2].astype(BF)
        r.back[rows, 2 * H : 3 * H] = (v[PAD - DIL : PAD - DIL + T2] * wide(r.mb[rows, :], H)).astype(BF)

    loop(0, R, T2, shifted)

    M = C // 2
    for i, m in enumerate(range(0, C, M)):
        cg = lax.dot_general(
            r.act[:, m : m + M], r.back[...], (((0,), (0,)), ((), ())), preferred_element_type=F32
        )
        if k.packed:
            for z in range(2):
                k.rs_pack(r, cg, 2 * i + z, z * (M // 2))
                k.rs_core(r, 2 * i + z)
            if i == 0:
                k.pg_plane(r)
        else:
            for j in range(3):
                r.conv_grad[j, m : m + M, :] = cg[:, j * H : j * H + H]

    minv1 = mean1 * inv1
    r.acc1[...] = jnp.zeros_like(r.acc1)
    both = lambda f, *ms: [f(r, m, h) for m in ms for h in range(2)]
    steps = (
        lambda: both(k.rs_diagonal, 2, 3),
        lambda: both(k.rs_plane, 0),
        lambda: (both(k.rs_plane, 1, 2), k.pg_column(r)),
        lambda: both(k.rs_plane, 3),
    )
    if k.packed:
        both(k.rs_diagonal, 0, 1)
    for q in range(4):
        rows = slice(q * Q, q * Q + Q)
        ag = lax.dot_general(
            r.back[rows, :], r.wf[...], (((1,), (1,)), ((), ())), preferred_element_type=F32
        )
        p = ag * r.slope[rows, :].astype(F32)
        r.big[rows, 0:C] = p
        r.acc1[0] += colsum(p)
        r.acc1[1] += colsum(p * (r.x[rows, :].astype(F32) * inv1 - minv1))
        if k.packed:
            steps[q]()
    k.ar_begin(r, 3, squash(r.acc1[0]), squash(r.acc1[1]))
    k.ar_middle(r, 3)
    if k.packed:
        both(k.rs_column, 0, 1)
    block_output()
    if k.packed:
        both(k.rs_column, 2)
    unbias = N / (N - 1.0)
    new1[0:1, :] = MOMENTUM * r.run1[0:1, :] + (1.0 - MOMENTUM) * mean1
    new1[1:2, :] = MOMENTUM * r.run1[1:2, :] + (1.0 - MOMENTUM) * (var1 * unbias)
    new2[0:1, :] = MOMENTUM * r.run2[0:1, :] + (1.0 - MOMENTUM) * mean2
    new2[1:2, :] = MOMENTUM * r.run2[1:2, :] + (1.0 - MOMENTUM) * (var2 * unbias)
    bsum1, gsum1 = k.ar_end(r, 3)
    gb1[...] = bsum1.reshape(C)
    gg1[...] = gsum1.reshape(C)
    a1 = inv1 * gain1
    lin1 = -a1 * (gsum1 / N) * inv1
    off1 = -a1 * (bsum1 / N) + a1 * (gsum1 / N) * minv1

    def last(at):
        rows = pl.ds(at, 128)
        v = r.og[rows, :].astype(F32) * row_weight(at, 128)
        v = v + r.big[rows, 0:C] * a1 + r.x[rows, :].astype(F32) * lin1 + off1
        ig[rows, :] = v.astype(BF)

    if k.packed:
        both(k.rs_column, 3)
    loop(0, R, 128, last)
    if k.packed:
        k.pg_end(r)
        k.rs_end(r)


def hand_out(n, large, *refs):
    ins, outs, sems = refs[:n], refs[n : 2 * n], refs[2 * n]
    copies = [pltpu.make_async_copy(ins[i], outs[i], sems.at[i]) for i in range(n)]
    for cp in copies:
        cp.start()
    for cp in copies:
        cp.wait()


def body(
    mesh,
    activations,
    out_grad,
    species,
    first_start,
    species_weight,
    conv_weight,
    point_weight,
    gain_one,
    bias_one,
    gain_two,
    bias_two,
    running_one,
    running_two,
):
    rows, C = activations.shape
    ndp, nsub = mesh.shape["dp"], mesh.shape["sub"]
    cw, hw = conv_weight.shape[1:]
    taps, H = conv_weight.shape[0], hw * nsub
    packed = cw == 96 and hw == 96 and nsub == 4 and ndp % 2 == 0
    if not packed:
        conv_weight = lax.all_gather(conv_weight, "dp", axis=1, tiled=True)
        conv_weight = lax.all_gather(conv_weight, "sub", axis=2, tiled=True)
        conv_weight = jnp.transpose(conv_weight, (1, 0, 2)).reshape(C, taps * H)
        point_weight = lax.all_gather(point_weight, "dp", axis=1, tiled=True)
        point_weight = lax.all_gather(point_weight, "sub", axis=0, tiled=True)
    k = Kernel(mesh, rows, C, H, packed)
    scratch = k.scratch()
    here = pl.BlockSpec(memory_space=pl.ANY)
    vmem = pl.BlockSpec(memory_space=pltpu.VMEM)
    shapes = [
        ((rows, C), BF),
        ((rows, C), BF),
        ((taps, cw, hw) if packed else (taps, C, H), F32),
        ((hw, cw) if packed else (H, C), F32),
        ((C,), F32),
        ((C,), F32),
        ((H,), F32),
        ((H,), F32),
        ((2, C), F32),
        ((2, H), F32),
    ]
    held = [packed or i not in (2, 3) for i in range(len(shapes))]
    outs = pl.pallas_call(
        functools.partial(kernel, k, 13, len(shapes), list(scratch)),
        out_shape=[
            pltpu.VMEM(*s) if in_vmem else jax.ShapeDtypeStruct(*s) for s, in_vmem in zip(shapes, held)
        ],
        in_specs=[here] * 13,
        out_specs=[vmem] * len(shapes),
        scratch_shapes=list(scratch.values()),
        compiler_params=pltpu.CompilerParams(
            collective_id=0, has_side_effects=True, vmem_limit_bytes=(55 if packed else 54) * 2**20
        ),
    )(
        activations,
        out_grad,
        species,
        first_start,
        species_weight,
        conv_weight,
        point_weight,
        gain_one,
        bias_one,
        gain_two,
        bias_two,
        running_one,
        running_two,
    )
    keep = [i for i in range(len(shapes)) if held[i]]
    n = len(keep)
    given = pl.pallas_call(
        functools.partial(hand_out, n, 2),
        out_shape=[jax.ShapeDtypeStruct(*shapes[i]) for i in keep],
        in_specs=[vmem] * n,
        out_specs=[here] * n,
        scratch_shapes=[pltpu.SemaphoreType.DMA((n,))],
        compiler_params=pltpu.CompilerParams(vmem_limit_bytes=2**20),
    )(*[pltpu.with_memory_space_constraint(outs[i], pltpu.VMEM) for i in keep])
    outs = list(outs)
    for i, v in zip(keep, given):
        outs[i] = v
    if not packed:
        conv_grad, point_grad = outs[2], outs[3]
        conv_grad = lax.psum_scatter(conv_grad, "dp", scatter_dimension=1, tiled=True)
        point_grad = lax.psum_scatter(point_grad, "dp", scatter_dimension=1, tiled=True)
        outs[2] = lax.psum_scatter(conv_grad, "sub", scatter_dimension=2, tiled=True)
        outs[3] = lax.psum_scatter(point_grad, "sub", scatter_dimension=0, tiled=True)
    return tuple(outs)


def solution(mesh):
    in_specs = (
        P(("dp", "sub"), None),
        P(("dp", "sub"), None),
        P(("dp", "sub")),
        P(("dp", "sub")),
        P(),
        P(None, "dp", "sub"),
        P("sub", "dp"),
        P(),
        P(),
        P(),
        P(),
        P(),
        P(),
    )
    out_specs = (
        P(("dp", "sub"), None),
        P(("dp", "sub"), None),
        P(None, "dp", "sub"),
        P("sub", "dp"),
        P(),
        P(),
        P(),
        P(),
        P(),
        P(),
    )
    return jax.shard_map(
        functools.partial(body, mesh), mesh=mesh, in_specs=in_specs, out_specs=out_specs, check_vma=False
    )
```

```python
import functools

import jax
import jax.numpy as jnp
from jax import lax
from jax.experimental import pallas as pl
from jax.experimental.pallas import tpu as pltpu
from jax.sharding import PartitionSpec as P

DIL = 11
SEQ_LEN = 1024
EPSILON = 0.001
MOMENTUM = 0.9
PAD = 16
HALF_SLOPE = 0.851
BF = jnp.bfloat16
F32 = jnp.float32
MESH = pl.DeviceIdType.MESH
PARTS = ((0, 48), (48, 48), (96, 48), (144, 48), (192, 32), (224, 80))
CONV_ROWS, SLOT_ROWS = 224, 304
SIDE = 112


def gelu_all(u):
    t = jnp.tanh(u)
    s = 0.5 * t + 0.5
    return (u * s) * (1.0 / HALF_SLOPE), s + u * (0.5 - 0.5 * t * t)


def colsum(v):
    return jnp.sum(v.reshape(v.shape[0] // 8, 8, v.shape[1]), axis=0)


def squash(v):
    return jnp.sum(v, axis=0, keepdims=True)


def loop(first, last, tile, f):
    def one(i, carry):
        f(pl.multiple_of(first + i * tile, tile))
        return carry

    lax.fori_loop(0, (last - first) // tile, one, 0)


def row_tile(start, tile):
    return start + lax.broadcasted_iota(jnp.int32, (tile, 128), 0)


def wide(m, n):
    return jnp.concatenate([m] * (n // 128), axis=1)


def lanes_of(rows):
    return lax.broadcasted_iota(jnp.int32, (rows, 128), 1)


def join(pieces):
    lane = lanes_of(pieces[0].shape[0])
    return [jnp.where(lane < 96 - 32 * i, pieces[i], pieces[i + 1]) for i in range(3)]


def split(tiles):
    lane = lanes_of(tiles[0].shape[0])
    return [
        tiles[0],
        jnp.where(lane >= 96, tiles[0], tiles[1]),
        jnp.where(lane >= 64, tiles[1], tiles[2]),
        tiles[2],
    ]


def free(i, lane):
    at = (96 * i + 96) % 128
    return (lane >= at) & (lane < at + 32)


def narrow(v, i):
    return pltpu.roll(v, 96 - 32 * i, 1)


def widen(blocks, i):
    lane = lanes_of(blocks[0].shape[0])
    moved = [pltpu.roll(b, 32 + 32 * j, 1) for j, b in enumerate(blocks)]
    inside = lambda j: (lane >= (96 * i + 32 * j) % 128) & (lane < (96 * i + 32 * j) % 128 + 32)
    return jnp.where(inside(0), moved[0], jnp.where(inside(1), moved[1], moved[2]))


class Kernel:
    def __init__(self, mesh, rows, channels, hidden, packed):
        self.ndp, self.nsub = mesh.shape["dp"], mesh.shape["sub"]
        self.rows, self.C, self.H = rows, channels, hidden
        self.packed = packed
        self.total = rows * self.ndp * self.nsub
        self.chips = self.ndp * self.nsub // 2
        self.nz = self.ndp // 2
        self.cw, self.hw = channels // self.ndp, hidden // self.nsub
        self.half = self.cw // 2
        self.sent, self.coming, self.local = [], {}, {}

    def scratch(self):
        R, C, H = self.rows, self.C, self.H
        V, D = pltpu.VMEM, pltpu.SemaphoreType.DMA
        s = dict(
            x=V((R, C), BF),
            og=V((R, C), BF),
            act=V((R, C), BF),
            slope=V((R, C), BF),
            big=V((R + 2 * PAD, 3 * H), F32),
            conv=V((R, H), F32),
            p2g=V((R, H), F32),
            act2=V((R, H), BF),
            back=V((R, 3 * H), BF),
            mb=V((R, 128), F32),
            ma=V((R, 128), F32),
            hs=V((2, PAD, H), F32),
            halo=V((2, PAD, H), F32),
            es=V((2, PAD, 2 * H + 128), F32),
            edge=V((2, PAD, 2 * H + 128), F32),
            acc1=V((2, 8, C), F32),
            acc2=V((2, 8, H), F32),
            c0=V((2, 2, C), F32),
            c1=V((2, 2, H), F32),
            c2=V((2, 2, H), F32),
            c3=V((2, 2, C), F32),
            s0=V((self.chips, 2, C), F32),
            s1=V((self.chips, 2, H), F32),
            s2=V((self.chips, 2, H), F32),
            s3=V((self.chips, 2, C), F32),
            wf=V((C, 3 * H), BF),
            pf=V((H, C), BF),
            sw=V((2, C), F32),
            g1=V((C,), F32),
            b1=V((C,), F32),
            g2=V((H,), F32),
            b2=V((H,), F32),
            run1=V((2, C), F32),
            run2=V((2, H), F32),
            species=pltpu.SMEM((R,), jnp.int32),
            first=pltpu.SMEM((1,), jnp.int32),
            ar_send=D((4, 2)),
            ar_recv=D((4, 2)),
            insem=D((24,)),
            halo_send=D((2, 2)),
            halo_recv=D((2, 2)),
        )
        if self.packed:
            nz = self.nz
            s.update(
                cshard=V((3, self.cw, self.hw), BF),
                pshard=V((self.hw, self.cw), BF),
                ag_send=D((len(PARTS), 3)),
                ag_z=D((len(PARTS),)),
                ag_own=D((len(PARTS), 2)),
                ag_oth=D((len(PARTS), 2)),
                ag_d=D((len(PARTS),)),
                ag_core=D((len(PARTS), 4)),
                ra=V((nz, 2, 2, 2, SIDE, 128), F32),
                rs=V((nz, 2, 2, 2, SIDE, 128), BF),
                rc=V((nz, 2, 2, 2, SIDE, 128), BF),
                st=V((nz, 2, 2, 2, SIDE, 128), BF),
                rd=V((nz, 2, SIDE, 128), BF),
                rxy=V((nz, 2, 2, SIDE, 128), BF),
                rz=V((2, 3, SIDE, 128), BF),
                rs_send=D((nz, 2, 3)),
                rs_core=D((nz, 2)),
                rs_d=D((nz, 2)),
                rs_xy=D((nz, 2, 2)),
                rz_send=D((2,)),
                rs_z=D((2,)),
                pa=V((2, 2, nz, 80, 128), F32),
                ps=V((2, 2, nz, 80, 128), BF),
                pc=V((2, 2, nz, 80, 128), BF),
                pt=V((2, 2, nz, 80, 128), BF),
                pd=V((nz, 80, 128), BF),
                pxy=V((2, nz, 80, 128), BF),
                pz=V((3, 80, 128), BF),
                p_send=D((4,)),
                p_recv=D((5,)),
            )
            s.update({f"w{j}": V((2, 2, 2, nz, n, 128), BF) for j, (_, n) in enumerate(PARTS)})
        return s

    def place(self):
        self.dp, self.sub = lax.axis_index("dp"), lax.axis_index("sub")
        self.z, self.y = self.dp // 2, lax.rem(self.dp, 2)
        self.x, self.c = self.sub // 2, lax.rem(self.sub, 2)
        n = self.ndp * self.nsub
        me = self.dp * self.nsub + self.sub
        nxt, prv = lax.rem(me + 1, n), lax.rem(me + n - 1, n)
        far = lax.rem(me + jnp.where(self.c == 1, 1, n - 1), n)
        self.core_nbr = (self.dp, self.x * 2 + 1 - self.c)
        self.x_nbr = (self.dp, (1 - self.x) * 2 + self.c)
        self.y_nbr = (self.z * 2 + 1 - self.y, self.sub)
        self.next = (nxt // self.nsub, lax.rem(nxt, self.nsub))
        self.prev = (prv // self.nsub, lax.rem(prv, self.nsub))
        self.far = (far // self.nsub, lax.rem(far, self.nsub))
        self.chip = self.dp * (self.nsub // 2) + self.x

    def z_device(self, d):
        return (lax.rem(self.z + d, self.nz) * 2 + self.y, self.sub)

    def each_chip(self, f):
        if self.chips == 16 and self.nsub == 4:
            z, y, x = self.z, self.y, self.x
            zs = (z, z + 1 - 2 * lax.rem(z, 2), lax.rem(z + 2, 4), 3 - z)
            for d in range(15, 0, -1):
                yy = 1 - y if (d // 2) % 2 else y
                xx = 1 - x if d % 2 else x
                f((zs[d // 4] * 2 + yy, xx * 2 + self.c))
        else:
            side = self.nsub // 2

            def one(d, carry):
                chip = lax.rem(self.chip + d, self.chips)
                f((chip // side, lax.rem(chip, side) * 2 + self.c))
                return carry

            lax.fori_loop(1, self.chips, one, 0)

    def greet(self):
        b = pltpu.get_barrier_semaphore()

        def hello(device):
            pl.semaphore_signal(b, inc=1, device_id=device, device_id_type=MESH)

        self.each_chip(hello)
        hello(self.far)
        hello(self.core_nbr)

    def greeted(self):
        pl.semaphore_wait(pltpu.get_barrier_semaphore(), self.chips + 1)

    def put(self, src, dst, send, recv, device, key=None, ref=None):
        pltpu.make_async_remote_copy(
            src, dst, send, recv, device_id=device, device_id_type=MESH
        ).start()
        self.sent.append((src, send))
        if key is not None:
            self.coming[key] = (dst if ref is None else ref, recv)

    def arrived(self, *keys):
        for key in keys:
            ref, sem = self.coming.pop(key)
            pltpu.make_async_copy(ref, ref, sem).wait()

    def fetch(self, key, src, dst, sem):
        self.local[key] = cp = pltpu.make_async_copy(src, dst, sem)
        cp.start()

    def have(self, *keys):
        for key in keys:
            self.local.pop(key).wait()

    def drain(self):
        self.have(*list(self.local))
        self.arrived(*list(self.coming))
        for ref, sem in self.sent:
            pltpu.make_async_copy(ref, ref, sem).wait()


    def ar_begin(self, r, i, top, low):
        cs = getattr(r, f"c{i}")
        cs[self.c, 0:1, :] = top
        cs[self.c, 1:2, :] = low
        mine = cs.at[self.c]
        self.put(mine, mine, r.ar_send.at[i, 0], r.ar_recv.at[i, 0], self.core_nbr, ("c", i))

    def ar_middle(self, r, i):
        cs, sl = getattr(r, f"c{i}"), getattr(r, f"s{i}")
        self.arrived(("c", i))
        sl[self.chip] = cs[0] + cs[1]
        mine = sl.at[self.chip]
        most = sl.at[pl.ds(0, self.chips - 1)]
        send, recv = r.ar_send.at[i, 1], r.ar_recv.at[i, 1]

        def one(device):
            pltpu.make_async_remote_copy(
                mine, mine, send, recv, device_id=device, device_id_type=MESH
            ).start()

        self.each_chip(one)
        self.sent.append((most, send))
        self.coming["s", i] = (most, recv)

    def ar_end(self, r, i):
        sl = getattr(r, f"s{i}")
        self.arrived(("s", i))
        if self.chips <= 16:
            total = sl[0]
            for k in range(1, self.chips):
                total = total + sl[k]
        else:
            total = lax.fori_loop(1, self.chips, lambda k, t: t + sl[k], sl[0])
        return total[0:1, :], total[1:2, :]

    def group(self, ref, flip_y=False, flip_x=False):
        y = 1 - self.y if flip_y else self.y
        x = 1 - self.x if flip_x else self.x
        return ref.at[y, x, self.c]

    def ag_pack(self, r):
        lane = lanes_of(96)
        full = lambda v: jnp.concatenate([v.astype(F32), jnp.zeros((96, 32), F32)], axis=1)
        place = lambda v, i: pltpu.roll(v, lax.rem(96 * i, 128), 1).astype(BF)
        here = (self.y, self.x, self.c, 0)
        t2, p = full(r.cshard[2]), full(r.pshard[...])
        rest = jnp.concatenate([narrow(t2, i)[32:96] for i in range(3)], axis=0)
        for j in range(2):
            v = place(jnp.where(lane < 96, full(r.cshard[j]), rest[96 * j : 96 * j + 96]), self.sub)
            for h in range(2):
                (r.w0, r.w1, r.w2, r.w3)[2 * j + h][here] = v[48 * h : 48 * h + 48]
        r.w4[here] = place(t2[0:32], self.sub)
        rest = jnp.concatenate([narrow(p[80:96], i) for i in range(3)] + [jnp.zeros((32, 128), F32)], axis=0)
        r.w5[here] = place(jnp.where(lane[0:80] < 96, p[0:80], rest), self.dp)

    def ag_start(self, r, j):
        grp = self.group(getattr(r, f"w{j}"))
        slot, some = grp.at[0], grp.at[pl.ds(1, self.nz - 1)]
        for d in range(1, self.nz):
            pltpu.make_async_remote_copy(
                slot, grp.at[self.nz - d], r.ag_send.at[j, 0], r.ag_z.at[j],
                device_id=self.z_device(d), device_id_type=MESH,
            ).start()
        self.sent.append((some, r.ag_send.at[j, 0]))
        self.coming["z", j] = (some, r.ag_z.at[j])
        self.put(slot, slot, r.ag_send.at[j, 1], r.ag_own.at[j, 0], self.y_nbr, ("yo", j))
        self.put(slot, slot, r.ag_send.at[j, 1], r.ag_own.at[j, 1], self.x_nbr, ("xo", j))

    def to_core(self, r, j, i, grp):
        self.put(grp, grp, r.ag_send.at[j, 2], r.ag_core.at[j, i], self.core_nbr, ("core", j, i))

    def ag_plane(self, r, j):
        self.arrived(("z", j))
        grp = self.group(getattr(r, f"w{j}"))
        some = grp.at[pl.ds(1, self.nz - 1)]
        self.put(some, some, r.ag_send.at[j, 1], r.ag_oth.at[j, 0], self.y_nbr, ("yr", j))
        self.put(some, some, r.ag_send.at[j, 1], r.ag_oth.at[j, 1], self.x_nbr, ("xr", j))
        self.to_core(r, j, 0, grp)

    def ag_diagonal(self, r, j):
        g = getattr(r, f"w{j}")
        by_y, by_x = self.group(g, flip_y=True), self.group(g, flip_x=True)
        h = j % 2
        first, second = (by_y, by_x) if h == 0 else (by_x, by_y)
        self.arrived(("yx"[h] + "o", j), ("yx"[h] + "r", j))
        self.put(
            first, first, r.ag_send.at[j, 1], r.ag_d.at[j], (self.x_nbr, self.y_nbr)[h], ("d", j)
        )
        self.to_core(r, j, 1, first)
        self.arrived(("xy"[h] + "o", j), ("xy"[h] + "r", j))
        self.to_core(r, j, 2, second)

    def ag_last(self, r, j):
        self.arrived(("d", j))
        self.to_core(r, j, 3, self.group(getattr(r, f"w{j}"), True, True))

    def each_slot(self):
        for z in range(self.nz):
            at = lax.rem(z - self.z + self.nz, self.nz)
            for y in range(2):
                yield z, y, at

    def ag_unpack(self, r, k):
        H, cw, hw = self.H, self.cw, self.hw
        for j in ((0, 1), (2, 3), (4,), (5,))[k]:
            self.arrived(*[("core", j, i) for i in range(4)])

        def slot(j, y, s, at):
            return getattr(r, f"w{j}").at[y, s // 2, s % 2, at]

        def keep(ref, row, lane, tiles):
            for i, t in enumerate(tiles):
                ref[row : row + t.shape[0], lane + 128 * i : lane + 128 * i + 128] = t.astype(BF)

        if k < 3:
            for z, y, at in self.each_slot():
                low = (z * 2 + y) * cw
                if k < 2:
                    for h in range(2):
                        tiles = join([slot(2 * k + h, y, s, at)[...].astype(F32) for s in range(4)])
                        keep(r.wf, low + 48 * h, k * H, tiles)
                else:
                    keep(r.wf, low, 2 * H, join([slot(4, y, s, at)[...].astype(F32) for s in range(4)]))
                    pieces = []
                    for s in range(4):
                        parts = [slot(j, y, s, at) for j in range(4)]
                        cut = lambda j, a, b: parts[j][a:b, :].astype(F32)
                        pieces.append(widen((
                            jnp.concatenate([cut(0, 0, 48), cut(1, 0, 16)], axis=0),
                            jnp.concatenate([cut(1, 16, 48), cut(2, 0, 32)], axis=0),
                            jnp.concatenate([cut(2, 32, 48), cut(3, 0, 48)], axis=0),
                        ), s))
                    keep(r.wf, low + 32, 2 * H, join(pieces))
        else:
            ats = {z: at for z, _, at in self.each_slot()}
            for s in range(4):
                for q in range(2):
                    got = [slot(5, dp % 2, s, ats[dp // 2])[...].astype(F32) for dp in range(4 * q, 4 * q + 4)]
                    keep(r.pf, s * hw, 4 * q * cw, join([v[0:80] for v in got]))
                    rest = [widen([v[16 * i : 16 * i + 16] for i in range(3)], dp) for dp, v in enumerate(got)]
                    keep(r.pf, s * hw + 80, 4 * q * cw, join(rest))

    def rs_pack(self, r, cg, m, first):
        H, cw = self.H, self.cw
        mine = self.c == 0
        lane = lanes_of(96)
        for y in range(2):
            low = first + y * cw
            taps = [
                split([cg[low : low + cw, t * H + 128 * i : t * H + 128 * i + 128] for i in range(3)])
                for t in range(3)
            ]
            for x in range(2):
                both = []
                for s in (2 * x, 2 * x + 1):
                    t2 = taps[2][s]
                    rest = jnp.concatenate([narrow(t2[32:96], i) for i in range(3)], axis=0)
                    gap = free(s, lane)
                    both.append((
                        jnp.where(gap, rest[0:96], taps[0][s]),
                        jnp.where(gap, rest[96:192], taps[1][s]),
                        t2[0:32],
                    ))
                own = [jnp.where(mine, p, q) for p, q in zip(*both)]
                other = [jnp.where(mine, q, p).astype(BF) for p, q in zip(*both)]
                for ref, v in ((r.ra, own), (r.rs, other)):
                    ref[m, 0, y, x, 0:96, :] = v[0]
                    ref[m, 0, y, x, 96:112, :] = v[1][0:16]
                    ref[m, 1, y, x, 0:80, :] = v[1][16:96]
                    ref[m, 1, y, x, 80:112, :] = v[2]

    def rs_core(self, r, m):
        for h in range(2):
            self.put(r.rs.at[m, h], r.rc.at[m, h], r.rs_send.at[m, h, 0], r.rs_core.at[m, h], self.core_nbr, ("rc", m, h))

    def rs_diagonal(self, r, m, h):
        self.arrived(("rc", m, h))
        for y in range(2):
            for x in range(2):
                r.ra[m, h, y, x] += r.rc[m, h, y, x].astype(F32)
        y, x = 1 - self.y, 1 - self.x
        r.st[m, h, y, x] = r.ra[m, h, y, x].astype(BF)
        self.put(
            r.st.at[m, h, y, x], r.rd.at[m, h], r.rs_send.at[m, h, 1], r.rs_d.at[m, h],
            (self.x_nbr, self.y_nbr)[h], ("rd", m, h),
        )

    def rs_plane(self, r, m, h):
        self.arrived(("rd", m, h))
        via_y, via_x = (1 - self.y, self.x), (self.y, 1 - self.x)
        y, x = (via_y, via_x)[h]
        r.ra[m, h, y, x] += r.rd[m, h].astype(F32)
        for i, ((y, x), to) in enumerate(((via_y, self.y_nbr), (via_x, self.x_nbr))):
            r.st[m, h, y, x] = r.ra[m, h, y, x].astype(BF)
            self.put(r.st.at[m, h, y, x], r.rxy.at[m, h, i], r.rs_send.at[m, h, 2], r.rs_xy.at[m, h, i], to, ("rp", m, h, i))

    def rs_column(self, r, m, h):
        y, x = self.y, self.x
        self.arrived(("rp", m, h, 0), ("rp", m, h, 1))
        r.ra[m, h, y, x] += r.rxy[m, h, 0].astype(F32) + r.rxy[m, h, 1].astype(F32)
        r.st[m, h, y, x] = r.ra[m, h, y, x].astype(BF)
        d = lax.rem(self.z - m + self.nz, self.nz)

        @pl.when(d != 0)
        def _():
            pltpu.make_async_remote_copy(
                r.st.at[m, h, y, x], r.rz.at[h, d - 1], r.rz_send.at[h], r.rs_z.at[h],
                device_id=(m * 2 + self.y, self.sub), device_id_type=MESH,
            ).start()

        if m == self.nz - 1:
            self.sent.append((r.rz.at[h], r.rz_send.at[h]))
            self.coming["rz", h] = (r.rz.at[h], r.rs_z.at[h])

    def rs_end(self, r):
        v = []
        for h in range(2):
            self.arrived(("rz", h))
            t = r.ra[self.z, h, self.y, self.x]
            for i in range(3):
                t = t + r.rz[h, i].astype(F32)
            v.append(t)
        v = pltpu.roll(jnp.concatenate(v, axis=0), lax.rem(128 - lax.rem(96 * self.sub, 128), 128), 1)
        r.conv_grad[0] = v[0:96, 0:96]
        r.conv_grad[1] = v[96:192, 0:96]
        r.conv_grad[2, 0:32, :] = v[192:224, 0:96]
        r.conv_grad[2, 32:96, :] = widen([v[64 * i : 64 * i + 64] for i in range(3)], 0)[:, 0:96]

    def pg_pack(self, r, pg):
        cw, hw = self.cw, self.hw
        mine = self.c == 0
        lane = lanes_of(80)
        pieces = []
        for s in range(4):
            rows = slice(s * hw, s * hw + hw)
            pieces.append([
                p
                for q in range(2)
                for p in split([pg[rows, 4 * q * cw + 128 * i : 4 * q * cw + 128 * i + 128] for i in range(3)])
            ])
        for dp in range(self.ndp):
            for x in range(2):
                both = []
                for s in (2 * x, 2 * x + 1):
                    p = pieces[s][dp]
                    rest = jnp.concatenate([narrow(p[80:96], i) for i in range(3)] + [p[0:32]], axis=0)
                    both.append(jnp.where(free(dp, lane), rest, p[0:80]))
                r.pa[dp % 2, x, dp // 2] = jnp.where(mine, both[0], both[1])
                r.ps[dp % 2, x, dp // 2] = jnp.where(mine, both[1], both[0]).astype(BF)

    def pg_core(self, r):
        self.put(r.ps, r.pc, r.p_send.at[0], r.p_recv.at[0], self.core_nbr, "pc")

    def pg_diagonal(self, r):
        self.arrived("pc")
        for y in range(2):
            for x in range(2):
                r.pa[y, x] += r.pc[y, x].astype(F32)
        y, x = 1 - self.y, 1 - self.x
        r.pt[y, x] = r.pa[y, x].astype(BF)
        self.put(r.pt.at[y, x], r.pd, r.p_send.at[1], r.p_recv.at[1], self.x_nbr, "pd")

    def pg_plane(self, r):
        self.arrived("pd")
        via_y, via_x = (1 - self.y, self.x), (self.y, 1 - self.x)
        r.pa[via_y[0], via_y[1]] += r.pd[...].astype(F32)
        for i, ((y, x), to) in enumerate(((via_y, self.y_nbr), (via_x, self.x_nbr))):
            r.pt[y, x] = r.pa[y, x].astype(BF)
            self.put(r.pt.at[y, x], r.pxy.at[i], r.p_send.at[2], r.p_recv.at[2 + i], to, ("pp", i))

    def pg_column(self, r):
        y, x = self.y, self.x
        self.arrived(("pp", 0), ("pp", 1))
        r.pa[y, x] += r.pxy[0].astype(F32) + r.pxy[1].astype(F32)
        r.pt[y, x] = r.pa[y, x].astype(BF)
        for d in range(1, self.nz):
            to = lax.rem(self.z + d, self.nz)
            pltpu.make_async_remote_copy(
                r.pt.at[y, x, to], r.pz.at[self.nz - d - 1], r.p_send.at[3], r.p_recv.at[4],
                device_id=self.z_device(d), device_id_type=MESH,
            ).start()
        self.sent.append((r.pz, r.p_send.at[3]))
        self.coming["pz"] = (r.pz, r.p_recv.at[4])

    def pg_end(self, r):
        self.arrived("pz")
        v = r.pa[self.y, self.x, self.z]
        for i in range(3):
            v = v + r.pz[i].astype(F32)
        v = pltpu.roll(v, lax.rem(128 - lax.rem(96 * self.dp, 128), 128), 1)
        r.point_grad[0:80, :] = v[:, 0:96]
        r.point_grad[80:96, :] = widen([v[16 * i : 16 * i + 16] for i in range(3)], 0)[:, 0:96]

    def halo_up(self, r):
        R, H = self.rows, self.H
        r.hs[1] = r.big[R : R + PAD, 0:H] * wide(r.ma[R - PAD : R], H)
        self.put(r.hs.at[1], r.halo.at[1], r.halo_send.at[0, 1], r.halo_recv.at[0, 1], self.next, ("h", 1))

    def halo_down(self, r):
        H = self.H
        r.hs[0] = r.big[PAD : 2 * PAD, 2 * H : 3 * H] * wide(r.mb[0:PAD], H)
        self.put(r.hs.at[0], r.halo.at[0], r.halo_send.at[0, 0], r.halo_recv.at[0, 0], self.prev, ("h", 0))

    def halo_end(self, r):
        R, H = self.rows, self.H
        self.arrived(("h", 0), ("h", 1))
        r.big[R + PAD : R + 2 * PAD, 2 * H : 3 * H] = r.halo[0]
        r.big[0:PAD, 0:H] = r.halo[1]

    def edges_begin(self, r):
        R, H = self.rows, self.H
        for j, (at, m, to) in enumerate(((0, r.mb, self.prev), (R - PAD, r.ma, self.next))):
            mask = m[at : at + PAD]
            r.es[j, :, 0:H] = r.p2g[at : at + PAD, :] * wide(mask, H)
            r.es[j, :, H : 2 * H] = r.conv[at : at + PAD, :] * wide(mask, H)
            r.es[j, :, 2 * H :] = mask
            self.put(r.es.at[j], r.edge.at[j], r.halo_send.at[1, j], r.halo_recv.at[1, j], to, ("e", j))

    def edges_end(self, r, a2, lin2, off2):
        R, H = self.rows, self.H
        self.arrived(("e", 0), ("e", 1))
        for j, at in ((0, R + PAD), (1, 0)):
            r.big[at : at + PAD, 0:H] = (
                r.edge[j, :, 0:H] * a2 + r.edge[j, :, H : 2 * H] * lin2 + wide(r.edge[j, :, 2 * H :], H) * off2
            )


class Refs:
    pass


def kernel(k, n_in, n_out, names, *refs):
    r = Refs()
    for name, ref in zip(names, refs[n_in + n_out :]):
        setattr(r, name, ref)
    k.sent, k.coming, k.local = [], {}, {}
    k.place()
    work(k, r, refs[:n_in], refs[n_in : n_in + n_out])
    k.drain()


def work(k, r, ins, outs):
    (x_hbm, og_hbm, species, first, sw, conv_w, point_w, g1, b1, g2, b2, run1, run2) = ins
    (out, ig, r.conv_grad, r.point_grad, gg1, gb1, gg2, gb2, new1, new2) = outs
    R, C, H, N = k.rows, k.C, k.H, k.total
    Q = R // 4
    r.bg = ig
    k.greet()
    if k.packed:
        k.fetch("cw", conv_w, r.cshard, r.insem.at[5])
        k.fetch("pw", point_w, r.pshard, r.insem.at[6])
    for q in range(4):
        rows = pl.ds(q * Q, Q)
        k.fetch(("x", q), x_hbm.at[rows], r.x.at[rows], r.insem.at[q])
    small = dict(first=first, g1=g1, b1=b1, g2=g2, b2=b2, sw=sw, run1=run1, run2=run2, species=species)
    for i, (name, ref) in enumerate(small.items()):
        k.fetch(name, ref, getattr(r, name), r.insem.at[7 + i])
    k.fetch("og", og_hbm, r.og, r.insem.at[4])
    if not k.packed:
        k.fetch("cw", conv_w, r.wf, r.insem.at[5])
        k.fetch("pw", point_w, r.pf, r.insem.at[6])
    else:
        k.have("cw", "pw")
        k.ag_pack(r)

    def sums(q):
        k.have(("x", q))
        v = r.x[q * Q : q * Q + Q, :].astype(F32)
        r.acc1[0] += colsum(v)
        r.acc1[1] += colsum(v * v)

    r.acc1[...] = jnp.zeros_like(r.acc1)
    k.greeted()
    if k.packed:
        for j in range(5):
            k.ag_start(r, j)
    for q in range(4):
        sums(q)
    k.ar_begin(r, 0, squash(r.acc1[0]), squash(r.acc1[1]))

    k.have("first")
    fs = r.first[0]
    starts = [fs + SEQ_LEN * j for j in range(R // SEQ_LEN)]
    k.ar_middle(r, 0)
    def masks(at):
        row = row_tile(at, 128)
        before = jnp.ones((128, 128), F32)
        after = jnp.ones((128, 128), F32)
        for s in starts:
            before = jnp.where((row >= s) & (row < s + DIL), 0.0, before)
            after = jnp.where((row >= s - DIL) & (row < s), 0.0, after)
        r.mb[pl.ds(at, 128), :] = before
        r.ma[pl.ds(at, 128), :] = after

    loop(0, R, 128, masks)
    if k.packed:
        for j in range(5):
            k.ag_plane(r, j)
        k.ag_start(r, 5)
    k.have("g1", "b1")
    sum1, sq1 = k.ar_end(r, 0)
    mean1 = sum1 / N
    var1 = sq1 / N - mean1 * mean1
    inv1 = lax.rsqrt(var1 + EPSILON)
    gain1 = r.g1[...].reshape(1, C)
    scale1 = (HALF_SLOPE * gain1) * inv1
    shift1 = HALF_SLOPE * r.b1[...].reshape(1, C) - mean1 * scale1

    def act_tile(at):
        rows = pl.ds(at, 256)
        u = r.x[rows, :].astype(F32) * scale1 + shift1
        a, s = gelu_all(u)
        r.act[rows, :] = a.astype(BF)
        r.slope[rows, :] = s.astype(BF)

    steps = (
        lambda: (k.ag_diagonal(r, 0), k.ag_diagonal(r, 1)),
        lambda: (k.ag_diagonal(r, 2), k.ag_diagonal(r, 3)),
        lambda: (k.ag_diagonal(r, 4), k.ag_plane(r, 5)),
        lambda: (k.ag_last(r, 0), k.ag_last(r, 1)),
    )
    for q in range(4):
        loop(q * Q, q * Q + Q, 256, act_tile)
        if k.packed:
            steps[q]()
    if k.packed:
        k.ag_last(r, 2)
        k.ag_last(r, 3)
        k.ag_unpack(r, 0)
        k.ag_last(r, 4)
        k.ag_unpack(r, 1)
    else:
        k.have("cw", "pw")

    def product(at, rows, lanes):
        r.big[PAD + at : PAD + at + rows, lanes] = jnp.dot(
            r.act[at : at + rows, :], r.wf[:, lanes], preferred_element_type=F32
        )

    product(0, R // 2, slice(0, 2 * H))
    product(R // 2, R // 2, slice(0, 2 * H))
    if k.packed:
        k.ag_unpack(r, 2)
    k.halo_up(r)
    product(0, R // 2, slice(2 * H, 3 * H))
    k.halo_down(r)
    product(R // 2, R // 2, slice(2 * H, 3 * H))
    if k.packed:
        k.ag_diagonal(r, 5)
    r.acc2[...] = jnp.zeros_like(r.acc2)
    T = 256

    def gather_taps(at):
        rows = pl.ds(at, T)
        lo = r.big[pl.ds(at, T + 2 * PAD), 0:H][PAD - DIL : PAD - DIL + T]
        mid = r.big[pl.ds(at + PAD, T), H : 2 * H]
        hi = r.big[pl.ds(at, T + 2 * PAD), 2 * H : 3 * H][PAD + DIL : PAD + DIL + T]
        v = lo * wide(r.mb[rows, :], H) + mid + hi * wide(r.ma[rows, :], H)
        r.conv[rows, :] = v
        r.acc2[0] += colsum(v)
        r.acc2[1] += colsum(v * v)

    loop(T, R - T, T, gather_taps)
    k.halo_end(r)
    gather_taps(0)
    gather_taps(R - T)
    k.ar_begin(r, 1, squash(r.acc2[0]), squash(r.acc2[1]))
    k.ar_middle(r, 1)
    if k.packed:
        k.ag_last(r, 5)

    k.have("og", "sw", "species", "g2", "b2", "run1", "run2")
    at_start = [r.species[0]] + [r.species[s] for s in starts]
    weights = [jnp.where(sp == 0, r.sw[0:1, :], r.sw[1:2, :]) for sp in at_start]

    def row_weight(at, tile):
        row = row_tile(at, tile)
        w = jnp.broadcast_to(weights[0], (tile, C))
        for s, v in zip(starts, weights[1:]):
            w = jnp.where(wide(row, C) >= s, v, w)
        return w

    def branch_grad(at):
        rows = pl.ds(at, 128)
        r.bg[rows, :] = (r.og[rows, :].astype(F32) * row_weight(at, 128)).astype(BF)

    loop(0, R, 128, branch_grad)
    if k.packed:
        k.ag_unpack(r, 3)

    def act_two_grad(at):
        rows = pl.ds(at, 1024)
        r.p2g[rows, :] = lax.dot_general(
            r.bg[rows, :], r.pf[...], (((1,), (1,)), ((), ())), preferred_element_type=F32
        )

    loop(0, R, 1024, act_two_grad)
    sum2, sq2 = k.ar_end(r, 1)
    mean2 = sum2 / N
    var2 = sq2 / N - mean2 * mean2
    inv2 = lax.rsqrt(var2 + EPSILON)
    minv2 = mean2 * inv2
    gain2 = r.g2[...].reshape(1, H)
    gain2h, bias2h = HALF_SLOPE * gain2, HALF_SLOPE * r.b2[...].reshape(1, H)
    r.acc2[...] = jnp.zeros_like(r.acc2)

    def second_norm(at):
        rows = pl.ds(at, 256)
        zh = r.conv[rows, :] * inv2 - minv2
        a, s = gelu_all(zh * gain2h + bias2h)
        r.act2[rows, :] = a.astype(BF)
        p = r.p2g[rows, :] * s
        r.p2g[rows, :] = p
        r.acc2[0] += colsum(p)
        r.acc2[1] += colsum(p * zh)

    loop(0, R, 256, second_norm)
    k.ar_begin(r, 2, squash(r.acc2[0]), squash(r.acc2[1]))
    k.edges_begin(r)
    k.ar_middle(r, 2)

    def block_output():
        for q in range(2):
            rows = pl.ds(q * 1024, 1024)
            br = jnp.dot(r.act2[rows, :], r.pf[...], preferred_element_type=F32)
            out[rows, :] = (r.x[rows, :].astype(F32) + br).astype(BF)

    pg = lax.dot_general(
        r.act2[...], r.bg[...], (((0,), (0,)), ((), ())), preferred_element_type=F32
    )
    if k.packed:
        k.pg_pack(r, pg)
        k.pg_core(r)
    else:
        r.point_grad[...] = pg
    bsum, gsum = k.ar_end(r, 2)
    gb2[...] = bsum.reshape(H)
    gg2[...] = gsum.reshape(H)
    a2 = inv2 * gain2
    lin2 = -a2 * (gsum / N) * inv2
    off2 = -a2 * (bsum / N) + a2 * (gsum / N) * minv2

    def cot(at):
        rows = pl.ds(at, 256)
        r.big[pl.ds(at + PAD, 256), 0:H] = (
            r.p2g[rows, :] * a2 + r.conv[rows, :] * lin2 + off2
        )

    loop(0, R, 256, cot)
    if k.packed:
        k.pg_diagonal(r)
    k.edges_end(r, a2, lin2, off2)
    T2 = 128

    def shifted(at):
        rows = pl.ds(at, T2)
        v = r.big[pl.ds(at, T2 + 2 * PAD), 0:H]
        r.back[rows, 0:H] = (v[PAD + DIL : PAD + DIL + T2] * wide(r.ma[rows, :], H)).astype(BF)
        r.back[rows, H : 2 * H] = v[PAD : PAD + T2].astype(BF)
        r.back[rows, 2 * H : 3 * H] = (v[PAD - DIL : PAD - DIL + T2] * wide(r.mb[rows, :], H)).astype(BF)

    loop(0, R, T2, shifted)

    M = C // 2
    for i, m in enumerate(range(0, C, M)):
        cg = lax.dot_general(
            r.act[:, m : m + M], r.back[...], (((0,), (0,)), ((), ())), preferred_element_type=F32
        )
        if k.packed:
            for z in range(2):
                k.rs_pack(r, cg, 2 * i + z, z * (M // 2))
                k.rs_core(r, 2 * i + z)
            if i == 0:
                k.pg_plane(r)
        else:
            for j in range(3):
                r.conv_grad[j, m : m + M, :] = cg[:, j * H : j * H + H]

    minv1 = mean1 * inv1
    r.acc1[...] = jnp.zeros_like(r.acc1)
    both = lambda f, *ms: [f(r, m, h) for m in ms for h in range(2)]
    steps = (
        lambda: both(k.rs_diagonal, 2, 3),
        lambda: both(k.rs_plane, 0),
        lambda: (both(k.rs_plane, 1, 2), k.pg_column(r)),
        lambda: both(k.rs_plane, 3),
    )
    if k.packed:
        both(k.rs_diagonal, 0, 1)
    for q in range(4):
        rows = slice(q * Q, q * Q + Q)
        ag = lax.dot_general(
            r.back[rows, :], r.wf[...], (((1,), (1,)), ((), ())), preferred_element_type=F32
        )
        p = ag * r.slope[rows, :].astype(F32)
        r.big[rows, 0:C] = p
        r.acc1[0] += colsum(p)
        r.acc1[1] += colsum(p * (r.x[rows, :].astype(F32) * inv1 - minv1))
        if k.packed:
            steps[q]()
    k.ar_begin(r, 3, squash(r.acc1[0]), squash(r.acc1[1]))
    k.ar_middle(r, 3)
    if k.packed:
        both(k.rs_column, 0, 1)
    block_output()
    if k.packed:
        both(k.rs_column, 2)
    unbias = N / (N - 1.0)
    new1[0:1, :] = MOMENTUM * r.run1[0:1, :] + (1.0 - MOMENTUM) * mean1
    new1[1:2, :] = MOMENTUM * r.run1[1:2, :] + (1.0 - MOMENTUM) * (var1 * unbias)
    new2[0:1, :] = MOMENTUM * r.run2[0:1, :] + (1.0 - MOMENTUM) * mean2
    new2[1:2, :] = MOMENTUM * r.run2[1:2, :] + (1.0 - MOMENTUM) * (var2 * unbias)
    bsum1, gsum1 = k.ar_end(r, 3)
    gb1[...] = bsum1.reshape(C)
    gg1[...] = gsum1.reshape(C)
    a1 = inv1 * gain1
    lin1 = -a1 * (gsum1 / N) * inv1
    off1 = -a1 * (bsum1 / N) + a1 * (gsum1 / N) * minv1

    def last(at):
        rows = pl.ds(at, 128)
        v = r.og[rows, :].astype(F32) * row_weight(at, 128)
        v = v + r.big[rows, 0:C] * a1 + r.x[rows, :].astype(F32) * lin1 + off1
        ig[rows, :] = v.astype(BF)

    if k.packed:
        both(k.rs_column, 3)
    loop(0, R, 128, last)
    if k.packed:
        k.pg_end(r)
        k.rs_end(r)


def hand_out(n, large, *refs):
    ins, outs, sems = refs[:n], refs[n : 2 * n], refs[2 * n]
    copies = [pltpu.make_async_copy(ins[i], outs[i], sems.at[i]) for i in range(n)]
    for cp in copies:
        cp.start()
    for cp in copies:
        cp.wait()


def body(
    mesh,
    activations,
    out_grad,
    species,
    first_start,
    species_weight,
    conv_weight,
    point_weight,
    gain_one,
    bias_one,
    gain_two,
    bias_two,
    running_one,
    running_two,
):
    rows, C = activations.shape
    ndp, nsub = mesh.shape["dp"], mesh.shape["sub"]
    cw, hw = conv_weight.shape[1:]
    taps, H = conv_weight.shape[0], hw * nsub
    packed = cw == 96 and hw == 96 and nsub == 4 and ndp % 2 == 0
    if not packed:
        conv_weight = lax.all_gather(conv_weight, "dp", axis=1, tiled=True)
        conv_weight = lax.all_gather(conv_weight, "sub", axis=2, tiled=True)
        conv_weight = jnp.transpose(conv_weight, (1, 0, 2)).reshape(C, taps * H)
        point_weight = lax.all_gather(point_weight, "dp", axis=1, tiled=True)
        point_weight = lax.all_gather(point_weight, "sub", axis=0, tiled=True)
    k = Kernel(mesh, rows, C, H, packed)
    scratch = k.scratch()
    here = pl.BlockSpec(memory_space=pl.ANY)
    vmem = pl.BlockSpec(memory_space=pltpu.VMEM)
    shapes = [
        ((rows, C), BF),
        ((rows, C), BF),
        ((taps, cw, hw) if packed else (taps, C, H), F32),
        ((hw, cw) if packed else (H, C), F32),
        ((C,), F32),
        ((C,), F32),
        ((H,), F32),
        ((H,), F32),
        ((2, C), F32),
        ((2, H), F32),
    ]
    held = [packed or i not in (2, 3) for i in range(len(shapes))]
    outs = pl.pallas_call(
        functools.partial(kernel, k, 13, len(shapes), list(scratch)),
        out_shape=[
            pltpu.VMEM(*s) if in_vmem else jax.ShapeDtypeStruct(*s) for s, in_vmem in zip(shapes, held)
        ],
        in_specs=[here] * 13,
        out_specs=[vmem] * len(shapes),
        scratch_shapes=list(scratch.values()),
        compiler_params=pltpu.CompilerParams(
            collective_id=0, has_side_effects=True, vmem_limit_bytes=(55 if packed else 54) * 2**20
        ),
    )(
        activations,
        out_grad,
        species,
        first_start,
        species_weight,
        conv_weight,
        point_weight,
        gain_one,
        bias_one,
        gain_two,
        bias_two,
        running_one,
        running_two,
    )
    keep = [i for i in range(len(shapes)) if held[i]]
    n = len(keep)
    given = pl.pallas_call(
        functools.partial(hand_out, n, 2),
        out_shape=[jax.ShapeDtypeStruct(*shapes[i]) for i in keep],
        in_specs=[vmem] * n,
        out_specs=[here] * n,
        scratch_shapes=[pltpu.SemaphoreType.DMA((n,))],
        compiler_params=pltpu.CompilerParams(vmem_limit_bytes=2**20),
    )(*[pltpu.with_memory_space_constraint(outs[i], pltpu.VMEM) for i in keep])
    outs = list(outs)
    for i, v in zip(keep, given):
        outs[i] = v
    if not packed:
        conv_grad, point_grad = outs[2], outs[3]
        conv_grad = lax.psum_scatter(conv_grad, "dp", scatter_dimension=1, tiled=True)
        point_grad = lax.psum_scatter(point_grad, "dp", scatter_dimension=1, tiled=True)
        outs[2] = lax.psum_scatter(conv_grad, "sub", scatter_dimension=2, tiled=True)
        outs[3] = lax.psum_scatter(point_grad, "sub", scatter_dimension=0, tiled=True)
    return tuple(outs)


def solution(mesh):
    in_specs = (
        P(("dp", "sub"), None),
        P(("dp", "sub"), None),
        P(("dp", "sub")),
        P(("dp", "sub")),
        P(),
        P(None, "dp", "sub"),
        P("sub", "dp"),
        P(),
        P(),
        P(),
        P(),
        P(),
        P(),
    )
    out_specs = (
        P(("dp", "sub"), None),
        P(("dp", "sub"), None),
        P(None, "dp", "sub"),
        P("sub", "dp"),
        P(),
        P(),
        P(),
        P(),
        P(),
        P(),
    )
    return jax.shard_map(
        functools.partial(body, mesh), mesh=mesh, in_specs=in_specs, out_specs=out_specs, check_vma=False
    )
```
